128 devices in a mesh: gx: 8 (over x_hi, y), gy: 16 (over z, x_lo, core).
Axes of the slice: x: 4 (x_hi: 2, x_lo: 2; x = x_hi * 2 + x_lo), y: 4, z: 4, core: 2. Of those that a mesh axis runs over, the one named last changes fastest.
Arguments:
- level_set: float32 [256, 256, 1024], P('gx', 'gy'), may hold values from -12 to 12
- flow_velocity: float32 [3, 128, 128, 512], P(None, ('gx', 'gy')), may hold values from -2 to 2
- band_mask: int32 [16, 16, 64], P('gx', 'gy'), may hold values from 0 to 1, as said below
Outputs:
- new_level_set: float32 [256, 256, 1024], P('gx', 'gy')
- flow_curvature: float32 [128, 128, 512], P(('gx', 'gy'))
- flow_fraction: float32 [128, 128, 512], P(('gx', 'gy'))
The draws below stay inside these ranges and needn't reach their ends.
Inputs may be any that keep to these rules, and one draw needn't show every extreme that they name: `band_mask`: tiles in the band mark where the interface lies; their share varies along x.
All inputs are finite; a program needn't handle non-finite values.
Results may differ from the reference program's by a relative error of at most 0.0003.
Values sent between devices are 32-bit elements; how exact they have to be, the bound alone decides.
No kernel may reach another device: no remote copies, remote signals or barrier semaphores. Data moves between devices by JAX's collectives and lax.ppermute only.
A program may use at most 320 MiB of HBM per device.

```python
import jax
import jax.numpy as jnp
from jax import lax

NZ = 1024
SWEEPS = 4
NX = 256
NY = 256
MX = 128
MY = 128
MZ = 512
TX = 16
TY = 16
TZ = 64


def draw_band_mask(key, part):
    key = jax.random.fold_in(key, 11)
    tile_rows = jnp.arange(TX, dtype=jnp.int32)
    distance = jnp.abs(2 * tile_rows + 1 - TX)
    threshold = 60 - 56 * distance // TX
    tickets = jax.random.randint(key, (TX, TY, TZ), 0, 64, dtype=jnp.int32)
    return (tickets < threshold[:, None, None]).astype(jnp.int32)


def level_of(rng, extent, cuts, least, high):
    def one(dim, parts):
        heights = jax.random.uniform(jax.random.fold_in(jax.random.fold_in(rng, 6), dim), (parts,), jnp.float32, least / len(cuts), high / len(cuts))
        return jnp.repeat(jnp.exp(heights), extent[dim] // parts).reshape((-1,) + (1,) * (len(extent) - dim - 1))

    level = one(*cuts[0])
    for cut in cuts[1:]:
        level = level * one(*cut)
    return level


def centred(rng, dims, deviation, limit, cuts=(), kind=jnp.bfloat16):
    loudness = level_of(rng, dims, cuts, -0.22, 0.18) if cuts else 1.0
    result = jax.random.normal(rng, dims, jnp.float32) * deviation * loudness
    return jnp.minimum(jnp.maximum(result, -limit), limit).astype(kind)


def setup_inputs(seed: int = 0) -> dict:
    arg_keys = jax.random.split(jax.random.key(seed), 4)
    return {
        "level_set": centred(arg_keys[0], (NX, NY, NZ), 2.0, 12.0, ((0, 8), (1, 16)), jnp.float32),
        "flow_velocity": centred(arg_keys[1], (3, MX, MY, MZ), 0.5, 2.0, ((1, 128),), jnp.float32),
        "band_mask": draw_band_mask(jax.random.fold_in(arg_keys[3], 71), 0),
    }


time_step = 0.25
pseudo_step = 0.3
weno_eps = 1e-06
front_width = 1.5

def squared(values):
    return values * values

def wrap_pad(values, depth, along_axes):
    for along in along_axes:
        length = values.shape[along]
        values = jnp.concatenate([lax.slice_in_dim(values, length - depth, length, axis=along), values, lax.slice_in_dim(values, 0, depth, axis=along)], axis=along)
    return values

def wrap_depth(values, depth):
    return wrap_pad(values, depth, (values.ndim - 1,))

def refine(coarse, along):
    inner_count = coarse.shape[along] - 2
    lower_cells = lax.slice_in_dim(coarse, 0, inner_count, axis=along)
    middle = lax.slice_in_dim(coarse, 1, inner_count + 1, axis=along)
    upper_cells = lax.slice_in_dim(coarse, 2, inner_count + 2, axis=along)
    even_cells = 0.25 * lower_cells + 0.75 * middle
    odd_cells = 0.75 * middle + 0.25 * upper_cells
    paired = jnp.stack([even_cells, odd_cells], axis=along + 1)
    new_shape = coarse.shape[:along] + (2 * inner_count,) + coarse.shape[along + 1:]
    return paired.reshape(new_shape)

def fine_velocity(coarse_padded):
    refined = refine(coarse_padded, 1)
    refined = refine(refined, 2)
    return refine(wrap_depth(refined, 1), 3)

def band_cells(tiles):
    tile_x, tile_y, tile_z = tiles.shape
    spread = jnp.broadcast_to(tiles.astype(jnp.float32)[:, None, :, None, :, None], (tile_x, 16, tile_y, 16, tile_z, 16))
    return spread.reshape(tile_x * 16, tile_y * 16, tile_z * 16)

def weno_blend(first, second, third, fourth, fifth):
    cand_one = first / 3.0 - 7.0 * second / 6.0 + 11.0 * third / 6.0
    cand_two = -second / 6.0 + 5.0 * third / 6.0 + fourth / 3.0
    cand_three = third / 3.0 + 5.0 * fourth / 6.0 - fifth / 6.0
    rough_one = 13.0 / 12.0 * squared(first - 2.0 * second + third) + 0.25 * squared(first - 4.0 * second + 3.0 * third)
    rough_two = 13.0 / 12.0 * squared(second - 2.0 * third + fourth) + 0.25 * squared(second - fourth)
    rough_three = 13.0 / 12.0 * squared(third - 2.0 * fourth + fifth) + 0.25 * squared(3.0 * third - 4.0 * fourth + fifth)
    weight_one = 0.1 / squared(weno_eps + rough_one)
    weight_two = 0.6 / squared(weno_eps + rough_two)
    weight_three = 0.3 / squared(weno_eps + rough_three)
    return (weight_one * cand_one + weight_two * cand_two + weight_three * cand_three) / (weight_one + weight_two + weight_three)

def weno_pair(padded, along):
    count_out = padded.shape[along] - 6
    differences = lax.slice_in_dim(padded, 1, count_out + 6, axis=along) - lax.slice_in_dim(padded, 0, count_out + 5, axis=along)
    slopes = [lax.slice_in_dim(differences, offset, offset + count_out, axis=along) for offset in range(6)]
    minus_side = weno_blend(slopes[0], slopes[1], slopes[2], slopes[3], slopes[4])
    plus_side = weno_blend(slopes[5], slopes[4], slopes[3], slopes[2], slopes[1])
    return (minus_side, plus_side)

def advect_rate(padded, velocity, band):
    pieces = [padded[:, 3:-3], padded[3:-3], wrap_depth(padded[3:-3, 3:-3], 3)]
    total = jnp.zeros(band.shape, jnp.float32)
    for along in range(3):
        minus_side, plus_side = weno_pair(pieces[along], along)
        speed = velocity[along]
        total = total + jnp.where(speed > 0, speed * minus_side, speed * plus_side)
    return -band * total

def rk_first(start, rate):
    return start + time_step * rate

def rk_second(start, first_section, rate):
    return 0.75 * start + 0.25 * (first_section + time_step * rate)

def rk_third(start, second_section, rate):
    return start / 3.0 + 2.0 / 3.0 * (second_section + time_step * rate)

def level_sign(values):
    return values / jnp.sqrt(values * values + 1.0)

def sweep_once(padded, sign_field):
    centre = padded[1:-1, 1:-1]
    backs = [centre - padded[:-2, 1:-1], centre - padded[1:-1, :-2], centre - jnp.roll(centre, 1, axis=2)]
    fores = [padded[2:, 1:-1] - centre, padded[1:-1, 2:] - centre, jnp.roll(centre, -1, axis=2) - centre]
    growing = jnp.zeros(centre.shape, jnp.float32)
    falling = jnp.zeros(centre.shape, jnp.float32)
    for along in range(3):
        growing = growing + jnp.maximum(squared(jnp.maximum(backs[along], 0.0)), squared(jnp.minimum(fores[along], 0.0)))
        falling = falling + jnp.maximum(squared(jnp.minimum(backs[along], 0.0)), squared(jnp.maximum(fores[along], 0.0)))
    slope_norm = jnp.sqrt(jnp.where(sign_field > 0, growing, falling))
    return centre - pseudo_step * sign_field * (slope_norm - 1.0)

def curvature(padded):
    grad_x = 0.5 * (padded[2:, 1:-1, 1:-1] - padded[:-2, 1:-1, 1:-1])
    grad_y = 0.5 * (padded[1:-1, 2:, 1:-1] - padded[1:-1, :-2, 1:-1])
    grad_z = 0.5 * (padded[1:-1, 1:-1, 2:] - padded[1:-1, 1:-1, :-2])
    length_inv = 1.0 / jnp.sqrt(grad_x * grad_x + grad_y * grad_y + grad_z * grad_z + 1.0)
    normal_x = grad_x * length_inv
    normal_y = grad_y * length_inv
    normal_z = grad_z * length_inv
    return 0.5 * (normal_x[2:, 1:-1, 1:-1] - normal_x[:-2, 1:-1, 1:-1]) + 0.5 * (normal_y[1:-1, 2:, 1:-1] - normal_y[1:-1, :-2, 1:-1]) + 0.5 * (normal_z[1:-1, 1:-1, 2:] - normal_z[1:-1, 1:-1, :-2])

def volume_fraction(values):
    return 0.5 * (1.0 + jnp.tanh(values / front_width))

def restrict(values):
    size_x, size_y, size_z = values.shape
    return values.reshape(size_x // 2, 2, size_y // 2, 2, size_z // 2, 2).mean(axis=(1, 3, 5))

def reference(level_set, flow_velocity, band_mask):
    refined = fine_velocity(wrap_pad(flow_velocity, 1, (1, 2)))
    velocity = (refined[0], refined[1], refined[2])
    band = band_cells(band_mask)
    rate = advect_rate(wrap_pad(level_set, 3, (0, 1)), velocity, band)
    first_section = rk_first(level_set, rate)
    rate = advect_rate(wrap_pad(first_section, 3, (0, 1)), velocity, band)
    second_section = rk_second(level_set, first_section, rate)
    rate = advect_rate(wrap_pad(second_section, 3, (0, 1)), velocity, band)
    advected = rk_third(level_set, second_section, rate)
    sign_field = level_sign(advected)
    current = advected
    for number in range(SWEEPS):
        current = sweep_once(wrap_pad(current, 1, (0, 1)), sign_field)
    kappa = curvature(wrap_depth(wrap_pad(current, 2, (0, 1)), 2))
    return (current, restrict(kappa), restrict(volume_fraction(current)))
```

```python
import functools

import jax
import jax.numpy as jnp
from jax import lax
from jax.experimental import pallas as pl
from jax.experimental.pallas import tpu as pltpu
from jax.sharding import PartitionSpec as P

SWEEPS = 4
TIME_STEP = 0.25
PSEUDO_STEP = 0.3
EPS = 1e-06
FRONT = 1.5
WIDE = SWEEPS + 2

ROWS, LANES = 8, 128
HIGH = lax.Precision.HIGHEST


def params(mib):
    return pltpu.CompilerParams(vmem_limit_bytes=mib * 2**20)


def f32(*shape):
    return jax.ShapeDtypeStruct(shape, jnp.float32)


def cost(vector_ops):
    return pl.CostEstimate(flops=vector_ops * 1024, bytes_accessed=2**23, transcendentals=0)


def shifted(col, step):
    lane = lax.broadcasted_iota(jnp.int32, (ROWS, LANES), 1)
    turned = pltpu.roll(col, (-step) % LANES, 1)
    if step > 0:
        return jnp.where(lane >= LANES - step, pltpu.roll(turned, ROWS - 1, 0), turned)
    return jnp.where(lane < -step, pltpu.roll(turned, 1, 0), turned)


def inverse(values):
    return pl.reciprocal(values, approx=True)


def correction(rough1, rough2, rough3, third1, third2):
    r1, r2, r3 = inverse(rough1), inverse(rough2), inverse(rough3)
    w1 = r1 * r1
    w12 = w1 + 6.0 * (r2 * r2)
    w3 = 3.0 * (r3 * r3)
    return (4.0 * w1 * third1 + (w3 - w12) * third2) * inverse(w12 + w3)


def upwind_part(speed, central, corr):
    return speed * central + jnp.abs(speed) * corr


class March:
    def __init__(self, get):
        self.get = get
        self.made = {}

    def once(self, name, j, make):
        key = (name, j)
        if key not in self.made:
            self.made[key] = make()
        return self.made[key]

    def p(self, j):
        return self.once("p", j, lambda: self.get(j))

    def d(self, j):
        return self.once("d", j, lambda: self.p(j + 1) - self.p(j))

    def curve(self, j):
        return self.once("c", j, lambda: self.d(j) - self.d(j - 1))

    def gap(self, j):
        return self.once("g", j, lambda: self.curve(j + 1) - self.curve(j))

    def third(self, j):
        return self.once("t", j, lambda: self.gap(j) - self.gap(j - 1))

    def base(self, j):
        return self.once("h", j, lambda: (4.0 / 3.0) * (self.gap(j) * self.gap(j)) + EPS)

    def cross(self, j):
        return self.once("x", j, lambda: self.curve(j) * self.curve(j + 1))

    def twice(self, j):
        return self.once("a", j, lambda: (self.curve(j) + self.curve(j)) * self.curve(j))

    def less(self, j):
        return self.once("l", j, lambda: self.base(j) - self.cross(j))

    def mid(self, j):
        return self.once("m", j, lambda: self.base(j) + self.cross(j))

    def up(self, j):
        return self.once("u", j, lambda: self.less(j) + self.twice(j + 1))

    def down(self, j):
        return self.once("v", j, lambda: self.less(j) + self.twice(j))

    def central(self, i):
        return 6.0 * (self.p(i + 1) - self.p(i - 1)) - (self.gap(i) + self.gap(i - 1))

    def part(self, i, speed):
        minus = speed < 0
        corr = correction(
            jnp.where(minus, self.up(i - 2), self.down(i + 1)),
            jnp.where(minus, self.mid(i - 1), self.mid(i)),
            jnp.where(minus, self.down(i), self.up(i - 1)),
            jnp.where(minus, self.third(i - 1), self.third(i + 1)),
            self.third(i),
        )
        return upwind_part(speed, self.central(i), corr)


def depth_part(col, speed):
    before, after = shifted(col, -1), shifted(col, 1)
    here = (after - col) - (col - before)
    m1, p1 = shifted(here, -1), shifted(here, 1)
    m2, p2 = shifted(here, -2), shifted(here, 2)
    minus = speed < 0
    a = jnp.where(minus, m2, p2)
    b = jnp.where(minus, m1, p1)
    d = jnp.where(minus, p1, m1)
    g1, g2, g3 = b - a, here - b, d - here
    corr = correction(
        (4.0 / 3.0) * (g1 * g1) + EPS + b * (b + g1),
        (4.0 / 3.0) * (g2 * g2) + EPS + b * here,
        (4.0 / 3.0) * (g3 * g3) + EPS + here * (here - g3),
        g2 - g1,
        g3 - g2,
    )
    return upwind_part(speed, 6.0 * (after - before) - (p1 - m1), corr)


def loop(low, high, body):
    def step(i, carry):
        body(i)
        return carry

    lax.fori_loop(low, high, step, 0)


def pack_velocity(rows_ref, out_ref):
    def to(g):
        for c in range(3):
            for r in range(10):
                block, low = (g, r - 1) if 1 <= r <= 8 else ((g + 15, 7) if r == 0 else (g + 1, 0))
                start = c * 512 + lax.rem(block, 16) * 32 + low
                out_ref[g, pl.ds((c * 10 + r) * 4, 4), :] = rows_ref[pl.ds(start, 4, stride=8), :]

    loop(0, 16, to)


def unpack_level(rows_ref, p_ref, ylo_ref, yhi_ref):
    def to(x):
        for y in range(16):
            col = rows_ref[pl.ds(x * 128 + (y // 8) * 64 + y % 8, 8, stride=8), :]
            p_ref[x, y] = col
            if y < 3:
                ylo_ref[x, y] = col
            if y >= 13:
                yhi_ref[x, y - 13] = col

    loop(0, 32, to)


def refine_velocity(lo_ref, mid_ref, hi_ref, band_ref, v_ref, fine):
    k = lax.broadcasted_iota(jnp.int32, (256, 256), 0)
    n = lax.broadcasted_iota(jnp.int32, (256, 256), 1)
    beside = jnp.where(n % 2 == 0, n // 2 - 1, n // 2 + 1)
    beside = jnp.where(beside < 0, 255, jnp.where(beside > 127, 128, beside))
    table = jnp.where(k == n // 2, 0.75, 0.0) + jnp.where(k == beside, 0.25, 0.0)
    row = lax.broadcasted_iota(jnp.int32, (120, 128), 0) % 4
    lane = lax.broadcasted_iota(jnp.int32, (120, 128), 1)

    def along_z(slot, plane):
        after = jnp.where(row == 3, pltpu.roll(plane, 3, 0), pltpu.roll(plane, 119, 0))
        prior = jnp.where(row == 0, pltpu.roll(plane, 117, 0), pltpu.roll(plane, 1, 0))
        wide = jnp.concatenate([plane, jnp.where(lane < 64, after, prior)], axis=1)
        out = jnp.dot(wide, table, precision=HIGH, preferred_element_type=jnp.float32)
        fine[slot, pl.ds(0, 120, stride=2), :] = out[:, :128]
        fine[slot, pl.ds(1, 120, stride=2), :] = out[:, 128:]

    along_z(0, lo_ref[...])
    loop(0, 16, lambda i: along_z(i + 1, mid_ref[i]))
    along_z(17, hi_ref[...])

    def along_xy(i):
        band = band_ref[lax.div(i, 8)]
        for c in range(3):
            for odd in range(2):
                line = []
                for r in range(10):
                    at = pl.ds((c * 10 + r) * 8, 8)
                    line.append(0.75 * fine[i + 1, at, :] + 0.25 * fine[i + 2 * odd, at, :])
                for y in range(16):
                    m = y // 2 + 1
                    v_ref[c, 2 * i + odd, y] = (0.75 * line[m] + 0.25 * line[m - 1 + 2 * (y % 2)]) * band

    loop(0, 16, along_xy)


def inner_rate(p_ref, v_ref, acc_ref):
    def x_line(y):
        march = March(lambda x: p_ref[x, y])
        for x in range(32):
            if 3 <= x < 29:
                acc_ref[x, y] = march.part(x, v_ref[0, x, y])
            else:
                acc_ref[x, y] = jnp.zeros((ROWS, LANES), jnp.float32)

    def y_line(x):
        march = March(lambda y: p_ref[x, y])
        for y in range(16):
            total = acc_ref[x, y] + depth_part(march.p(y), v_ref[2, x, y])
            if 3 <= y < 13:
                total = total + march.part(y, v_ref[1, x, y])
            acc_ref[x, y] = total

    loop(0, 16, x_line)
    loop(0, 32, y_line)


def section(start, current, rate, number):
    if number == 0:
        return current + rate
    if number == 1:
        return 0.75 * start + 0.25 * (current + rate)
    return start * (1.0 / 3.0) + (2.0 / 3.0) * (current + rate)


def edge_rate(number, edge, acc_ref, start_ref, p_ref, v_ref, xlo_ref, xhi_ref, ylo_ref, yhi_ref, new_ref, nlo_ref, nhi_ref, side):
    def x_line(y):
        low = March(lambda x: xlo_ref[x + 3, y] if x < 0 else p_ref[x, y])
        high = March(lambda x: xhi_ref[x - 32, y] if x >= 32 else p_ref[x, y])
        for k in range(3):
            side[k, y] = low.part(k, v_ref[0, k, y])
            side[k + 3, y] = high.part(29 + k, v_ref[0, 29 + k, y])

    loop(0, 16, x_line)

    def y_line(x, side_x):
        low = March(lambda y: ylo_ref[x, y + 3] if y < 0 else p_ref[x, y])
        high = March(lambda y: yhi_ref[x, y - 16] if y >= 16 else p_ref[x, y])
        for y in range(16):
            rate = acc_ref[x, y]
            if side_x is not None:
                rate = rate + side[side_x, y]
            if y < 3:
                rate = rate + low.part(y, v_ref[1, x, y])
            if y >= 13:
                rate = rate + high.part(y, v_ref[1, x, y])
            start = None if number == 0 else start_ref[x, y]
            new = section(start, p_ref[x, y], rate, number)
            new_ref[x, y] = new
            if y < edge:
                nlo_ref[x, y] = new
            if y >= 16 - edge:
                nhi_ref[x, y - (16 - edge)] = new

    loop(0, 3, lambda x: y_line(x, x))
    loop(3, 29, lambda x: y_line(x, None))
    loop(29, 32, lambda x: y_line(x, x - 26))


def finish(adv_ref, xlo_ref, xhi_ref, ylo_ref, yhi_ref, clo_ref, chi_ref, new_ref, send_ref, q0, q1, push, nx, ny, nz, lump):
    w = WIDE
    size_x, size_y = 32 + 2 * w, 16 + 2 * w

    def place(x, y, col):
        q0[x, y] = col
        push[x, y] = (PSEUDO_STEP * col) * lax.rsqrt(col * col + 1.0)

    def fill_mid(x):
        for y in range(w):
            place(x + w, y, ylo_ref[x, y])
            place(x + w, y + 16 + w, yhi_ref[x, y])
        for y in range(16):
            place(x + w, y + w, adv_ref[x, y])

    def fill_side(x):
        for y in range(w):
            place(x, y, clo_ref[x, y])
            place(x, y + 16 + w, chi_ref[x, y])
            place(x + 32 + w, y, clo_ref[x + w, y])
            place(x + 32 + w, y + 16 + w, chi_ref[x + w, y])
        for y in range(16):
            place(x, y + w, xlo_ref[x, y])
            place(x + 32 + w, y + w, xhi_ref[x, y])

    loop(0, 32, fill_mid)
    loop(0, w, fill_side)

    def sweep(src, dst, k):
        def line(x):
            cols = {}

            def at(y):
                if y not in cols:
                    cols[y] = src[x, y]
                return cols[y]

            for y in range(k, size_y - k):
                col = at(y)
                c = push[x, y]
                sign = jnp.where(c > 0, 1.0, -1.0)
                here = sign * col
                total = None
                for pair in (
                    (src[x - 1, y], src[x + 1, y]),
                    (at(y - 1), at(y + 1)),
                    (shifted(col, -1), shifted(col, 1)),
                ):
                    rise = jnp.maximum(here - jnp.minimum(sign * pair[0], sign * pair[1]), 0.0)
                    total = rise * rise if total is None else total + rise * rise
                slope = total * lax.rsqrt(jnp.maximum(total, 1e-30))
                dst[x, y] = (col + c) - c * slope

        loop(k, size_x - k, line)

    buffers = (q0, q1)
    for k in range(SWEEPS):
        sweep(buffers[k % 2], buffers[(k + 1) % 2], k + 1)
    last = buffers[SWEEPS % 2]

    def normals(x):
        xs = x + w - 1
        cols = {}

        def at(y):
            if y not in cols:
                cols[y] = last[xs, y + w]
            return cols[y]

        across, along, deep = {}, {}, {}
        for y in range(-1, 17):
            gx = last[xs + 1, y + w] - last[xs - 1, y + w]
            gy = at(y + 1) - at(y - 1)
            gz = shifted(at(y), 1) - shifted(at(y), -1)
            scale = lax.rsqrt(gx * gx + gy * gy + gz * gz + 4.0)
            across[y], along[y], deep[y] = gx * scale, gy * scale, gz * scale
        for j in range(8):
            a, b = 2 * j, 2 * j + 1
            nx[x, j] = across[a] + across[b]
            ny[x, j] = (along[b] + along[b + 1]) - (along[a - 1] + along[a])
            nz[x, j] = deep[a] + deep[b]

    loop(0, 34, normals)

    def gather(i):
        a, b = 2 * i + 1, 2 * i + 2
        for j in range(8):
            deep = nz[a, j] + nz[b, j]
            total = (nx[b, j] + nx[b + 1, j]) - (nx[a - 1, j] + nx[a, j]) + (ny[a, j] + ny[b, j])
            lump[pl.ds(i * 64 + j * 8, 8), :] = total + (shifted(deep, 1) - shifted(deep, -1))
            share = None
            for x in range(2):
                for y in range(2):
                    xx, yy = 2 * i + x, 2 * j + y
                    col = last[xx + w, yy + w]
                    new_ref[pl.ds(xx * 128 + (yy // 8) * 64 + yy % 8, 8, stride=8), :] = col
                    bend = jnp.tanh(col * (1.0 / FRONT))
                    share = bend if share is None else share + bend
            lump[pl.ds(1024 + i * 64 + j * 8, 8), :] = share

    loop(0, 16, gather)

    k = lax.broadcasted_iota(jnp.int32, (256, 128), 0)
    n = lax.broadcasted_iota(jnp.int32, (256, 128), 1)
    table = jnp.where(lax.div(k, 2) == n, 1.0 / 16.0, 0.0)

    def restrict(i):
        for kind in range(2):
            base = kind * 1024 + i * 64
            left = [lump[pl.ds(base + 2 * z, 8, stride=8), :] for z in range(4)]
            right = [lump[pl.ds(base + 2 * z + 1, 8, stride=8), :] for z in range(4)]
            wide = jnp.concatenate([jnp.concatenate(left, axis=0), jnp.concatenate(right, axis=0)], axis=1)
            out = jnp.dot(wide, table, precision=HIGH, preferred_element_type=jnp.float32)
            send_ref[i, pl.ds(kind * 32, 32), :] = out + 0.5 if kind else out

    loop(0, 16, restrict)


def call(kernel, outs, *args, scratch=(), mib=48, ops=1000, name=None):
    return pl.pallas_call(
        kernel,
        out_shape=outs,
        in_specs=[pl.BlockSpec(memory_space=pltpu.VMEM)] * len(args),
        out_specs=jax.tree.map(lambda _: pl.BlockSpec(memory_space=pltpu.VMEM), outs),
        scratch_shapes=[pltpu.VMEM(s, jnp.float32) for s in scratch],
        compiler_params=params(mib),
        cost_estimate=cost(ops),
        name=name,
    )(*args)


def moved(values, axis, step):
    count = lax.axis_size(axis)
    return lax.ppermute(values, axis, [(i, (i + step) % count) for i in range(count)])


def star(p, ylo, yhi, width):
    return (
        moved(p[32 - width :], "gx", 1),
        moved(p[:width], "gx", -1),
        moved(yhi, "gy", 1),
        moved(ylo, "gy", -1),
    )


def per_device(level_set, flow_velocity, band_mask):
    col = (ROWS, LANES)
    block = f32(32, 16, *col)
    level_rows = level_set.reshape(32, 2, 8, 8, 128).transpose(0, 1, 3, 2, 4).reshape(4096, 128)
    flow_rows = flow_velocity.reshape(3, 16, 8, 4, 128).transpose(0, 1, 3, 2, 4).reshape(1536, 128)
    band = band_mask.reshape(2, 8, 8).astype(jnp.float32) * (-TIME_STEP / 12.0)
    band = jnp.broadcast_to(band[..., None], (2, 8, 8, 16)).reshape(2, 8, 128)

    send = call(pack_velocity, f32(16, 120, 128), flow_rows, name="pack", mib=8)
    coarse = lax.all_to_all(send, "gy", split_axis=0, concat_axis=0, tiled=True)
    start, ylo, yhi = call(
        unpack_level, (block, f32(32, 3, *col), f32(32, 3, *col)), level_rows, name="unpack", mib=8
    )
    halo = star(start, ylo, yhi, 3)
    below, above = moved(coarse[15], "gx", 1), moved(coarse[0], "gx", -1)
    velocity = call(
        refine_velocity, f32(3, 32, 16, *col), below, coarse, above, band, scratch=[(18, 240, 128)], name="refine", mib=24
    )
    current = start
    for number in range(3):
        acc = call(inner_rate, block, current, velocity, name="inner", mib=24, ops=512 * 140)
        edge = WIDE if number == 2 else 3
        current, ylo, yhi = call(
            functools.partial(edge_rate, number, edge),
            (block, f32(32, edge, *col), f32(32, edge, *col)),
            acc, start, current, velocity, *halo,
            scratch=[(6, 16, *col)],
            name="edge", mib=24, ops=512 * 30,
        )
        halo = star(current, ylo, yhi, edge)
    xlo, xhi, ylo, yhi = halo
    sides = jnp.concatenate([xlo, xhi], axis=0)
    clo = moved(sides[:, 16 - WIDE :], "gy", 1)
    chi = moved(sides[:, :WIDE], "gy", -1)
    ext = (32 + 2 * WIDE, 16 + 2 * WIDE, *col)
    new_rows, packed = call(
        finish,
        (f32(4096, 128), f32(16, 64, 128)),
        current, xlo, xhi, ylo, yhi, clo, chi,
        scratch=[ext, ext, ext] + [(34, 8, *col)] * 3 + [(2048, 128)],
        name="finish", mib=48, ops=512 * 250,
    )
    returned = lax.all_to_all(packed, "gy", split_axis=0, concat_axis=0, tiled=True).reshape(16, 2, 4, 8, 128)
    new_level = new_rows.reshape(32, 2, 8, 8, 128).transpose(0, 1, 3, 2, 4).reshape(32, 16, 1024)
    flows = [returned[:, k].transpose(0, 2, 1, 3).reshape(1, 128, 512) for k in range(2)]
    return (new_level, flows[0], flows[1])


def solution(mesh):
    placed = (P("gx", "gy", None), P(None, ("gx", "gy"), None, None), P("gx", "gy", None))
    return jax.shard_map(
        per_device,
        mesh=mesh,
        in_specs=placed,
        out_specs=(P("gx", "gy", None), P(("gx", "gy"), None, None), P(("gx", "gy"), None, None)),
        check_vma=False,
    )
```

```python
import functools

import jax
import jax.numpy as jnp
from jax import lax
from jax.experimental import pallas as pl
from jax.experimental.pallas import tpu as pltpu
from jax.sharding import PartitionSpec as P

SWEEPS = 4
TIME_STEP = 0.25
PSEUDO_STEP = 0.3
EPS = 1e-06
FRONT = 1.5
WIDE = SWEEPS + 2

ROWS, LANES = 8, 128
HIGH = lax.Precision.HIGHEST


def params(mib):
    return pltpu.CompilerParams(vmem_limit_bytes=mib * 2**20)


def f32(*shape):
    return jax.ShapeDtypeStruct(shape, jnp.float32)


def cost(vector_ops):
    return pl.CostEstimate(flops=vector_ops * 1024, bytes_accessed=2**23, transcendentals=0)


def shifted(col, step):
    lane = lax.broadcasted_iota(jnp.int32, (ROWS, LANES), 1)
    turned = pltpu.roll(col, (-step) % LANES, 1)
    if step > 0:
        return jnp.where(lane >= LANES - step, pltpu.roll(turned, ROWS - 1, 0), turned)
    return jnp.where(lane < -step, pltpu.roll(turned, 1, 0), turned)


def inverse(values):
    return pl.reciprocal(values, approx=True)


def correction(rough1, rough2, rough3, third1, third2):
    r1, r2, r3 = inverse(rough1), inverse(rough2), inverse(rough3)
    w1 = r1 * r1
    w12 = w1 + 6.0 * (r2 * r2)
    w3 = 3.0 * (r3 * r3)
    return (4.0 * w1 * third1 + (w3 - w12) * third2) * inverse(w12 + w3)


def upwind_part(speed, central, corr):
    return speed * central + jnp.abs(speed) * corr


class March:
    def __init__(self, get):
        self.get = get
        self.made = {}

    def once(self, name, j, make):
        key = (name, j)
        if key not in self.made:
            self.made[key] = make()
        return self.made[key]

    def p(self, j):
        return self.once("p", j, lambda: self.get(j))

    def d(self, j):
        return self.once("d", j, lambda: self.p(j + 1) - self.p(j))

    def curve(self, j):
        return self.once("c", j, lambda: self.d(j) - self.d(j - 1))

    def gap(self, j):
        return self.once("g", j, lambda: self.curve(j + 1) - self.curve(j))

    def third(self, j):
        return self.once("t", j, lambda: self.gap(j) - self.gap(j - 1))

    def base(self, j):
        return self.once("h", j, lambda: (4.0 / 3.0) * (self.gap(j) * self.gap(j)) + EPS)

    def cross(self, j):
        return self.once("x", j, lambda: self.curve(j) * self.curve(j + 1))

    def twice(self, j):
        return self.once("a", j, lambda: (self.curve(j) + self.curve(j)) * self.curve(j))

    def less(self, j):
        return self.once("l", j, lambda: self.base(j) - self.cross(j))

    def mid(self, j):
        return self.once("m", j, lambda: self.base(j) + self.cross(j))

    def up(self, j):
        return self.once("u", j, lambda: self.less(j) + self.twice(j + 1))

    def down(self, j):
        return self.once("v", j, lambda: self.less(j) + self.twice(j))

    def central(self, i):
        return 6.0 * (self.p(i + 1) - self.p(i - 1)) - (self.gap(i) + self.gap(i - 1))

    def part(self, i, speed):
        minus = speed < 0
        corr = correction(
            jnp.where(minus, self.up(i - 2), self.down(i + 1)),
            jnp.where(minus, self.mid(i - 1), self.mid(i)),
            jnp.where(minus, self.down(i), self.up(i - 1)),
            jnp.where(minus, self.third(i - 1), self.third(i + 1)),
            self.third(i),
        )
        return upwind_part(speed, self.central(i), corr)


def depth_rate(slope, here, turned, speed):
    m2, m1, p1, p2 = turned
    minus = speed < 0
    a = jnp.where(minus, m2, p2)
    b = jnp.where(minus, m1, p1)
    d = jnp.where(minus, p1, m1)
    g1, g2, g3 = b - a, here - b, d - here
    corr = correction(
        (4.0 / 3.0) * (g1 * g1) + EPS + b * (b + g1),
        (4.0 / 3.0) * (g2 * g2) + EPS + b * here,
        (4.0 / 3.0) * (g3 * g3) + EPS + here * (here - g3),
        g2 - g1,
        g3 - g2,
    )
    return upwind_part(speed, slope - (p1 - m1), corr)


def depth_part(col, speed):
    before, after = shifted(col, -1), shifted(col, 1)
    here = (after - col) - (col - before)
    return depth_rate(6.0 * (after - before), here, [shifted(here, step) for step in (-2, -1, 1, 2)], speed)


def loop(low, high, body):
    def step(i, carry):
        body(i)
        return carry

    lax.fori_loop(low, high, step, 0)


def pack_velocity(rows_ref, out_ref):
    def to(g):
        for c in range(3):
            for r in range(10):
                block, low = (g, r - 1) if 1 <= r <= 8 else ((g + 15, 7) if r == 0 else (g + 1, 0))
                start = c * 512 + lax.rem(block, 16) * 32 + low
                out_ref[g, pl.ds((c * 10 + r) * 4, 4), :] = rows_ref[pl.ds(start, 4, stride=8), :]

    loop(0, 16, to)


def unpack_level(rows_ref, p_ref, ylo_ref, yhi_ref):
    def to(x):
        for y in range(16):
            col = rows_ref[pl.ds(x * 128 + (y // 8) * 64 + y % 8, 8, stride=8), :]
            p_ref[x, y] = col
            if y < 3:
                ylo_ref[x, y] = col
            if y >= 13:
                yhi_ref[x, y - 13] = col

    loop(0, 32, to)


def refine_table():
    k = lax.broadcasted_iota(jnp.int32, (256, 256), 0)
    n = lax.broadcasted_iota(jnp.int32, (256, 256), 1)
    beside = jnp.where(n % 2 == 0, n // 2 - 1, n // 2 + 1)
    beside = jnp.where(beside < 0, 255, jnp.where(beside > 127, 128, beside))
    return jnp.where(k == n // 2, 0.75, 0.0) + jnp.where(k == beside, 0.25, 0.0)


def refine_z(plane, table):
    count = plane.shape[0]
    row = lax.broadcasted_iota(jnp.int32, plane.shape, 0) % 4
    lane = lax.broadcasted_iota(jnp.int32, plane.shape, 1)
    after = jnp.where(row == 3, pltpu.roll(plane, 3, 0), pltpu.roll(plane, count - 1, 0))
    prior = jnp.where(row == 0, pltpu.roll(plane, count - 3, 0), pltpu.roll(plane, 1, 0))
    wide = jnp.concatenate([plane, jnp.where(lane < 64, after, prior)], axis=1)
    out = jnp.dot(wide, table, precision=HIGH, preferred_element_type=jnp.float32)
    return out[:, :128], out[:, 128:]


def band_blocks(band_ref):
    k = lax.broadcasted_iota(jnp.int32, (64, 128), 0)
    n = lax.broadcasted_iota(jnp.int32, (64, 128), 1)
    spread = jnp.where(lax.rem(k, 8) == lax.div(n, 16), -TIME_STEP / 12.0, 0.0)
    row = lax.broadcasted_iota(jnp.int32, (8, 64), 0)
    tile = lax.div(lax.broadcasted_iota(jnp.int32, (8, 64), 1), 8)
    blocks = []
    for half in range(2):
        mask = jnp.broadcast_to(band_ref[half].astype(jnp.float32), (8, 64))
        mask = jnp.where(row == tile, mask, 0.0)
        blocks.append(jnp.dot(mask, spread, precision=HIGH, preferred_element_type=jnp.float32))
    return blocks


def refine_inner(mid_ref, band_ref, v_ref, ends_ref, fine, band):
    table = refine_table()
    for half, block in enumerate(band_blocks(band_ref)):
        band[half] = block

    def along_z(k):
        left, right = refine_z(mid_ref[pl.ds(k * 480, 480), :], table)
        fine[pl.ds(k * 960, 480, stride=2), :] = left
        fine[pl.ds(k * 960 + 1, 480, stride=2), :] = right

    loop(0, 4, along_z)
    for end, plane in enumerate((0, 15)):
        ends_ref[end] = fine[pl.ds(plane * 240, 240), :]

    def along_xy(i):
        for c in range(3):
            near, far = [], []
            for r in range(10):
                at = (c * 10 + r) * 8
                near.append(fine[pl.ds(i * 240 + at, 8), :])
                far.append(fine[pl.ds(i * 240 + 240 + at, 8), :])
            for k in range(2):
                x = 2 * i + 1 + k
                line = [0.75 * a + 0.25 * b for a, b in (zip(far, near) if k else zip(near, far))]
                along_y(c, x, line, band[lax.div(x, 16)], v_ref)

    loop(0, 15, along_xy)


def along_y(c, x, line, band, v_ref):
    scaled = [band * value for value in line]
    for y in range(16):
        m = y // 2 + 1
        v_ref[c, x, y] = 0.75 * scaled[m] + 0.25 * scaled[m - 1 + 2 * (y % 2)]


def refine_ends(lo_ref, hi_ref, ends_ref, band_ref, p_ref, v_in, acc_in, v_out, acc_out, fine, ends, part, sems):
    table = refine_table()
    blocks = band_blocks(band_ref)
    for side, ref in enumerate((lo_ref, hi_ref)):
        left, right = refine_z(ref[pl.ds(384, 120), :], table)
        fine[pl.ds(side * 240, 120, stride=2), :] = left
        fine[pl.ds(side * 240 + 1, 120, stride=2), :] = right
    for side in range(2):
        for c in range(3):
            line = []
            for r in range(10):
                at = (c * 10 + r) * 8
                line.append(0.75 * ends_ref[side, pl.ds(at, 8), :] + 0.25 * fine[pl.ds(side * 240 + at, 8), :])
            along_y(c, side, line, blocks[side], ends)
    for side in range(2):
        x = 31 * side
        march = March(lambda y: p_ref[x, y])
        for y in range(16):
            total = depth_part(march.p(y), ends[2, side, y])
            if 3 <= y < 13:
                total = total + march.part(y, ends[1, side, y])
            part[side, y] = total
    copies = []
    for side in range(2):
        copies.append((part.at[side], acc_out.at[31 * side]))
        for c in range(3):
            copies.append((ends.at[c, side], v_out.at[c, 31 * side]))
    copies = [pltpu.make_async_copy(src, dst, sems.at[k]) for k, (src, dst) in enumerate(copies)]
    for copy in copies:
        copy.start()
    for copy in copies:
        copy.wait()


def inner_rate(first, p_ref, v_ref, acc_ref, curve, slope, even, odd):
    def x_line(y):
        march = March(lambda x: p_ref[x, y])
        for x in range(32):
            col = march.p(x)
            before, after = shifted(col, -1), shifted(col, 1)
            curve[x, y] = (after - col) - (col - before)
            slope[x, y] = 6.0 * (after - before)
            if 3 <= x < 29:
                acc_ref[x, y] = march.part(x, v_ref[0, x, y])
            else:
                acc_ref[x, y] = jnp.zeros((ROWS, LANES), jnp.float32)

    loop(0, 16, x_line)

    def turn(x, turned):
        for y in range(16):
            col = curve[x, y]
            for k, step in enumerate((-2, -1, 1, 2)):
                turned[k, y] = shifted(col, step)

    def y_line(x, turned):
        march = March(lambda y: p_ref[x, y])
        for y in range(16):
            total = acc_ref[x, y] + depth_rate(slope[x, y], curve[x, y], [turned[k, y] for k in range(4)], v_ref[2, x, y])
            if 3 <= y < 13:
                total = total + march.part(y, v_ref[1, x, y])
            acc_ref[x, y] = total

    low = 1 if first else 0
    count = 30 if first else 32
    turn(low, even)

    def two(k):
        x = low + 2 * k
        turn(x + 1, odd)
        y_line(x, even)
        turn(jnp.minimum(x + 2, 31), even)
        y_line(x + 1, odd)

    loop(0, count // 2, two)


def section(start, current, rate, number):
    if number == 0:
        return current + rate
    if number == 1:
        return 0.75 * start + 0.25 * (current + rate)
    return start * (1.0 / 3.0) + (2.0 / 3.0) * (current + rate)


def edge_rate(
    number, edge, acc_ref, start_ref, p_ref, v_ref, xlo_ref, xhi_ref, ylo_ref, yhi_ref,
    new_ref, nxlo_ref, nxhi_ref, nylo_ref, nyhi_ref, side,
):
    def from_rows(ref, x, y):
        return ref[pl.ds((x * 16 + y) * 8, 8), :]

    def x_line(y):
        low = March(lambda x: from_rows(xlo_ref, x + 3, y) if x < 0 else p_ref[x, y])
        high = March(lambda x: from_rows(xhi_ref, x - 32, y) if x >= 32 else p_ref[x, y])
        for k in range(3):
            side[k, y] = low.part(k, v_ref[0, k, y])
            side[k + 3, y] = high.part(29 + k, v_ref[0, 29 + k, y])

    loop(0, 16, x_line)

    def y_line(x, side_x, outs):
        low = March(lambda y: ylo_ref[x, y + 3] if y < 0 else p_ref[x, y])
        high = March(lambda y: yhi_ref[x, y - 16] if y >= 16 else p_ref[x, y])
        for y in range(16):
            rate = acc_ref[x, y]
            if side_x is not None:
                rate = rate + side[side_x, y]
            if y < 3:
                rate = rate + low.part(y, v_ref[1, x, y])
            if y >= 13:
                rate = rate + high.part(y, v_ref[1, x, y])
            start = None if number == 0 else start_ref[x, y]
            new = section(start, p_ref[x, y], rate, number)
            new_ref[x, y] = new
            if outs is not None:
                outs[0][pl.ds((outs[1] * 16 + y) * 8, 8), :] = new
            if y < edge:
                nylo_ref[x, y] = new
            if y >= 16 - edge:
                nyhi_ref[x, y - (16 - edge)] = new

    loop(0, 3, lambda x: y_line(x, x, (nxlo_ref, x)))
    loop(29, 32, lambda x: y_line(x, x - 26, (nxhi_ref, x - (32 - edge))))
    if edge > 3:
        loop(3, edge, lambda x: y_line(x, None, (nxlo_ref, x)))
        loop(32 - edge, 29, lambda x: y_line(x, None, (nxhi_ref, x - (32 - edge))))
    loop(edge, 32 - edge, lambda x: y_line(x, None, None))


def pushes(col):
    push = (PSEUDO_STEP * col) * lax.rsqrt(col * col + 1.0)
    return push, jnp.where(col > 0, 1.0, -1.0)


def turn(src, x, ys, turned):
    for y in ys:
        col = src[x, y]
        turned[0, y] = shifted(col, -1)
        turned[1, y] = shifted(col, 1)


def sweep_line(src, dst, push, sign, x, ys, turned):
    cols = {}

    def at(y):
        if y not in cols:
            cols[y] = src[x, y]
        return cols[y]

    for y in ys:
        col, c, s = at(y), push[x, y], sign[x, y]
        here = s * col
        total = None
        for pair in ((src[x - 1, y], src[x + 1, y]), (at(y - 1), at(y + 1)), (turned[0, y], turned[1, y])):
            floor = 1e-15 if total is None else 0.0
            rise = jnp.maximum(here - jnp.minimum(s * pair[0], s * pair[1]), floor)
            total = rise * rise if total is None else total + rise * rise
        dst[x, y] = (col + c) - (c * total) * lax.rsqrt(total)


def sweep_rows(src, dst, push, sign, place, pairs, ys, even, odd):
    turn(src, place(0), ys, even)

    def two(j):
        x = place(j)
        turn(src, x + 1, ys, odd)
        sweep_line(src, dst, push, sign, x, ys, even)
        turn(src, place(jnp.minimum(j + 1, pairs - 1)), ys, even)
        sweep_line(src, dst, push, sign, x + 1, ys, odd)

    loop(0, pairs, two)


def sweep_core(adv_ref, *refs):
    levels, (push, sign, even, odd) = refs[:SWEEPS], refs[SWEEPS:]

    def prepare(x):
        for y in range(16):
            push[x, y], sign[x, y] = pushes(adv_ref[x, y])

    loop(0, 32, prepare)
    src = adv_ref
    for k in range(1, SWEEPS + 1):
        dst = levels[k - 1]
        sweep_rows(src, dst, push, sign, lambda j, k=k: k + 2 * j, 16 - k, range(k, 16 - k), even, odd)
        src = dst


def pack_corners(xlo_ref, xhi_ref, _, low_ref, high_ref):
    k = 0
    for dx in range(1, WIDE):
        for ref, x in ((xlo_ref, WIDE - dx), (xhi_ref, dx - 1)):
            for dy in range(1, WIDE - dx + 1):
                low_ref[k] = ref[pl.ds((x * 16 + dy - 1) * 8, 8), :]
                high_ref[k] = ref[pl.ds((x * 16 + 16 - dy) * 8, 8), :]
                k += 1


CORNERS = WIDE * (WIDE - 1)


def finish(
    adv_ref, xlo_ref, xhi_ref, ylo_ref, yhi_ref, clo_ref, chi_ref, one_ref, two_ref, three_ref, four_ref,
    new_ref, send_ref, q0, q1, push, sign, nx, ny, nz, lump, even, odd,
):
    w = WIDE
    size_x, size_y = 32 + 2 * w, 16 + 2 * w

    def put(x, y, col):
        q0[x, y] = col
        push[x, y], sign[x, y] = pushes(col)

    def fill_mid(x):
        for y in range(w):
            put(x + w, y, ylo_ref[x, y])
            put(x + w, y + 16 + w, yhi_ref[x, y])
        for y in range(16):
            put(x + w, y + w, adv_ref[x, y])

    def fill_side(x):
        for y in range(16):
            put(x, y + w, xlo_ref[pl.ds((x * 16 + y) * 8, 8), :])
            put(x + 32 + w, y + w, xhi_ref[pl.ds((x * 16 + y) * 8, 8), :])

    loop(0, 32, fill_mid)
    loop(0, w, fill_side)
    k = 0
    for dx in range(1, w):
        for x in (w - dx, w + 31 + dx):
            for dy in range(1, w - dx + 1):
                put(x, w - dy, clo_ref[k])
                put(x, w + 15 + dy, chi_ref[k])
                k += 1

    src, dst = q0, q1
    for k, core_ref in enumerate((one_ref, two_ref, three_ref, four_ref), 1):
        def end_rows(j, k=k):
            return k + 2 * j + jnp.where(j >= 3, 32 - 2 * k, 0)

        sweep_rows(src, dst, push, sign, end_rows, 6, range(k, size_y - k), even, odd)
        sides = [*range(k, k + w), *range(size_y - k - w, size_y - k)]
        sweep_rows(src, dst, push, sign, lambda j, k=k: w + k + 2 * j, 16 - k, sides, even, odd)
        inside = range(k, 16 - k)
        if k < SWEEPS:
            for x in (k, k + 1, 30 - k, 31 - k):
                for y in inside:
                    dst[x + w, y + w] = core_ref[x, y]
            inside = (k, k + 1, 14 - k, 15 - k)

        def take(x, core_ref=core_ref, inside=inside, dst=dst):
            for y in inside:
                dst[x + w, y + w] = core_ref[x, y]

        loop(k, 32 - k, take)
        src, dst = dst, src
    last = src

    def normals(x):
        xs = x + w - 1
        cols = {}

        def at(y):
            if y not in cols:
                cols[y] = last[xs, y + w]
            return cols[y]

        across, along, deep = {}, {}, {}
        for y in range(-1, 17):
            gx = last[xs + 1, y + w] - last[xs - 1, y + w]
            gy = at(y + 1) - at(y - 1)
            gz = shifted(at(y), 1) - shifted(at(y), -1)
            scale = lax.rsqrt(gx * gx + gy * gy + gz * gz + 4.0)
            across[y], along[y], deep[y] = gx * scale, gy * scale, gz * scale
        for j in range(8):
            a, b = 2 * j, 2 * j + 1
            nx[x, j] = across[a] + across[b]
            ny[x, j] = (along[b] + along[b + 1]) - (along[a - 1] + along[a])
            nz[x, j] = deep[a] + deep[b]

    loop(0, 34, normals)

    def gather(i):
        a, b = 2 * i + 1, 2 * i + 2
        for j in range(8):
            deep = nz[a, j] + nz[b, j]
            total = (nx[b, j] + nx[b + 1, j]) - (nx[a - 1, j] + nx[a, j]) + (ny[a, j] + ny[b, j])
            lump[pl.ds(i * 64 + j * 8, 8), :] = total + (shifted(deep, 1) - shifted(deep, -1))
            share = None
            for x in range(2):
                for y in range(2):
                    xx, yy = 2 * i + x, 2 * j + y
                    col = last[xx + w, yy + w]
                    new_ref[pl.ds(xx * 128 + (yy // 8) * 64 + yy % 8, 8, stride=8), :] = col
                    bend = jnp.tanh(col * (1.0 / FRONT))
                    share = bend if share is None else share + bend
            lump[pl.ds(1024 + i * 64 + j * 8, 8), :] = share

    loop(0, 16, gather)

    k = lax.broadcasted_iota(jnp.int32, (256, 128), 0)
    n = lax.broadcasted_iota(jnp.int32, (256, 128), 1)
    table = jnp.where(lax.div(k, 2) == n, 1.0 / 16.0, 0.0)

    def restrict(g):
        halves = []
        for odd_row in range(2):
            rows = []
            for kind in range(2):
                for i in range(4):
                    base = kind * 1024 + (4 * g + i) * 64 + odd_row
                    rows += [lump[pl.ds(base + 2 * z, 8, stride=8), :] for z in range(4)]
            halves.append(jnp.concatenate(rows, axis=0))
        out = jnp.dot(jnp.concatenate(halves, axis=1), table, precision=HIGH, preferred_element_type=jnp.float32)
        for i in range(4):
            send_ref[4 * g + i, pl.ds(0, 32), :] = out[i * 32 : i * 32 + 32]
            send_ref[4 * g + i, pl.ds(32, 32), :] = out[128 + i * 32 : 160 + i * 32] + 0.5

    loop(0, 4, restrict)


def call(kernel, outs, *args, scratch=(), mib=48, ops=1000, name=None, anywhere=(), aliases=None):
    def spec(k):
        return pl.BlockSpec(memory_space=pl.ANY if k in anywhere else pltpu.VMEM)

    aliases = aliases or {}
    flat = outs if isinstance(outs, tuple) else (outs,)
    specs = tuple(pl.BlockSpec(memory_space=pl.ANY if k in aliases.values() else pltpu.VMEM) for k in range(len(flat)))
    return pl.pallas_call(
        kernel,
        out_shape=outs,
        in_specs=[spec(k) for k in range(len(args))],
        out_specs=specs if isinstance(outs, tuple) else specs[0],
        scratch_shapes=[pltpu.VMEM(s, jnp.float32) if isinstance(s, tuple) else s for s in scratch],
        input_output_aliases=aliases,
        compiler_params=params(mib),
        cost_estimate=cost(ops),
        name=name,
    )(*args)


def moved(values, axis, step):
    count = lax.axis_size(axis)
    return lax.ppermute(values, axis, [(i, (i + step) % count) for i in range(count)])


def star(xlo, xhi, ylo, yhi):
    return (moved(xhi, "gx", 1), moved(xlo, "gx", -1), moved(yhi, "gy", 1), moved(ylo, "gy", -1))


def per_device(level_set, flow_velocity, band_mask):
    col = (ROWS, LANES)
    block = f32(32, 16, *col)
    level_rows = level_set.reshape(32, 2, 8, 8, 128).transpose(0, 1, 3, 2, 4).reshape(4096, 128)
    flow_rows = flow_velocity.reshape(3, 16, 8, 4, 128).transpose(0, 1, 3, 2, 4).reshape(1536, 128)

    send = call(pack_velocity, f32(16, 120, 128), flow_rows, name="pack", mib=8)
    coarse = lax.all_to_all(send, "gy", split_axis=0, concat_axis=0, tiled=True)
    start, ylo, yhi = call(
        unpack_level, (block, f32(32, 3, *col), f32(32, 3, *col)), level_rows, name="unpack", mib=8
    )
    xlo = jnp.concatenate([start[:3].reshape(384, 128), coarse[0]], axis=0)
    xhi = jnp.concatenate([start[29:].reshape(384, 128), coarse[15]], axis=0)
    halo = star(xlo, xhi, ylo, yhi)
    velocity, ends = call(
        refine_inner, (f32(3, 32, 16, *col), f32(2, 240, 128)), coarse.reshape(1920, 128), band_mask,
        scratch=[(3840, 128), (2, *col)], name="refine", mib=24,
    )
    current = start
    for number in range(3):
        acc = call(
            functools.partial(inner_rate, number == 0), block, current, velocity,
            scratch=[block.shape, block.shape, (4, 16, *col), (4, 16, *col)], name="inner", mib=24, ops=512 * 140,
        )
        if number == 0:
            velocity, acc = call(
                refine_ends, (f32(3, 32, 16, *col), block), halo[0], halo[1], ends, band_mask, current, velocity, acc,
                scratch=[(480, 128), (3, 2, 16, *col), (2, 16, *col), pltpu.SemaphoreType.DMA((8,))],
                name="ends", mib=16, anywhere=(5, 6), aliases={5: 0, 6: 1},
            )
        edge = WIDE if number == 2 else 3
        x_edge, y_edge = f32(edge * 128, 128), f32(32, edge, *col)
        current, *edges = call(
            functools.partial(edge_rate, number, edge), (block, x_edge, x_edge, y_edge, y_edge),
            acc, start, current, velocity, *halo,
            scratch=[(6, 16, *col)], name="edge", mib=24, ops=512 * 30,
        )
        halo = star(*edges)
    xlo, xhi, ylo, yhi = halo
    levels = call(
        sweep_core, (block,) * SWEEPS, current,
        scratch=[block.shape, block.shape, (2, 16, *col), (2, 16, *col)], name="core", mib=8, ops=512 * 90,
    )
    corner = f32(CORNERS, *col)
    corner_low, corner_high = call(
        pack_corners, (corner, corner), xlo, xhi, levels[-1], name="corners", mib=4, anywhere=(2,)
    )
    clo, chi = moved(corner_high, "gy", 1), moved(corner_low, "gy", -1)
    ext = (32 + 2 * WIDE, 16 + 2 * WIDE, *col)
    new_rows, packed = call(
        finish, (f32(4096, 128), f32(16, 64, 128)), current, xlo, xhi, ylo, yhi, clo, chi, *levels,
        scratch=[ext] * 4 + [(34, 8, *col)] * 3 + [(2048, 128), (2, 28, *col), (2, 28, *col)],
        name="finish", mib=30, ops=512 * 250,
    )
    returned = lax.all_to_all(packed, "gy", split_axis=0, concat_axis=0, tiled=True).reshape(16, 2, 4, 8, 128)
    new_level = new_rows.reshape(32, 2, 8, 8, 128).transpose(0, 1, 3, 2, 4).reshape(32, 16, 1024)
    flows = [returned[:, k].transpose(0, 2, 1, 3).reshape(1, 128, 512) for k in range(2)]
    return (new_level, flows[0], flows[1])


def solution(mesh):
    placed = (P("gx", "gy", None), P(None, ("gx", "gy"), None, None), P("gx", "gy", None))
    return jax.shard_map(
        per_device,
        mesh=mesh,
        in_specs=placed,
        out_specs=(P("gx", "gy", None), P(("gx", "gy"), None, None), P(("gx", "gy"), None, None)),
        check_vma=False,
    )
```

```python
import functools

import jax
import jax.numpy as jnp
from jax import lax
from jax.experimental import pallas as pl
from jax.experimental.pallas import tpu as pltpu
from jax.sharding import PartitionSpec as P

SWEEPS = 4
TIME_STEP = 0.25
PSEUDO_STEP = 0.3
EPS = 1e-06
FRONT = 1.5
WIDE = SWEEPS + 2

ROWS, LANES = 8, 128
HIGH = lax.Precision.HIGHEST


def params(mib):
    return pltpu.CompilerParams(vmem_limit_bytes=mib * 2**20)


def f32(*shape):
    return jax.ShapeDtypeStruct(shape, jnp.float32)


def cost(vector_ops):
    return pl.CostEstimate(flops=vector_ops * 1024, bytes_accessed=2**23, transcendentals=0)


def shifted(col, step):
    lane = lax.broadcasted_iota(jnp.int32, (ROWS, LANES), 1)
    turned = pltpu.roll(col, (-step) % LANES, 1)
    if step > 0:
        return jnp.where(lane >= LANES - step, pltpu.roll(turned, ROWS - 1, 0), turned)
    return jnp.where(lane < -step, pltpu.roll(turned, 1, 0), turned)


def inverse(values):
    return pl.reciprocal(values, approx=True)


def correction(rough1, rough2, rough3, third1, third2):
    r1, r2, r3 = inverse(rough1), inverse(rough2), inverse(rough3)
    w1 = r1 * r1
    w12 = w1 + 6.0 * (r2 * r2)
    w3 = 3.0 * (r3 * r3)
    return (4.0 * w1 * third1 + (w3 - w12) * third2) * inverse(w12 + w3)


def upwind_part(speed, central, corr):
    return speed * central + jnp.abs(speed) * corr


class March:
    def __init__(self, get):
        self.get = get
        self.made = {}

    def once(self, name, j, make):
        key = (name, j)
        if key not in self.made:
            self.made[key] = make()
        return self.made[key]

    def p(self, j):
        return self.once("p", j, lambda: self.get(j))

    def d(self, j):
        return self.once("d", j, lambda: self.p(j + 1) - self.p(j))

    def curve(self, j):
        return self.once("c", j, lambda: self.d(j) - self.d(j - 1))

    def gap(self, j):
        return self.once("g", j, lambda: self.curve(j + 1) - self.curve(j))

    def third(self, j):
        return self.once("t", j, lambda: self.gap(j) - self.gap(j - 1))

    def base(self, j):
        return self.once("h", j, lambda: (4.0 / 3.0) * (self.gap(j) * self.gap(j)) + EPS)

    def cross(self, j):
        return self.once("x", j, lambda: self.curve(j) * self.curve(j + 1))

    def twice(self, j):
        return self.once("a", j, lambda: (self.curve(j) + self.curve(j)) * self.curve(j))

    def less(self, j):
        return self.once("l", j, lambda: self.base(j) - self.cross(j))

    def mid(self, j):
        return self.once("m", j, lambda: self.base(j) + self.cross(j))

    def up(self, j):
        return self.once("u", j, lambda: self.less(j) + self.twice(j + 1))

    def down(self, j):
        return self.once("v", j, lambda: self.less(j) + self.twice(j))

    def central(self, i):
        return 6.0 * (self.p(i + 1) - self.p(i - 1)) - (self.gap(i) + self.gap(i - 1))

    def part(self, i, speed):
        minus = speed < 0
        corr = correction(
            jnp.where(minus, self.up(i - 2), self.down(i + 1)),
            jnp.where(minus, self.mid(i - 1), self.mid(i)),
            jnp.where(minus, self.down(i), self.up(i - 1)),
            jnp.where(minus, self.third(i - 1), self.third(i + 1)),
            self.third(i),
        )
        return upwind_part(speed, self.central(i), corr)


def depth_rate(slope, here, turned, speed):
    m2, m1, p1, p2 = turned
    minus = speed < 0
    a = jnp.where(minus, m2, p2)
    b = jnp.where(minus, m1, p1)
    d = jnp.where(minus, p1, m1)
    g1, g2, g3 = b - a, here - b, d - here
    corr = correction(
        (4.0 / 3.0) * (g1 * g1) + EPS + b * (b + g1),
        (4.0 / 3.0) * (g2 * g2) + EPS + b * here,
        (4.0 / 3.0) * (g3 * g3) + EPS + here * (here - g3),
        g2 - g1,
        g3 - g2,
    )
    return upwind_part(speed, slope - (p1 - m1), corr)


def depth_part(col, speed):
    before, after = shifted(col, -1), shifted(col, 1)
    here = (after - col) - (col - before)
    return depth_rate(6.0 * (after - before), here, [shifted(here, step) for step in (-2, -1, 1, 2)], speed)


def loop(low, high, body):
    def step(i, carry):
        body(i)
        return carry

    lax.fori_loop(low, high, step, 0)


def pack_velocity(rows_ref, out_ref):
    def to(g):
        for c in range(3):
            for r in range(10):
                block, low = (g, r - 1) if 1 <= r <= 8 else ((g + 15, 7) if r == 0 else (g + 1, 0))
                start = c * 512 + lax.rem(block, 16) * 32 + low
                out_ref[g, pl.ds((c * 10 + r) * 4, 4), :] = rows_ref[pl.ds(start, 4, stride=8), :]

    loop(0, 16, to)


def unpack_level(rows_ref, p_ref, ylo_ref, yhi_ref):
    def to(x):
        for y in range(16):
            col = rows_ref[pl.ds(x * 128 + (y // 8) * 64 + y % 8, 8, stride=8), :]
            p_ref[x, y] = col
            if y < 3:
                ylo_ref[x, y] = col
            if y >= 13:
                yhi_ref[x, y - 13] = col

    loop(0, 32, to)


def refine_table():
    k = lax.broadcasted_iota(jnp.int32, (256, 256), 0)
    n = lax.broadcasted_iota(jnp.int32, (256, 256), 1)
    beside = jnp.where(n % 2 == 0, n // 2 - 1, n // 2 + 1)
    beside = jnp.where(beside < 0, 255, jnp.where(beside > 127, 128, beside))
    return jnp.where(k == n // 2, 0.75, 0.0) + jnp.where(k == beside, 0.25, 0.0)


def refine_z(plane, table):
    count = plane.shape[0]
    row = lax.broadcasted_iota(jnp.int32, plane.shape, 0) % 4
    lane = lax.broadcasted_iota(jnp.int32, plane.shape, 1)
    after = jnp.where(row == 3, pltpu.roll(plane, 3, 0), pltpu.roll(plane, count - 1, 0))
    prior = jnp.where(row == 0, pltpu.roll(plane, count - 3, 0), pltpu.roll(plane, 1, 0))
    wide = jnp.concatenate([plane, jnp.where(lane < 64, after, prior)], axis=1)
    out = jnp.dot(wide, table, precision=HIGH, preferred_element_type=jnp.float32)
    return out[:, :128], out[:, 128:]


def band_blocks(band_ref):
    k = lax.broadcasted_iota(jnp.int32, (64, 128), 0)
    n = lax.broadcasted_iota(jnp.int32, (64, 128), 1)
    spread = jnp.where(lax.rem(k, 8) == lax.div(n, 16), -TIME_STEP / 12.0, 0.0)
    row = lax.broadcasted_iota(jnp.int32, (8, 64), 0)
    tile = lax.div(lax.broadcasted_iota(jnp.int32, (8, 64), 1), 8)
    blocks = []
    for half in range(2):
        mask = jnp.broadcast_to(band_ref[half].astype(jnp.float32), (8, 64))
        mask = jnp.where(row == tile, mask, 0.0)
        blocks.append(jnp.dot(mask, spread, precision=HIGH, preferred_element_type=jnp.float32))
    return blocks


def refine_inner(mid_ref, band_ref, v_ref, ends_ref, fine, band):
    table = refine_table()
    for half, block in enumerate(band_blocks(band_ref)):
        band[half] = block

    def along_z(k):
        left, right = refine_z(mid_ref[pl.ds(k * 480, 480), :], table)
        fine[pl.ds(k * 960, 480, stride=2), :] = left
        fine[pl.ds(k * 960 + 1, 480, stride=2), :] = right

    loop(0, 4, along_z)
    for end, plane in enumerate((0, 15)):
        ends_ref[end] = fine[pl.ds(plane * 240, 240), :]

    def along_xy(i):
        for c in range(3):
            near, far = [], []
            for r in range(10):
                at = (c * 10 + r) * 8
                near.append(fine[pl.ds(i * 240 + at, 8), :])
                far.append(fine[pl.ds(i * 240 + 240 + at, 8), :])
            for k in range(2):
                x = 2 * i + 1 + k
                line = [0.75 * a + 0.25 * b for a, b in (zip(far, near) if k else zip(near, far))]
                along_y(c, x, line, band[lax.div(x, 16)], v_ref)

    loop(0, 15, along_xy)


def along_y(c, x, line, band, v_ref):
    scaled = [band * value for value in line]
    for y in range(16):
        m = y // 2 + 1
        v_ref[c, x, y] = 0.75 * scaled[m] + 0.25 * scaled[m - 1 + 2 * (y % 2)]


def refine_ends(lo_ref, hi_ref, ends_ref, band_ref, p_ref, v_in, acc_in, v_out, acc_out, fine, ends, part, sems):
    table = refine_table()
    blocks = band_blocks(band_ref)
    for side, ref in enumerate((lo_ref, hi_ref)):
        left, right = refine_z(ref[pl.ds(384, 120), :], table)
        fine[pl.ds(side * 240, 120, stride=2), :] = left
        fine[pl.ds(side * 240 + 1, 120, stride=2), :] = right
    for side in range(2):
        for c in range(3):
            line = []
            for r in range(10):
                at = (c * 10 + r) * 8
                line.append(0.75 * ends_ref[side, pl.ds(at, 8), :] + 0.25 * fine[pl.ds(side * 240 + at, 8), :])
            along_y(c, side, line, blocks[side], ends)
    for side in range(2):
        x = 31 * side
        march = March(lambda y: p_ref[x, y])
        for y in range(16):
            total = depth_part(march.p(y), ends[2, side, y])
            if 3 <= y < 13:
                total = total + march.part(y, ends[1, side, y])
            part[side, y] = total
    copies = []
    for side in range(2):
        copies.append((part.at[side], acc_out.at[31 * side]))
        for c in range(3):
            copies.append((ends.at[c, side], v_out.at[c, 31 * side]))
    copies = [pltpu.make_async_copy(src, dst, sems.at[k]) for k, (src, dst) in enumerate(copies)]
    for copy in copies:
        copy.start()
    for copy in copies:
        copy.wait()


def inner_rate(first, p_ref, v_ref, acc_ref, curve, slope, even, odd):
    def x_line(y):
        march = March(lambda x: p_ref[x, y])
        for x in range(32):
            col = march.p(x)
            before, after = shifted(col, -1), shifted(col, 1)
            curve[x, y] = (after - col) - (col - before)
            slope[x, y] = 6.0 * (after - before)
            if 3 <= x < 29:
                acc_ref[x, y] = march.part(x, v_ref[0, x, y])
            else:
                acc_ref[x, y] = jnp.zeros((ROWS, LANES), jnp.float32)

    loop(0, 16, x_line)

    def turn(x, turned):
        for y in range(16):
            col = curve[x, y]
            for k, step in enumerate((-2, -1, 1, 2)):
                turned[k, y] = shifted(col, step)

    def y_line(x, turned):
        march = March(lambda y: p_ref[x, y])
        for y in range(16):
            total = acc_ref[x, y] + depth_rate(slope[x, y], curve[x, y], [turned[k, y] for k in range(4)], v_ref[2, x, y])
            if 3 <= y < 13:
                total = total + march.part(y, v_ref[1, x, y])
            acc_ref[x, y] = total

    low = 1 if first else 0
    count = 30 if first else 32
    turn(low, even)

    def two(k):
        x = low + 2 * k
        turn(x + 1, odd)
        y_line(x, even)
        turn(jnp.minimum(x + 2, 31), even)
        y_line(x + 1, odd)

    loop(0, count // 2, two)


def section(start, current, rate, number):
    if number == 0:
        return current + rate
    if number == 1:
        return 0.75 * start + 0.25 * (current + rate)
    return start * (1.0 / 3.0) + (2.0 / 3.0) * (current + rate)


def turned_about(number, *pairs):
    return [pair[::-1] if number % 2 else pair for pair in pairs]


def edge_rate(
    number, edge, acc_ref, start_ref, p_ref, v_ref, x1_ref, x2_ref, y1_ref, y2_ref,
    new_ref, nxlo_ref, nxhi_ref, nylo_ref, nyhi_ref, side,
):
    (xlo_ref, xhi_ref), (ylo_ref, yhi_ref) = turned_about(number, (x1_ref, x2_ref), (y1_ref, y2_ref))

    def from_rows(ref, x, y):
        return ref[pl.ds((x * 16 + y) * 8, 8), :]

    def x_line(y):
        low = March(lambda x: from_rows(xlo_ref, x + 3, y) if x < 0 else p_ref[x, y])
        high = March(lambda x: from_rows(xhi_ref, x - 32, y) if x >= 32 else p_ref[x, y])
        for k in range(3):
            side[k, y] = low.part(k, v_ref[0, k, y])
            side[k + 3, y] = high.part(29 + k, v_ref[0, 29 + k, y])

    loop(0, 16, x_line)

    def y_line(x, side_x, outs):
        low = March(lambda y: ylo_ref[x, y + 3] if y < 0 else p_ref[x, y])
        high = March(lambda y: yhi_ref[x, y - 16] if y >= 16 else p_ref[x, y])
        for y in range(16):
            rate = acc_ref[x, y]
            if side_x is not None:
                rate = rate + side[side_x, y]
            if y < 3:
                rate = rate + low.part(y, v_ref[1, x, y])
            if y >= 13:
                rate = rate + high.part(y, v_ref[1, x, y])
            start = None if number == 0 else start_ref[x, y]
            new = section(start, p_ref[x, y], rate, number)
            new_ref[x, y] = new
            if outs is not None:
                outs[0][pl.ds((outs[1] * 16 + y) * 8, 8), :] = new
            if y < edge:
                nylo_ref[x, y] = new
            if y >= 16 - edge:
                nyhi_ref[x, y - (16 - edge)] = new

    loop(0, 3, lambda x: y_line(x, x, (nxlo_ref, x)))
    loop(29, 32, lambda x: y_line(x, x - 26, (nxhi_ref, x - (32 - edge))))
    if edge > 3:
        loop(3, edge, lambda x: y_line(x, None, (nxlo_ref, x)))
        loop(32 - edge, 29, lambda x: y_line(x, None, (nxhi_ref, x - (32 - edge))))
    loop(edge, 32 - edge, lambda x: y_line(x, None, None))


def pushes(col):
    push = (PSEUDO_STEP * col) * lax.rsqrt(col * col + 1.0)
    return push, jnp.where(col > 0, 1.0, -1.0)


def turn(src, x, ys, turned):
    for y in ys:
        col = src[x, y]
        turned[0, y] = shifted(col, -1)
        turned[1, y] = shifted(col, 1)


def sweep_line(src, dst, push, sign, x, ys, turned):
    cols = {}

    def at(y):
        if y not in cols:
            cols[y] = src[x, y]
        return cols[y]

    for y in ys:
        col, c, s = at(y), push[x, y], sign[x, y]
        here = s * col
        total = None
        for pair in ((src[x - 1, y], src[x + 1, y]), (at(y - 1), at(y + 1)), (turned[0, y], turned[1, y])):
            floor = 1e-15 if total is None else 0.0
            rise = jnp.maximum(here - jnp.minimum(s * pair[0], s * pair[1]), floor)
            total = rise * rise if total is None else total + rise * rise
        dst[x, y] = (col + c) - (c * total) * lax.rsqrt(total)


def sweep_rows(src, dst, push, sign, place, pairs, ys, even, odd):
    turn(src, place(0), ys, even)

    def two(j):
        x = place(j)
        turn(src, x + 1, ys, odd)
        sweep_line(src, dst, push, sign, x, ys, even)
        turn(src, place(jnp.minimum(j + 1, pairs - 1)), ys, even)
        sweep_line(src, dst, push, sign, x + 1, ys, odd)

    loop(0, pairs, two)


def sweep_core(adv_ref, *refs):
    levels, (push, sign, even, odd) = refs[:SWEEPS], refs[SWEEPS:]

    def prepare(x):
        for y in range(16):
            push[x, y], sign[x, y] = pushes(adv_ref[x, y])

    loop(0, 32, prepare)
    src = adv_ref
    for k in range(1, SWEEPS + 1):
        dst = levels[k - 1]
        sweep_rows(src, dst, push, sign, lambda j, k=k: k + 2 * j, 16 - k, range(k, 16 - k), even, odd)
        src = dst


def pack_corners(xhi_ref, xlo_ref, _, low_ref, high_ref):
    k = 0
    for dx in range(1, WIDE):
        for ref, x in ((xlo_ref, WIDE - dx), (xhi_ref, dx - 1)):
            for dy in range(1, WIDE - dx + 1):
                low_ref[k] = ref[pl.ds((x * 16 + dy - 1) * 8, 8), :]
                high_ref[k] = ref[pl.ds((x * 16 + 16 - dy) * 8, 8), :]
                k += 1


CORNERS = WIDE * (WIDE - 1)


def normals(last, xs, nx, ny, nz, at):
    cols = {}

    def col(y):
        if y not in cols:
            cols[y] = last[xs, y + WIDE]
        return cols[y]

    across, along, deep = {}, {}, {}
    for y in range(-1, 17):
        gx = last[xs + 1, y + WIDE] - last[xs - 1, y + WIDE]
        gy = col(y + 1) - col(y - 1)
        gz = shifted(col(y), 1) - shifted(col(y), -1)
        scale = lax.rsqrt(gx * gx + gy * gy + gz * gz + 4.0)
        across[y], along[y], deep[y] = gx * scale, gy * scale, gz * scale
    for j in range(8):
        a, b = 2 * j, 2 * j + 1
        nx[at, j] = across[a] + across[b]
        ny[at, j] = (along[b] + along[b + 1]) - (along[a - 1] + along[a])
        nz[at, j] = deep[a] + deep[b]


def gather(last, xs, nx, ny, nz, at, lump, slot, half, new, new_at):
    a, b = at, at + 1
    for j in range(8):
        deep = nz[a, j] + nz[b, j]
        total = (nx[b, j] + nx[b + 1, j]) - (nx[a - 1, j] + nx[a, j]) + (ny[a, j] + ny[b, j])
        lump[pl.ds(slot * 64 + j * 8, 8), :] = total + (shifted(deep, 1) - shifted(deep, -1))
        share = None
        for x in range(2):
            for y in range(2):
                yy = 2 * j + y
                col = last[xs + x, yy + WIDE]
                new[pl.ds(new_at + x * 128 + (yy // 8) * 64 + yy % 8, 8, stride=8), :] = col
                bend = jnp.tanh(col * (1.0 / FRONT))
                share = bend if share is None else share + bend
        lump[pl.ds(half + slot * 64 + j * 8, 8), :] = share


def restrict(lump, slots, half, send, send_at):
    k = lax.broadcasted_iota(jnp.int32, (256, 128), 0)
    n = lax.broadcasted_iota(jnp.int32, (256, 128), 1)
    table = jnp.where(lax.div(k, 2) == n, 1.0 / 16.0, 0.0)
    halves = []
    for odd_row in range(2):
        rows = []
        for kind in range(2):
            for i in slots:
                base = kind * half + i * 64 + odd_row
                rows += [lump[pl.ds(base + 2 * z, 8, stride=8), :] for z in range(4)]
        halves.append(jnp.concatenate(rows, axis=0))
    out = jnp.dot(jnp.concatenate(halves, axis=1), table, precision=HIGH, preferred_element_type=jnp.float32)
    for n, i in enumerate(slots):
        send[send_at(i), pl.ds(0, 32), :] = out[n * 32 : n * 32 + 32]
        send[send_at(i), pl.ds(32, 32), :] = out[(len(slots) + n) * 32 : (len(slots) + n) * 32 + 32] + 0.5


def sweep_sides(
    adv_ref, yhi_ref, ylo_ref, one_ref, two_ref, three_ref, four_ref,
    rims_ref, last_ref, q0, q1, push, sign, even, odd,
):
    w = WIDE
    size_y = 16 + 2 * w

    def put(x, y, col):
        q0[x, y] = col
        push[x, y], sign[x, y] = pushes(col)

    def fill(x):
        for y in range(w):
            put(x, y, ylo_ref[x, y])
            put(x, y + 16 + w, yhi_ref[x, y])
        for y in (0, 1, 2, 3, 12, 13, 14, 15):
            put(x, y + w, adv_ref[x, y])

    loop(0, 32, fill)
    src, dst = q0, q1
    for k, core_ref in enumerate((one_ref, two_ref, three_ref, four_ref), 1):
        dst = last_ref if k == SWEEPS else dst
        sides = [*range(k, k + w), *range(size_y - k - w, size_y - k)]
        sweep_rows(src, dst, push, sign, lambda j, k=k: k + 2 * j, 16 - k, sides, even, odd)
        inside = (k, k + 1, 14 - k, 15 - k) if k < SWEEPS else range(k, 16 - k)

        def take(x, core_ref=core_ref, inside=inside, dst=dst):
            for y in inside:
                dst[x, y + w] = core_ref[x, y]

        loop(k, 32 - k, take)
        if k < SWEEPS:
            for r, x in enumerate((k, k + 1, 30 - k, 31 - k)):
                for y in range(k, size_y - k):
                    inner = k + 2 <= y - w < 14 - k
                    rims_ref[k - 1, r, y] = core_ref[x, y - w] if inner else dst[x, y]
        src, dst = dst, src


def inner_outputs(last, new_ref, send_ref, nx, ny, nz, lump):
    loop(0, 22, lambda r: normals(last, r + 5, nx, ny, nz, r))

    def planes(n):
        gather(last, 2 * n + 6, nx, ny, nz, 2 * n + 1, lump, n, 640, new_ref, (2 * n + 6) * 128)

    loop(0, 10, planes)
    for x in (4, 5, 26, 27):
        for y in range(16):
            new_ref[pl.ds(x * 128 + (y // 8) * 64 + y % 8, 8, stride=8), :] = last[x, y + WIDE]
    for part in range(2):
        restrict(lump, range(5 * part, 5 * part + 5), 640, send_ref, lambda i: i)


def finish(
    adv_ref, xhi_ref, xlo_ref, yhi_ref, ylo_ref, clo_ref, chi_ref, rims_ref, rows_ref, send_mid_ref, _,
    new_ref, send_ref, q0, q1, push, sign, nx, ny, nz, lump, even, odd, ends, sems,
):
    w = WIDE
    size_x, size_y = 32 + 2 * w, 16 + 2 * w

    def put(x, y, col):
        q0[x, y] = col
        push[x, y], sign[x, y] = pushes(col)

    def fill_mid(r):
        x = r + jnp.where(r >= 4, 24, 0)
        for y in range(w):
            put(x + w, y, ylo_ref[x, y])
            put(x + w, y + 16 + w, yhi_ref[x, y])
        for y in range(16):
            put(x + w, y + w, adv_ref[x, y])

    def fill_side(x):
        for y in range(16):
            put(x, y + w, xlo_ref[pl.ds((x * 16 + y) * 8, 8), :])
            put(x + 32 + w, y + w, xhi_ref[pl.ds((x * 16 + y) * 8, 8), :])

    loop(0, 8, fill_mid)
    loop(0, w, fill_side)
    k = 0
    for dx in range(1, w):
        for x in (w - dx, w + 31 + dx):
            for dy in range(1, w - dx + 1):
                put(x, w - dy, clo_ref[k])
                put(x, w + 15 + dy, chi_ref[k])
                k += 1

    src, dst = q0, q1
    for k in range(1, SWEEPS + 1):

        def end_rows(j, k=k):
            return k + 2 * j + jnp.where(j >= 3, 32 - 2 * k, 0)

        sweep_rows(src, dst, push, sign, end_rows, 6, range(k, size_y - k), even, odd)
        if k < SWEEPS:
            for r, x in enumerate((k, k + 1, 30 - k, 31 - k)):
                for y in range(k, size_y - k):
                    dst[x + w, y] = rims_ref[k - 1, r, y]
        src, dst = dst, src
    last = src

    def take(r):
        x = SWEEPS + r + jnp.where(r >= 4, 16, 0)
        for y in range(SWEEPS, size_y - SWEEPS):
            last[x + w, y] = rows_ref[x, y]

    loop(0, 8, take)
    loop(0, 16, lambda r: normals(last, r + w - 1 + jnp.where(r >= 8, 18, 0), nx, ny, nz, r))

    def planes(n):
        far = jnp.where(n >= 3, 1, 0)
        gather(last, 2 * n + w + 20 * far, nx, ny, nz, 2 * n + 1 + 2 * far, lump, n, 384, ends, n * 256)

    loop(0, 6, planes)
    copies = [
        pltpu.make_async_copy(ends.at[pl.ds(1024 * k, 512)], new_ref.at[pl.ds(3584 * k, 512)], sems.at[k])
        for k in range(2)
    ]
    for copy in copies:
        copy.start()
    restrict(lump, range(6), 384, send_ref, lambda i: i + (10 if i >= 3 else 0))
    send_ref[pl.ds(3, 10)] = send_mid_ref[...]
    for copy in copies:
        copy.wait()


def call(kernel, outs, *args, scratch=(), mib=48, ops=1000, name=None, anywhere=(), aliases=None):
    def spec(k):
        return pl.BlockSpec(memory_space=pl.ANY if k in anywhere else pltpu.VMEM)

    aliases = aliases or {}
    flat = outs if isinstance(outs, tuple) else (outs,)
    specs = tuple(pl.BlockSpec(memory_space=pl.ANY if k in aliases.values() else pltpu.VMEM) for k in range(len(flat)))
    return pl.pallas_call(
        kernel,
        out_shape=outs,
        in_specs=[spec(k) for k in range(len(args))],
        out_specs=specs if isinstance(outs, tuple) else specs[0],
        scratch_shapes=[pltpu.VMEM(s, jnp.float32) if isinstance(s, tuple) else s for s in scratch],
        input_output_aliases=aliases,
        compiler_params=params(mib),
        cost_estimate=cost(ops),
        name=name,
    )(*args)


def moved(values, axis, step):
    count = lax.axis_size(axis)
    return lax.ppermute(values, axis, [(i, (i + step) % count) for i in range(count)])


def star(xlo, xhi, ylo, yhi):
    return (moved(xhi, "gx", 1), moved(xlo, "gx", -1), moved(yhi, "gy", 1), moved(ylo, "gy", -1))


def per_device(level_set, flow_velocity, band_mask):
    col = (ROWS, LANES)
    block = f32(32, 16, *col)
    level_rows = level_set.reshape(32, 2, 8, 8, 128).transpose(0, 1, 3, 2, 4).reshape(4096, 128)
    flow_rows = flow_velocity.reshape(3, 16, 8, 4, 128).transpose(0, 1, 3, 2, 4).reshape(1536, 128)

    send = call(pack_velocity, f32(16, 120, 128), flow_rows, name="pack", mib=8)
    coarse = lax.all_to_all(send, "gy", split_axis=0, concat_axis=0, tiled=True)
    start, ylo, yhi = call(
        unpack_level, (block, f32(32, 3, *col), f32(32, 3, *col)), level_rows, name="unpack", mib=8
    )
    xlo = jnp.concatenate([start[:3].reshape(384, 128), coarse[0]], axis=0)
    xhi = jnp.concatenate([start[29:].reshape(384, 128), coarse[15]], axis=0)
    halo = star(xlo, xhi, ylo, yhi)
    velocity, ends = call(
        refine_inner, (f32(3, 32, 16, *col), f32(2, 240, 128)), coarse.reshape(1920, 128), band_mask,
        scratch=[(3840, 128), (2, *col)], name="refine", mib=24,
    )
    current = start
    for number in range(3):
        acc = call(
            functools.partial(inner_rate, number == 0), block, current, velocity,
            scratch=[block.shape, block.shape, (4, 16, *col), (4, 16, *col)], name="inner", mib=24, ops=512 * 140,
        )
        if number == 0:
            velocity, acc = call(
                refine_ends, (f32(3, 32, 16, *col), block), halo[0], halo[1], ends, band_mask, current, velocity, acc,
                scratch=[(480, 128), (3, 2, 16, *col), (2, 16, *col), pltpu.SemaphoreType.DMA((8,))],
                name="ends", mib=16, anywhere=(5, 6), aliases={5: 0, 6: 1},
            )
        edge = WIDE if number == 2 else 3
        x_edge, y_edge = f32(edge * 128, 128), f32(32, edge, *col)
        current, *edges = call(
            functools.partial(edge_rate, number, edge), (block, x_edge, x_edge, y_edge, y_edge),
            acc, start, current, velocity, *sum(turned_about(number, halo[:2], halo[2:]), ()),
            scratch=[(6, 16, *col)], name="edge", mib=24, ops=512 * 30,
        )
        halo = star(*edges)
    xlo, xhi, ylo, yhi = halo
    levels = call(
        sweep_core, (block,) * SWEEPS, current,
        scratch=[block.shape, block.shape, (2, 16, *col), (2, 16, *col)], name="core", mib=8, ops=512 * 90,
    )
    corner = f32(CORNERS, *col)
    turns = [(2, 16 + 2 * WIDE, *col)] * 2
    side = (32, 16 + 2 * WIDE, *col)
    rims, last = call(
        sweep_sides, (f32(3, 4, *side[1:]), f32(*side)), current, yhi, ylo, *levels,
        scratch=[side] * 4 + turns, name="sides", mib=20, ops=512 * 70,
    )
    corner_low, corner_high = call(
        pack_corners, (corner, corner), xhi, xlo, rims, name="corners", mib=4, anywhere=(2,)
    )
    new_rows, send_mid = call(
        inner_outputs, (f32(4096, 128), f32(10, 64, 128)), last,
        scratch=[(22, 8, *col)] * 3 + [(1280, 128)], name="outputs", mib=12, ops=512 * 40,
    )
    clo, chi = moved(corner_high, "gy", 1), moved(corner_low, "gy", -1)
    ext = (32 + 2 * WIDE, 16 + 2 * WIDE, *col)
    new_rows, packed = call(
        finish, (f32(4096, 128), f32(16, 64, 128)),
        current, xhi, xlo, yhi, ylo, clo, chi, rims, last, send_mid, new_rows,
        scratch=[ext] * 4 + [(16, 8, *col)] * 3 + [(768, 128)] + turns + [(1536, 128), pltpu.SemaphoreType.DMA((2,))],
        name="finish", mib=30, ops=512 * 250, anywhere=(10,), aliases={10: 0},
    )
    returned = lax.all_to_all(packed, "gy", split_axis=0, concat_axis=0, tiled=True).reshape(16, 2, 4, 8, 128)
    new_level = new_rows.reshape(32, 2, 8, 8, 128).transpose(0, 1, 3, 2, 4).reshape(32, 16, 1024)
    flows = [returned[:, k].transpose(0, 2, 1, 3).reshape(1, 128, 512) for k in range(2)]
    return (new_level, flows[0], flows[1])


def solution(mesh):
    placed = (P("gx", "gy", None), P(None, ("gx", "gy"), None, None), P("gx", "gy", None))
    return jax.shard_map(
        per_device,
        mesh=mesh,
        in_specs=placed,
        out_specs=(P("gx", "gy", None), P(("gx", "gy"), None, None), P(("gx", "gy"), None, None)),
        check_vma=False,
    )
```

```python
import functools

import jax
import jax.numpy as jnp
from jax import lax
from jax.experimental import pallas as pl
from jax.experimental.pallas import tpu as pltpu
from jax.sharding import PartitionSpec as P

SWEEPS = 4
TIME_STEP = 0.25
PSEUDO_STEP = 0.3
EPS = 1e-06
FRONT = 1.5
WIDE = SWEEPS + 2

ROWS, LANES = 8, 128
HIGH = lax.Precision.HIGHEST


def params(mib):
    return pltpu.CompilerParams(vmem_limit_bytes=mib * 2**20)


def f32(*shape):
    return jax.ShapeDtypeStruct(shape, jnp.float32)


def cost(vector_ops):
    return pl.CostEstimate(flops=vector_ops * 1024, bytes_accessed=2**23, transcendentals=0)


def shifted(col, step):
    lane = lax.broadcasted_iota(jnp.int32, (ROWS, LANES), 1)
    turned = pltpu.roll(col, (-step) % LANES, 1)
    if step > 0:
        return jnp.where(lane >= LANES - step, pltpu.roll(turned, ROWS - 1, 0), turned)
    return jnp.where(lane < -step, pltpu.roll(turned, 1, 0), turned)


def inverse(values):
    return pl.reciprocal(values, approx=True)


def correction(rough1, rough2, rough3, third1, third2):
    r1, r2, r3 = inverse(rough1), inverse(rough2), inverse(rough3)
    w1 = r1 * r1
    w12 = w1 + 6.0 * (r2 * r2)
    w3 = 3.0 * (r3 * r3)
    return (4.0 * w1 * third1 + (w3 - w12) * third2) * inverse(w12 + w3)


def upwind_part(speed, central, corr):
    return speed * central + jnp.abs(speed) * corr


class March:
    def __init__(self, get):
        self.get = get
        self.made = {}

    def once(self, name, j, make):
        key = (name, j)
        if key not in self.made:
            self.made[key] = make()
        return self.made[key]

    def p(self, j):
        return self.once("p", j, lambda: self.get(j))

    def d(self, j):
        return self.once("d", j, lambda: self.p(j + 1) - self.p(j))

    def curve(self, j):
        return self.once("c", j, lambda: self.d(j) - self.d(j - 1))

    def gap(self, j):
        return self.once("g", j, lambda: self.curve(j + 1) - self.curve(j))

    def third(self, j):
        return self.once("t", j, lambda: self.gap(j) - self.gap(j - 1))

    def base(self, j):
        return self.once("h", j, lambda: (4.0 / 3.0) * (self.gap(j) * self.gap(j)) + EPS)

    def cross(self, j):
        return self.once("x", j, lambda: self.curve(j) * self.curve(j + 1))

    def twice(self, j):
        return self.once("a", j, lambda: (self.curve(j) + self.curve(j)) * self.curve(j))

    def less(self, j):
        return self.once("l", j, lambda: self.base(j) - self.cross(j))

    def mid(self, j):
        return self.once("m", j, lambda: self.base(j) + self.cross(j))

    def up(self, j):
        return self.once("u", j, lambda: self.less(j) + self.twice(j + 1))

    def down(self, j):
        return self.once("v", j, lambda: self.less(j) + self.twice(j))

    def central(self, i):
        return 6.0 * (self.p(i + 1) - self.p(i - 1)) - (self.gap(i) + self.gap(i - 1))

    def part(self, i, speed):
        minus = speed < 0
        corr = correction(
            jnp.where(minus, self.up(i - 2), self.down(i + 1)),
            jnp.where(minus, self.mid(i - 1), self.mid(i)),
            jnp.where(minus, self.down(i), self.up(i - 1)),
            jnp.where(minus, self.third(i - 1), self.third(i + 1)),
            self.third(i),
        )
        return upwind_part(speed, self.central(i), corr)


def depth_rate(slope, here, turned, speed):
    m2, m1, p1, p2 = turned
    minus = speed < 0
    a = jnp.where(minus, m2, p2)
    b = jnp.where(minus, m1, p1)
    d = jnp.where(minus, p1, m1)
    g1, g2, g3 = b - a, here - b, d - here
    corr = correction(
        (4.0 / 3.0) * (g1 * g1) + EPS + b * (b + g1),
        (4.0 / 3.0) * (g2 * g2) + EPS + b * here,
        (4.0 / 3.0) * (g3 * g3) + EPS + here * (here - g3),
        g2 - g1,
        g3 - g2,
    )
    return upwind_part(speed, slope - (p1 - m1), corr)


def loop(low, high, body):
    def step(i, carry):
        body(i)
        return carry

    lax.fori_loop(low, high, step, 0)


def pack_velocity(rows_ref, out_ref):
    def to(g):
        for c in range(3):
            for r in range(10):
                block, low = (g, r - 1) if 1 <= r <= 8 else ((g + 15, 7) if r == 0 else (g + 1, 0))
                start = c * 512 + lax.rem(block, 16) * 32 + low
                out_ref[g, pl.ds((c * 10 + r) * 4, 4), :] = rows_ref[pl.ds(start, 4, stride=8), :]

    loop(0, 16, to)


def unpack_level(rows_ref, p_ref, ylo_ref, yhi_ref):
    def to(x):
        for y in range(16):
            col = rows_ref[pl.ds(x * 128 + (y // 8) * 64 + y % 8, 8, stride=8), :]
            p_ref[x, y] = col
            if y < 3:
                ylo_ref[x, y] = col
            if y >= 13:
                yhi_ref[x, y - 13] = col

    loop(0, 32, to)


def refine_table():
    k = lax.broadcasted_iota(jnp.int32, (256, 256), 0)
    n = lax.broadcasted_iota(jnp.int32, (256, 256), 1)
    beside = jnp.where(n % 2 == 0, n // 2 - 1, n // 2 + 1)
    beside = jnp.where(beside < 0, 255, jnp.where(beside > 127, 128, beside))
    return jnp.where(k == n // 2, 0.75, 0.0) + jnp.where(k == beside, 0.25, 0.0)


def refine_z(plane, table):
    count = plane.shape[0]
    row = lax.broadcasted_iota(jnp.int32, plane.shape, 0) % 4
    lane = lax.broadcasted_iota(jnp.int32, plane.shape, 1)
    after = jnp.where(row == 3, pltpu.roll(plane, 3, 0), pltpu.roll(plane, count - 1, 0))
    prior = jnp.where(row == 0, pltpu.roll(plane, count - 3, 0), pltpu.roll(plane, 1, 0))
    wide = jnp.concatenate([plane, jnp.where(lane < 64, after, prior)], axis=1)
    out = jnp.dot(wide, table, precision=HIGH, preferred_element_type=jnp.float32)
    return out[:, :128], out[:, 128:]


def band_blocks(band_ref):
    k = lax.broadcasted_iota(jnp.int32, (64, 128), 0)
    n = lax.broadcasted_iota(jnp.int32, (64, 128), 1)
    spread = jnp.where(lax.rem(k, 8) == lax.div(n, 16), -TIME_STEP / 12.0, 0.0)
    row = lax.broadcasted_iota(jnp.int32, (8, 64), 0)
    tile = lax.div(lax.broadcasted_iota(jnp.int32, (8, 64), 1), 8)
    blocks = []
    for half in range(2):
        mask = jnp.broadcast_to(band_ref[half].astype(jnp.float32), (8, 64))
        mask = jnp.where(row == tile, mask, 0.0)
        blocks.append(jnp.dot(mask, spread, precision=HIGH, preferred_element_type=jnp.float32))
    return blocks


def refine_inner(mid_ref, band_ref, v_ref, ends_ref, fine, band):
    table = refine_table()
    for half, block in enumerate(band_blocks(band_ref)):
        band[half] = block

    def along_z(k):
        left, right = refine_z(mid_ref[pl.ds(k * 480, 480), :], table)
        fine[pl.ds(k * 960, 480, stride=2), :] = left
        fine[pl.ds(k * 960 + 1, 480, stride=2), :] = right

    loop(0, 4, along_z)
    for end, plane in enumerate((0, 15)):
        ends_ref[end] = fine[pl.ds(plane * 240, 240), :]

    def along_xy(i):
        for c in range(3):
            near, far = [], []
            for r in range(10):
                at = (c * 10 + r) * 8
                near.append(fine[pl.ds(i * 240 + at, 8), :])
                far.append(fine[pl.ds(i * 240 + 240 + at, 8), :])
            for k in range(2):
                x = 2 * i + 1 + k
                line = [0.75 * a + 0.25 * b for a, b in (zip(far, near) if k else zip(near, far))]
                along_y(c, x, line, band[lax.div(x, 16)], v_ref)

    loop(0, 15, along_xy)


def along_y(c, x, line, band, v_ref):
    scaled = [band * value for value in line]
    for y in range(16):
        m = y // 2 + 1
        v_ref[c, x, y] = 0.75 * scaled[m] + 0.25 * scaled[m - 1 + 2 * (y % 2)]


def refine_ends(lo_ref, hi_ref, ends_ref, band_ref, p_ref, tips_ref, v_in, acc_in, v_out, acc_out, fine, ends, part, sems):
    table = refine_table()
    blocks = band_blocks(band_ref)
    for side, ref in enumerate((lo_ref, hi_ref)):
        left, right = refine_z(ref[pl.ds(384, 120), :], table)
        fine[pl.ds(side * 240, 120, stride=2), :] = left
        fine[pl.ds(side * 240 + 1, 120, stride=2), :] = right
    for side in range(2):
        for c in range(3):
            line = []
            for r in range(10):
                at = (c * 10 + r) * 8
                line.append(0.75 * ends_ref[side, pl.ds(at, 8), :] + 0.25 * fine[pl.ds(side * 240 + at, 8), :])
            along_y(c, side, line, blocks[side], ends)
    for side in range(2):
        x = 31 * side
        march = March(lambda y: p_ref[x, y])
        for y in range(16):
            speed = ends[2, side, y]
            total = speed * jnp.where(speed < 0, tips_ref[side, 0, y], tips_ref[side, 1, y])
            if 3 <= y < 13:
                total = total + march.part(y, ends[1, side, y])
            part[side, y] = total
    copies = []
    for side in range(2):
        copies.append((part.at[side], acc_out.at[31 * side]))
        for c in range(3):
            copies.append((ends.at[c, side], v_out.at[c, 31 * side]))
    copies = [pltpu.make_async_copy(src, dst, sems.at[k]) for k, (src, dst) in enumerate(copies)]
    for copy in copies:
        copy.start()
    for copy in copies:
        copy.wait()


def inner_rate(p_ref, v_ref, acc_ref, curve, slope, even, odd):
    def x_line(y):
        march = March(lambda x: p_ref[x, y])
        for x in range(32):
            col = march.p(x)
            before, after = shifted(col, -1), shifted(col, 1)
            curve[x, y] = (after - col) - (col - before)
            slope[x, y] = 6.0 * (after - before)
            if 3 <= x < 29:
                acc_ref[x, y] = march.part(x, v_ref[0, x, y])
            else:
                acc_ref[x, y] = jnp.zeros((ROWS, LANES), jnp.float32)

    loop(0, 16, x_line)

    def turn(x, turned):
        for y in range(16):
            col = curve[x, y]
            for k, step in enumerate((-2, -1, 1, 2)):
                turned[k, y] = shifted(col, step)

    def y_line(x, turned):
        march = March(lambda y: p_ref[x, y])
        for y in range(16):
            total = acc_ref[x, y] + depth_rate(slope[x, y], curve[x, y], [turned[k, y] for k in range(4)], v_ref[2, x, y])
            if 3 <= y < 13:
                total = total + march.part(y, v_ref[1, x, y])
            acc_ref[x, y] = total

    turn(0, even)

    def two(k):
        x = 2 * k
        turn(x + 1, odd)
        y_line(x, even)
        turn(jnp.minimum(x + 2, 31), even)
        y_line(x + 1, odd)

    loop(0, 16, two)


def depth_both(slope, here, turned):
    m2, m1, p1, p2 = turned
    gm2, gm1, g0, g1 = m1 - m2, here - m1, p1 - here, p2 - p1
    bm2, bm1, b0, b1 = [(4.0 / 3.0) * (g * g) + EPS for g in (gm2, gm1, g0, g1)]
    third = g0 - gm1
    below = correction(bm2 + m1 * (m1 + gm2), bm1 + m1 * here, b0 + here * (here - g0), gm1 - gm2, third)
    above = correction(b1 + p1 * (p1 - g1), b0 + p1 * here, bm1 + here * (here + gm1), g1 - g0, third)
    central = slope - (p1 - m1)
    return central - below, central + above


def depth_sides(p_ref, both_ref, tips_ref, curve, slope, even, odd):
    def curves(x):
        for y in range(16):
            col = p_ref[x, y]
            before, after = shifted(col, -1), shifted(col, 1)
            curve[x, y] = (after - col) - (col - before)
            slope[x, y] = 6.0 * (after - before)

    def turned_row(x, turned):
        for y in range(16):
            col = curve[x, y]
            for k, step in enumerate((-2, -1, 1, 2)):
                turned[k, y] = shifted(col, step)

    def rates(x, turned):
        for y in range(16):
            both = depth_both(slope[x, y], curve[x, y], [turned[k, y] for k in range(4)])
            both_ref[0, x, y], both_ref[1, x, y] = both

    for x in range(3):
        curves(x)
    turned_row(0, even)

    def two(k):
        x = 2 * k
        turned_row(x + 1, odd)
        rates(x, even)
        turned_row(jnp.minimum(x + 2, 31), even)
        rates(x + 1, odd)
        curves(jnp.minimum(x + 3, 31))
        curves(jnp.minimum(x + 4, 31))

    loop(0, 16, two)
    for side in range(2):
        for k in range(2):
            for y in range(16):
                tips_ref[side, k, y] = both_ref[k, 31 * side, y]


def inner_rate_first(p_ref, v_ref, both_ref, acc_ref):
    def x_line(y):
        march = March(lambda x: p_ref[x, y])
        for x in range(32):
            if 3 <= x < 29:
                acc_ref[x, y] = march.part(x, v_ref[0, x, y])
            else:
                acc_ref[x, y] = jnp.zeros((ROWS, LANES), jnp.float32)

    def y_line(x):
        march = March(lambda y: p_ref[x, y])
        for y in range(16):
            speed = v_ref[2, x, y]
            total = acc_ref[x, y] + speed * jnp.where(speed < 0, both_ref[0, x, y], both_ref[1, x, y])
            if 3 <= y < 13:
                total = total + march.part(y, v_ref[1, x, y])
            acc_ref[x, y] = total

    loop(0, 16, x_line)
    loop(1, 31, y_line)


def refine_and_rate(mid_ref, band_ref, p_ref, both_ref, v_ref, ends_ref, acc_ref, fine, band):
    refine_inner(mid_ref, band_ref, v_ref, ends_ref, fine, band)
    inner_rate_first(p_ref, v_ref, both_ref, acc_ref)


def join_x(p_ref, coarse_ref, mark_ref, low_ref, high_ref):
    for x in range(3):
        for y in range(16):
            at = pl.ds((x * 16 + y) * 8, 8)
            low_ref[at, :] = p_ref[x, y]
            high_ref[at, :] = p_ref[29 + x, y]
    for k in range(15):
        low_ref[pl.ds(384 + 8 * k, 8), :] = coarse_ref[pl.ds(8 * k, 8), :]
        high_ref[pl.ds(384 + 8 * k, 8), :] = coarse_ref[pl.ds(1800 + 8 * k, 8), :]


def section(start, current, rate, number):
    if number == 0:
        return current + rate
    if number == 1:
        return 0.75 * start + 0.25 * (current + rate)
    return start * (1.0 / 3.0) + (2.0 / 3.0) * (current + rate)


def turned_about(number, *pairs):
    return [pair[::-1] if number % 2 else pair for pair in pairs]


def edge_rate(
    number, edge, acc_ref, start_ref, p_ref, v_ref, x1_ref, x2_ref, y1_ref, y2_ref,
    new_ref, nxlo_ref, nxhi_ref, nylo_ref, nyhi_ref, side,
):
    (xlo_ref, xhi_ref), (ylo_ref, yhi_ref) = turned_about(number, (x1_ref, x2_ref), (y1_ref, y2_ref))

    def from_rows(ref, x, y):
        return ref[pl.ds((x * 16 + y) * 8, 8), :]

    def x_line(y):
        low = March(lambda x: from_rows(xlo_ref, x + 3, y) if x < 0 else p_ref[x, y])
        high = March(lambda x: from_rows(xhi_ref, x - 32, y) if x >= 32 else p_ref[x, y])
        for k in range(3):
            side[k, y] = low.part(k, v_ref[0, k, y])
            side[k + 3, y] = high.part(29 + k, v_ref[0, 29 + k, y])

    loop(0, 16, x_line)

    def y_line(x, side_x, outs):
        low = March(lambda y: ylo_ref[x, y + 3] if y < 0 else p_ref[x, y])
        high = March(lambda y: yhi_ref[x, y - 16] if y >= 16 else p_ref[x, y])
        for y in range(16):
            rate = acc_ref[x, y]
            if side_x is not None:
                rate = rate + side[side_x, y]
            if y < 3:
                rate = rate + low.part(y, v_ref[1, x, y])
            if y >= 13:
                rate = rate + high.part(y, v_ref[1, x, y])
            start = None if number == 0 else start_ref[x, y]
            new = section(start, p_ref[x, y], rate, number)
            new_ref[x, y] = new
            if outs is not None:
                outs[0][pl.ds((outs[1] * 16 + y) * 8, 8), :] = new
            if y < edge:
                nylo_ref[x, y] = new
            if y >= 16 - edge:
                nyhi_ref[x, y - (16 - edge)] = new

    loop(0, 3, lambda x: y_line(x, x, (nxlo_ref, x)))
    loop(29, 32, lambda x: y_line(x, x - 26, (nxhi_ref, x - (32 - edge))))
    if edge > 3:
        loop(3, edge, lambda x: y_line(x, None, (nxlo_ref, x)))
        loop(32 - edge, 29, lambda x: y_line(x, None, (nxhi_ref, x - (32 - edge))))
    loop(edge, 32 - edge, lambda x: y_line(x, None, None))


def pushes(col):
    push = (PSEUDO_STEP * col) * lax.rsqrt(col * col + 1.0)
    return push, jnp.where(col > 0, 1.0, -1.0)


def turn(src, x, ys, turned):
    for y in ys:
        col = src[x, y]
        turned[0, y] = shifted(col, -1)
        turned[1, y] = shifted(col, 1)


def sweep_line(src, dst, push, sign, x, ys, turned):
    cols = {}

    def at(y):
        if y not in cols:
            cols[y] = src[x, y]
        return cols[y]

    for y in ys:
        col, c, s = at(y), push[x, y], sign[x, y]
        here = s * col
        total = None
        for pair in ((src[x - 1, y], src[x + 1, y]), (at(y - 1), at(y + 1)), (turned[0, y], turned[1, y])):
            floor = 1e-15 if total is None else 0.0
            rise = jnp.maximum(here - jnp.minimum(s * pair[0], s * pair[1]), floor)
            total = rise * rise if total is None else total + rise * rise
        dst[x, y] = (col + c) - (c * total) * lax.rsqrt(total)


def sweep_rows(src, dst, push, sign, place, pairs, ys, even, odd):
    turn(src, place(0), ys, even)

    def two(j):
        x = place(j)
        turn(src, x + 1, ys, odd)
        sweep_line(src, dst, push, sign, x, ys, even)
        turn(src, place(jnp.minimum(j + 1, pairs - 1)), ys, even)
        sweep_line(src, dst, push, sign, x + 1, ys, odd)

    loop(0, pairs, two)


def sweep_core(adv_ref, *refs):
    levels, (push, sign, even, odd) = refs[:SWEEPS], refs[SWEEPS:]

    def prepare(x):
        for y in range(16):
            push[x, y], sign[x, y] = pushes(adv_ref[x, y])

    loop(0, 32, prepare)
    src = adv_ref
    for k in range(1, SWEEPS + 1):
        dst = levels[k - 1]
        sweep_rows(src, dst, push, sign, lambda j, k=k: k + 2 * j, 16 - k, range(k, 16 - k), even, odd)
        src = dst


def pack_corners(xhi_ref, xlo_ref, _, low_ref, high_ref):
    k = 0
    for dx in range(1, WIDE):
        for ref, x in ((xlo_ref, WIDE - dx), (xhi_ref, dx - 1)):
            for dy in range(1, WIDE - dx + 1):
                low_ref[k] = ref[pl.ds((x * 16 + dy - 1) * 8, 8), :]
                high_ref[k] = ref[pl.ds((x * 16 + 16 - dy) * 8, 8), :]
                k += 1


CORNERS = WIDE * (WIDE - 1)


def normals(last, xs, nx, ny, nz, at):
    cols = {}

    def col(y):
        if y not in cols:
            cols[y] = last[xs, y + WIDE]
        return cols[y]

    across, along, deep = {}, {}, {}
    for y in range(-1, 17):
        gx = last[xs + 1, y + WIDE] - last[xs - 1, y + WIDE]
        gy = col(y + 1) - col(y - 1)
        gz = shifted(col(y), 1) - shifted(col(y), -1)
        scale = lax.rsqrt(gx * gx + gy * gy + gz * gz + 4.0)
        across[y], along[y], deep[y] = gx * scale, gy * scale, gz * scale
    for j in range(8):
        a, b = 2 * j, 2 * j + 1
        nx[at, j] = across[a] + across[b]
        ny[at, j] = (along[b] + along[b + 1]) - (along[a - 1] + along[a])
        nz[at, j] = deep[a] + deep[b]


def gather(last, xs, nx, ny, nz, at, lump, slot, half, new, new_at):
    a, b = at, at + 1
    for j in range(8):
        deep = nz[a, j] + nz[b, j]
        total = (nx[b, j] + nx[b + 1, j]) - (nx[a - 1, j] + nx[a, j]) + (ny[a, j] + ny[b, j])
        lump[pl.ds(slot * 64 + j * 8, 8), :] = total + (shifted(deep, 1) - shifted(deep, -1))
        share = None
        for x in range(2):
            for y in range(2):
                yy = 2 * j + y
                col = last[xs + x, yy + WIDE]
                new[pl.ds(new_at + x * 128 + (yy // 8) * 64 + yy % 8, 8, stride=8), :] = col
                bend = jnp.tanh(col * (1.0 / FRONT))
                share = bend if share is None else share + bend
        lump[pl.ds(half + slot * 64 + j * 8, 8), :] = share


def restrict(lump, slots, half, send, send_at):
    k = lax.broadcasted_iota(jnp.int32, (256, 128), 0)
    n = lax.broadcasted_iota(jnp.int32, (256, 128), 1)
    table = jnp.where(lax.div(k, 2) == n, 1.0 / 16.0, 0.0)
    halves = []
    for odd_row in range(2):
        rows = []
        for kind in range(2):
            for i in slots:
                base = kind * half + i * 64 + odd_row
                rows += [lump[pl.ds(base + 2 * z, 8, stride=8), :] for z in range(4)]
        halves.append(jnp.concatenate(rows, axis=0))
    out = jnp.dot(jnp.concatenate(halves, axis=1), table, precision=HIGH, preferred_element_type=jnp.float32)
    for n, i in enumerate(slots):
        send[send_at(i), pl.ds(0, 32), :] = out[n * 32 : n * 32 + 32]
        send[send_at(i), pl.ds(32, 32), :] = out[(len(slots) + n) * 32 : (len(slots) + n) * 32 + 32] + 0.5


def sweep_sides(
    adv_ref, yhi_ref, ylo_ref, one_ref, two_ref, three_ref, four_ref,
    rims_ref, last_ref, q0, q1, push, sign, even, odd,
):
    w = WIDE
    size_y = 16 + 2 * w

    def put(x, y, col):
        q0[x, y] = col
        push[x, y], sign[x, y] = pushes(col)

    def fill(x):
        for y in range(w):
            put(x, y, ylo_ref[x, y])
            put(x, y + 16 + w, yhi_ref[x, y])
        for y in (0, 1, 2, 3, 12, 13, 14, 15):
            put(x, y + w, adv_ref[x, y])

    loop(0, 32, fill)
    src, dst = q0, q1
    for k, core_ref in enumerate((one_ref, two_ref, three_ref, four_ref), 1):
        dst = last_ref if k == SWEEPS else dst
        sides = [*range(k, k + w), *range(size_y - k - w, size_y - k)]
        sweep_rows(src, dst, push, sign, lambda j, k=k: k + 2 * j, 16 - k, sides, even, odd)
        inside = (k, k + 1, 14 - k, 15 - k) if k < SWEEPS else range(k, 16 - k)

        def take(x, core_ref=core_ref, inside=inside, dst=dst):
            for y in inside:
                dst[x, y + w] = core_ref[x, y]

        loop(k, 32 - k, take)
        if k < SWEEPS:
            for r, x in enumerate((k, k + 1, 30 - k, 31 - k)):
                for y in range(k, size_y - k):
                    inner = k + 2 <= y - w < 14 - k
                    rims_ref[k - 1, r, y] = core_ref[x, y - w] if inner else dst[x, y]
        src, dst = dst, src


def inner_outputs(last, new_ref, send_ref, nx, ny, nz, lump):
    loop(0, 22, lambda r: normals(last, r + 5, nx, ny, nz, r))

    def planes(n):
        gather(last, 2 * n + 6, nx, ny, nz, 2 * n + 1, lump, n, 640, new_ref, (2 * n + 6) * 128)

    loop(0, 10, planes)
    for x in (4, 5, 26, 27):
        for y in range(16):
            new_ref[pl.ds(x * 128 + (y // 8) * 64 + y % 8, 8, stride=8), :] = last[x, y + WIDE]
    for part in range(2):
        restrict(lump, range(5 * part, 5 * part + 5), 640, send_ref, lambda i: i)


def finish(
    adv_ref, xhi_ref, xlo_ref, yhi_ref, ylo_ref, clo_ref, chi_ref, rims_ref, rows_ref, send_mid_ref, _,
    new_ref, send_ref, q0, q1, push, sign, nx, ny, nz, lump, even, odd, ends, sems,
):
    w = WIDE
    size_y = 16 + 2 * w

    def put(x, y, col):
        q0[x, y] = col
        push[x, y], sign[x, y] = pushes(col)

    def fill_mid(r):
        x = r + jnp.where(r >= 4, 24, 0)
        at = r + w + jnp.where(r >= 4, 8, 0)
        for y in range(w):
            put(at, y, ylo_ref[x, y])
            put(at, y + 16 + w, yhi_ref[x, y])
        for y in range(16):
            put(at, y + w, adv_ref[x, y])

    def fill_side(x):
        for y in range(16):
            put(x, y + w, xlo_ref[pl.ds((x * 16 + y) * 8, 8), :])
            put(x + 16 + w, y + w, xhi_ref[pl.ds((x * 16 + y) * 8, 8), :])

    loop(0, 8, fill_mid)
    loop(0, w, fill_side)
    k = 0
    for dx in range(1, w):
        for x in (w - dx, w + 15 + dx):
            for dy in range(1, w - dx + 1):
                put(x, w - dy, clo_ref[k])
                put(x, w + 15 + dy, chi_ref[k])
                k += 1

    src, dst = q0, q1
    for k in range(1, SWEEPS + 1):

        def end_rows(j, k=k):
            return k + 2 * j + jnp.where(j >= 3, 16 - 2 * k, 0)

        sweep_rows(src, dst, push, sign, end_rows, 6, range(k, size_y - k), even, odd)
        if k < SWEEPS:
            for r, x in enumerate((k, k + 1, 14 - k, 15 - k)):
                for y in range(k, size_y - k):
                    dst[x + w, y] = rims_ref[k - 1, r, y]
        src, dst = dst, src
    last = src

    def take(r):
        x = SWEEPS + r + jnp.where(r >= 4, 16, 0)
        for y in range(SWEEPS, size_y - SWEEPS):
            last[SWEEPS + r + w, y] = rows_ref[x, y]

    loop(0, 8, take)
    loop(0, 16, lambda r: normals(last, r + w - 1 + jnp.where(r >= 8, 2, 0), nx, ny, nz, r))

    def planes(n):
        far = jnp.where(n >= 3, 1, 0)
        gather(last, 2 * n + w + 4 * far, nx, ny, nz, 2 * n + 1 + 2 * far, lump, n, 384, ends, n * 256)

    loop(0, 6, planes)
    copies = [
        pltpu.make_async_copy(ends.at[pl.ds(1024 * k, 512)], new_ref.at[pl.ds(3584 * k, 512)], sems.at[k])
        for k in range(2)
    ]
    for copy in copies:
        copy.start()
    restrict(lump, range(6), 384, send_ref, lambda i: i + (10 if i >= 3 else 0))
    send_ref[pl.ds(3, 10)] = send_mid_ref[...]
    for copy in copies:
        copy.wait()


def call(kernel, outs, *args, scratch=(), mib=48, ops=1000, name=None, anywhere=(), aliases=None):
    def spec(k):
        return pl.BlockSpec(memory_space=pl.ANY if k in anywhere else pltpu.VMEM)

    aliases = aliases or {}
    flat = outs if isinstance(outs, tuple) else (outs,)
    specs = tuple(pl.BlockSpec(memory_space=pl.ANY if k in aliases.values() else pltpu.VMEM) for k in range(len(flat)))
    return pl.pallas_call(
        kernel,
        out_shape=outs,
        in_specs=[spec(k) for k in range(len(args))],
        out_specs=specs if isinstance(outs, tuple) else specs[0],
        scratch_shapes=[pltpu.VMEM(s, jnp.float32) if isinstance(s, tuple) else s for s in scratch],
        input_output_aliases=aliases,
        compiler_params=params(mib),
        cost_estimate=cost(ops),
        name=name,
    )(*args)


def moved(values, axis, step):
    count = lax.axis_size(axis)
    return lax.ppermute(values, axis, [(i, (i + step) % count) for i in range(count)])


def star(xlo, xhi, ylo, yhi):
    return (moved(xhi, "gx", 1), moved(xlo, "gx", -1), moved(yhi, "gy", 1), moved(ylo, "gy", -1))


def per_device(level_set, flow_velocity, band_mask):
    col = (ROWS, LANES)
    block = f32(32, 16, *col)
    level_rows = level_set.reshape(32, 2, 8, 8, 128).transpose(0, 1, 3, 2, 4).reshape(4096, 128)
    flow_rows = flow_velocity.reshape(3, 16, 8, 4, 128).transpose(0, 1, 3, 2, 4).reshape(1536, 128)

    send = call(pack_velocity, f32(16, 120, 128), flow_rows, name="pack", mib=4)
    coarse = lax.all_to_all(send, "gy", split_axis=0, concat_axis=0, tiled=True)
    start, ylo, yhi = call(
        unpack_level, (block, f32(32, 3, *col), f32(32, 3, *col)), level_rows, name="unpack", mib=4
    )
    both, tips = call(
        depth_sides, (f32(2, 32, 16, *col), f32(2, 2, 16, *col)), start,
        scratch=[block.shape, block.shape, (4, 16, *col), (4, 16, *col)], name="depth", mib=8, ops=512 * 90,
    )
    coarse = coarse.reshape(1920, 128)
    xlo, xhi = call(join_x, (f32(504, 128), f32(504, 128)), start, coarse, tips, name="join", mib=4)
    halo = star(xlo, xhi, ylo, yhi)
    velocity, ends, acc = call(
        refine_and_rate, (f32(3, 32, 16, *col), f32(2, 240, 128), block), coarse, band_mask, start, both,
        scratch=[(3840, 128), (2, *col)], name="refine", mib=10, ops=512 * 110,
    )
    current = start
    for number in range(3):
        if number == 0:
            velocity, acc = call(
                refine_ends, (f32(3, 32, 16, *col), block),
                halo[0], halo[1], ends, band_mask, current, tips, velocity, acc,
                scratch=[(480, 128), (3, 2, 16, *col), (2, 16, *col), pltpu.SemaphoreType.DMA((8,))],
                name="ends", mib=4, anywhere=(6, 7), aliases={6: 0, 7: 1},
            )
        else:
            acc = call(
                inner_rate, block, current, velocity,
                scratch=[block.shape, block.shape, (4, 16, *col), (4, 16, *col)],
                name="inner", mib=8, ops=512 * 140,
            )
        edge = WIDE if number == 2 else 3
        x_edge, y_edge = f32(edge * 128, 128), f32(32, edge, *col)
        current, *edges = call(
            functools.partial(edge_rate, number, edge), (block, x_edge, x_edge, y_edge, y_edge),
            acc, start, current, velocity, *sum(turned_about(number, halo[:2], halo[2:]), ()),
            scratch=[(6, 16, *col)], name="edge", mib=4, ops=512 * 30,
        )
        halo = star(*edges)
    xlo, xhi, ylo, yhi = halo
    levels = call(
        sweep_core, (block,) * SWEEPS, current,
        scratch=[block.shape, block.shape, (2, 16, *col), (2, 16, *col)], name="core", mib=8, ops=512 * 90,
    )
    corner = f32(CORNERS, *col)
    turns = [(2, 16 + 2 * WIDE, *col)] * 2
    side = (32, 16 + 2 * WIDE, *col)
    rims, last = call(
        sweep_sides, (f32(3, 4, *side[1:]), f32(*side)), current, yhi, ylo, *levels,
        scratch=[side] * 4 + turns, name="sides", mib=17, ops=512 * 70,
    )
    corner_low, corner_high = call(
        pack_corners, (corner, corner), xhi, xlo, rims, name="corners", mib=4, anywhere=(2,)
    )
    new_rows, send_mid = call(
        inner_outputs, (f32(4096, 128), f32(10, 64, 128)), last,
        scratch=[(22, 8, *col)] * 3 + [(1280, 128)], name="outputs", mib=12, ops=512 * 40,
    )
    clo, chi = moved(corner_high, "gy", 1), moved(corner_low, "gy", -1)
    ext = (16 + 2 * WIDE, 16 + 2 * WIDE, *col)
    new_rows, packed = call(
        finish, (f32(4096, 128), f32(16, 64, 128)),
        current, xhi, xlo, yhi, ylo, clo, chi, rims, last, send_mid, new_rows,
        scratch=[ext] * 4 + [(16, 8, *col)] * 3 + [(768, 128)] + turns + [(1536, 128), pltpu.SemaphoreType.DMA((2,))],
        name="finish", mib=18, ops=512 * 250, anywhere=(10,), aliases={10: 0},
    )
    returned = lax.all_to_all(packed, "gy", split_axis=0, concat_axis=0, tiled=True).reshape(16, 2, 4, 8, 128)
    new_level = new_rows.reshape(32, 2, 8, 8, 128).transpose(0, 1, 3, 2, 4).reshape(32, 16, 1024)
    flows = [returned[:, k].transpose(0, 2, 1, 3).reshape(1, 128, 512) for k in range(2)]
    return (new_level, flows[0], flows[1])


def solution(mesh):
    placed = (P("gx", "gy", None), P(None, ("gx", "gy"), None, None), P("gx", "gy", None))
    return jax.shard_map(
        per_device,
        mesh=mesh,
        in_specs=placed,
        out_specs=(P("gx", "gy", None), P(("gx", "gy"), None, None), P(("gx", "gy"), None, None)),
        check_vma=False,
    )
```

```python
import functools

import jax
import jax.numpy as jnp
from jax import lax
from jax.experimental import pallas as pl
from jax.experimental.pallas import tpu as pltpu
from jax.sharding import PartitionSpec as P

SWEEPS = 4
TIME_STEP = 0.25
PSEUDO_STEP = 0.3
EPS = 1e-06
FRONT = 1.5
WIDE = SWEEPS + 2

ROWS, LANES = 8, 128
HIGH = lax.Precision.HIGHEST


def params(mib):
    return pltpu.CompilerParams(vmem_limit_bytes=mib * 2**20)


def f32(*shape):
    return jax.ShapeDtypeStruct(shape, jnp.float32)


def cost(vector_ops):
    return pl.CostEstimate(flops=vector_ops * 1024, bytes_accessed=2**23, transcendentals=0)


def shifted(col, step):
    lane = lax.broadcasted_iota(jnp.int32, (ROWS, LANES), 1)
    turned = pltpu.roll(col, (-step) % LANES, 1)
    if step > 0:
        return jnp.where(lane >= LANES - step, pltpu.roll(turned, ROWS - 1, 0), turned)
    return jnp.where(lane < -step, pltpu.roll(turned, 1, 0), turned)


def inverse(values):
    return pl.reciprocal(values, approx=True)


def correction(rough1, rough2, rough3, third1, third2):
    r1, r2, r3 = inverse(rough1), inverse(rough2), inverse(rough3)
    w1 = r1 * r1
    w12 = w1 + 6.0 * (r2 * r2)
    w3 = 3.0 * (r3 * r3)
    return (4.0 * w1 * third1 + (w3 - w12) * third2) * inverse(w12 + w3)


def upwind_part(speed, central, corr):
    return speed * central + jnp.abs(speed) * corr


class March:
    def __init__(self, get):
        self.get = get
        self.made = {}

    def once(self, name, j, make):
        key = (name, j)
        if key not in self.made:
            self.made[key] = make()
        return self.made[key]

    def p(self, j):
        return self.once("p", j, lambda: self.get(j))

    def d(self, j):
        return self.once("d", j, lambda: self.p(j + 1) - self.p(j))

    def curve(self, j):
        return self.once("c", j, lambda: self.d(j) - self.d(j - 1))

    def gap(self, j):
        return self.once("g", j, lambda: self.curve(j + 1) - self.curve(j))

    def third(self, j):
        return self.once("t", j, lambda: self.gap(j) - self.gap(j - 1))

    def base(self, j):
        return self.once("h", j, lambda: (4.0 / 3.0) * (self.gap(j) * self.gap(j)) + EPS)

    def cross(self, j):
        return self.once("x", j, lambda: self.curve(j) * self.curve(j + 1))

    def twice(self, j):
        return self.once("a", j, lambda: (self.curve(j) + self.curve(j)) * self.curve(j))

    def less(self, j):
        return self.once("l", j, lambda: self.base(j) - self.cross(j))

    def mid(self, j):
        return self.once("m", j, lambda: self.base(j) + self.cross(j))

    def up(self, j):
        return self.once("u", j, lambda: self.less(j) + self.twice(j + 1))

    def down(self, j):
        return self.once("v", j, lambda: self.less(j) + self.twice(j))

    def central(self, i):
        return 6.0 * (self.p(i + 1) - self.p(i - 1)) - (self.gap(i) + self.gap(i - 1))

    def part(self, i, speed):
        minus = speed < 0
        corr = correction(
            jnp.where(minus, self.up(i - 2), self.down(i + 1)),
            jnp.where(minus, self.mid(i - 1), self.mid(i)),
            jnp.where(minus, self.down(i), self.up(i - 1)),
            jnp.where(minus, self.third(i - 1), self.third(i + 1)),
            self.third(i),
        )
        return upwind_part(speed, self.central(i), corr)


def depth_rate(slope, here, turned, speed):
    m2, m1, p1, p2 = turned
    minus = speed < 0
    a = jnp.where(minus, m2, p2)
    b = jnp.where(minus, m1, p1)
    d = jnp.where(minus, p1, m1)
    g1, g2, g3 = b - a, here - b, d - here
    corr = correction(
        (4.0 / 3.0) * (g1 * g1) + EPS + b * (b + g1),
        (4.0 / 3.0) * (g2 * g2) + EPS + b * here,
        (4.0 / 3.0) * (g3 * g3) + EPS + here * (here - g3),
        g2 - g1,
        g3 - g2,
    )
    return upwind_part(speed, slope - (p1 - m1), corr)


def loop_pairs(low, high, body):
    def step(i, carry):
        body(low + 2 * i)
        body(low + 2 * i + 1)
        return carry

    lax.fori_loop(0, (high - low) // 2, step, 0)


def loop(low, high, body):
    def step(i, carry):
        body(i)
        return carry

    lax.fori_loop(low, high, step, 0)


def pack_velocity(rows_ref, out_ref):
    def to(g):
        for c in range(3):
            for r in range(10):
                block, low = (g, r - 1) if 1 <= r <= 8 else ((g + 15, 7) if r == 0 else (g + 1, 0))
                start = c * 512 + lax.rem(block, 16) * 32 + low
                out_ref[g, pl.ds((c * 10 + r) * 4, 4), :] = rows_ref[pl.ds(start, 4, stride=8), :]

    loop(0, 16, to)


def unpack_level(rows_ref, p_ref, ylo_ref, yhi_ref):
    def to(x):
        for y in range(16):
            col = rows_ref[pl.ds(x * 128 + (y // 8) * 64 + y % 8, 8, stride=8), :]
            p_ref[x, y] = col
            if y < 3:
                ylo_ref[x, y] = col
            if y >= 13:
                yhi_ref[x, y - 13] = col

    loop(0, 32, to)


def refine_table():
    k = lax.broadcasted_iota(jnp.int32, (256, 256), 0)
    n = lax.broadcasted_iota(jnp.int32, (256, 256), 1)
    beside = jnp.where(n % 2 == 0, n // 2 - 1, n // 2 + 1)
    beside = jnp.where(beside < 0, 255, jnp.where(beside > 127, 128, beside))
    return jnp.where(k == n // 2, 0.75, 0.0) + jnp.where(k == beside, 0.25, 0.0)


def refine_z(plane, table):
    count = plane.shape[0]
    row = lax.broadcasted_iota(jnp.int32, plane.shape, 0) % 4
    lane = lax.broadcasted_iota(jnp.int32, plane.shape, 1)
    after = jnp.where(row == 3, pltpu.roll(plane, 3, 0), pltpu.roll(plane, count - 1, 0))
    prior = jnp.where(row == 0, pltpu.roll(plane, count - 3, 0), pltpu.roll(plane, 1, 0))
    wide = jnp.concatenate([plane, jnp.where(lane < 64, after, prior)], axis=1)
    out = jnp.dot(wide, table, precision=HIGH, preferred_element_type=jnp.float32)
    return out[:, :128], out[:, 128:]


def band_blocks(band_ref):
    k = lax.broadcasted_iota(jnp.int32, (64, 128), 0)
    n = lax.broadcasted_iota(jnp.int32, (64, 128), 1)
    spread = jnp.where(lax.rem(k, 8) == lax.div(n, 16), -TIME_STEP / 12.0, 0.0)
    row = lax.broadcasted_iota(jnp.int32, (8, 64), 0)
    tile = lax.div(lax.broadcasted_iota(jnp.int32, (8, 64), 1), 8)
    blocks = []
    for half in range(2):
        mask = jnp.broadcast_to(band_ref[half].astype(jnp.float32), (8, 64))
        mask = jnp.where(row == tile, mask, 0.0)
        blocks.append(jnp.dot(mask, spread, precision=HIGH, preferred_element_type=jnp.float32))
    return blocks


def refine_inner(mid_ref, band_ref, v_ref, ends_ref, fine, band):
    table = refine_table()
    for half, block in enumerate(band_blocks(band_ref)):
        band[half] = block

    def along_z(k):
        left, right = refine_z(mid_ref[pl.ds(k * 480, 480), :], table)
        fine[pl.ds(k * 960, 480, stride=2), :] = left
        fine[pl.ds(k * 960 + 1, 480, stride=2), :] = right

    loop(0, 4, along_z)
    for end, plane in enumerate((0, 15)):
        ends_ref[end] = fine[pl.ds(plane * 240, 240), :]

    def along_xy(i):
        for c in range(3):
            near, far = [], []
            for r in range(10):
                at = (c * 10 + r) * 8
                near.append(fine[pl.ds(i * 240 + at, 8), :])
                far.append(fine[pl.ds(i * 240 + 240 + at, 8), :])
            for k in range(2):
                x = 2 * i + 1 + k
                line = [0.75 * a + 0.25 * b for a, b in (zip(far, near) if k else zip(near, far))]
                along_y(c, x, line, band[lax.div(x, 16)], v_ref)

    loop(0, 15, along_xy)


def along_y(c, x, line, band, v_ref):
    scaled = [band * value for value in line]
    for y in range(16):
        m = y // 2 + 1
        v_ref[c, x, y] = 0.75 * scaled[m] + 0.25 * scaled[m - 1 + 2 * (y % 2)]


def refine_ends(lo_ref, hi_ref, ends_ref, band_ref, p_ref, tips_ref, v_in, acc_in, v_out, acc_out, fine, ends, part, sems):
    table = refine_table()
    blocks = band_blocks(band_ref)
    for side, ref in enumerate((lo_ref, hi_ref)):
        left, right = refine_z(ref[pl.ds(384, 120), :], table)
        fine[pl.ds(side * 240, 120, stride=2), :] = left
        fine[pl.ds(side * 240 + 1, 120, stride=2), :] = right
    for side in range(2):
        for c in range(3):
            line = []
            for r in range(10):
                at = (c * 10 + r) * 8
                line.append(0.75 * ends_ref[side, pl.ds(at, 8), :] + 0.25 * fine[pl.ds(side * 240 + at, 8), :])
            along_y(c, side, line, blocks[side], ends)
    for side in range(2):
        x = 31 * side
        march = March(lambda y: p_ref[x, y])
        for y in range(16):
            speed = ends[2, side, y]
            total = speed * jnp.where(speed < 0, tips_ref[side, 0, y], tips_ref[side, 1, y])
            if 3 <= y < 13:
                total = total + march.part(y, ends[1, side, y])
            part[side, y] = total
    copies = []
    for side in range(2):
        copies.append((part.at[side], acc_out.at[31 * side]))
        for c in range(3):
            copies.append((ends.at[c, side], v_out.at[c, 31 * side]))
    copies = [pltpu.make_async_copy(src, dst, sems.at[k]) for k, (src, dst) in enumerate(copies)]
    for copy in copies:
        copy.start()
    for copy in copies:
        copy.wait()


def inner_rate(p_ref, v_ref, acc_ref, curve, slope, even, odd):
    def x_line(y):
        march = March(lambda x: p_ref[x, y])
        for x in range(32):
            col = march.p(x)
            before, after = shifted(col, -1), shifted(col, 1)
            curve[x, y] = (after - col) - (col - before)
            slope[x, y] = 6.0 * (after - before)
            if 3 <= x < 29:
                acc_ref[x, y] = march.part(x, v_ref[0, x, y])
            else:
                acc_ref[x, y] = jnp.zeros((ROWS, LANES), jnp.float32)

    loop(0, 16, x_line)

    def turn(x, turned):
        for y in range(16):
            col = curve[x, y]
            for k, step in enumerate((-2, -1, 1, 2)):
                turned[k, y] = shifted(col, step)

    def y_line(x, turned):
        march = March(lambda y: p_ref[x, y])
        for y in range(16):
            total = acc_ref[x, y] + depth_rate(slope[x, y], curve[x, y], [turned[k, y] for k in range(4)], v_ref[2, x, y])
            if 3 <= y < 13:
                total = total + march.part(y, v_ref[1, x, y])
            acc_ref[x, y] = total

    turn(0, even)

    def two(k):
        x = 2 * k
        turn(x + 1, odd)
        y_line(x, even)
        turn(jnp.minimum(x + 2, 31), even)
        y_line(x + 1, odd)

    loop(0, 16, two)


def depth_both(slope, here, turned):
    m2, m1, p1, p2 = turned
    gm2, gm1, g0, g1 = m1 - m2, here - m1, p1 - here, p2 - p1
    bm2, bm1, b0, b1 = [(4.0 / 3.0) * (g * g) + EPS for g in (gm2, gm1, g0, g1)]
    third = g0 - gm1
    below = correction(bm2 + m1 * (m1 + gm2), bm1 + m1 * here, b0 + here * (here - g0), gm1 - gm2, third)
    above = correction(b1 + p1 * (p1 - g1), b0 + p1 * here, bm1 + here * (here + gm1), g1 - g0, third)
    central = slope - (p1 - m1)
    return central - below, central + above


def depth_sides(p_ref, both_ref, tips_ref, curve, slope, even, odd):
    def curves(x):
        for y in range(16):
            col = p_ref[x, y]
            before, after = shifted(col, -1), shifted(col, 1)
            curve[x, y] = (after - col) - (col - before)
            slope[x, y] = 6.0 * (after - before)

    def turned_row(x, turned):
        for y in range(16):
            col = curve[x, y]
            for k, step in enumerate((-2, -1, 1, 2)):
                turned[k, y] = shifted(col, step)

    def rates(x, turned):
        for y in range(16):
            both = depth_both(slope[x, y], curve[x, y], [turned[k, y] for k in range(4)])
            both_ref[0, x, y], both_ref[1, x, y] = both

    for x in range(3):
        curves(x)
    turned_row(0, even)

    def two(k):
        x = 2 * k
        turned_row(x + 1, odd)
        rates(x, even)
        turned_row(jnp.minimum(x + 2, 31), even)
        rates(x + 1, odd)
        curves(jnp.minimum(x + 3, 31))
        curves(jnp.minimum(x + 4, 31))

    loop(0, 16, two)
    for side in range(2):
        for k in range(2):
            for y in range(16):
                tips_ref[side, k, y] = both_ref[k, 31 * side, y]


def inner_rate_first(p_ref, v_ref, both_ref, acc_ref):
    def x_line(y):
        march = March(lambda x: p_ref[x, y])
        for x in range(32):
            if 3 <= x < 29:
                acc_ref[x, y] = march.part(x, v_ref[0, x, y])
            else:
                acc_ref[x, y] = jnp.zeros((ROWS, LANES), jnp.float32)

    def y_line(x):
        march = March(lambda y: p_ref[x, y])
        for y in range(16):
            speed = v_ref[2, x, y]
            total = acc_ref[x, y] + speed * jnp.where(speed < 0, both_ref[0, x, y], both_ref[1, x, y])
            if 3 <= y < 13:
                total = total + march.part(y, v_ref[1, x, y])
            acc_ref[x, y] = total

    loop(0, 16, x_line)
    loop_pairs(1, 31, y_line)


def refine_and_rate(mid_ref, band_ref, p_ref, both_ref, v_ref, ends_ref, acc_ref, fine, band):
    refine_inner(mid_ref, band_ref, v_ref, ends_ref, fine, band)
    inner_rate_first(p_ref, v_ref, both_ref, acc_ref)


def join_x(p_ref, coarse_ref, mark_ref, low_ref, high_ref):
    for x in range(3):
        for y in range(16):
            at = pl.ds((x * 16 + y) * 8, 8)
            low_ref[at, :] = p_ref[x, y]
            high_ref[at, :] = p_ref[29 + x, y]
    for k in range(15):
        low_ref[pl.ds(384 + 8 * k, 8), :] = coarse_ref[pl.ds(8 * k, 8), :]
        high_ref[pl.ds(384 + 8 * k, 8), :] = coarse_ref[pl.ds(1800 + 8 * k, 8), :]


def section(start, current, rate, number):
    if number == 0:
        return current + rate
    if number == 1:
        return 0.75 * start + 0.25 * (current + rate)
    return start * (1.0 / 3.0) + (2.0 / 3.0) * (current + rate)


def turned_about(number, *pairs):
    return [pair[::-1] if number % 2 else pair for pair in pairs]


def edge_rate(
    number, edge, acc_ref, start_ref, p_ref, v_ref, x1_ref, x2_ref, y1_ref, y2_ref,
    new_ref, nxlo_ref, nxhi_ref, nylo_ref, nyhi_ref, side,
):
    (xlo_ref, xhi_ref), (ylo_ref, yhi_ref) = turned_about(number, (x1_ref, x2_ref), (y1_ref, y2_ref))

    def from_rows(ref, x, y):
        return ref[pl.ds((x * 16 + y) * 8, 8), :]

    def x_line(y):
        low = March(lambda x: from_rows(xlo_ref, x + 3, y) if x < 0 else p_ref[x, y])
        high = March(lambda x: from_rows(xhi_ref, x - 32, y) if x >= 32 else p_ref[x, y])
        for k in range(3):
            side[k, y] = low.part(k, v_ref[0, k, y])
            side[k + 3, y] = high.part(29 + k, v_ref[0, 29 + k, y])

    loop_pairs(0, 16, x_line)

    def y_line(x, side_x, outs):
        low = March(lambda y: ylo_ref[x, y + 3] if y < 0 else p_ref[x, y])
        high = March(lambda y: yhi_ref[x, y - 16] if y >= 16 else p_ref[x, y])
        for y in range(16):
            rate = acc_ref[x, y]
            if side_x is not None:
                rate = rate + side[side_x, y]
            if y < 3:
                rate = rate + low.part(y, v_ref[1, x, y])
            if y >= 13:
                rate = rate + high.part(y, v_ref[1, x, y])
            start = None if number == 0 else start_ref[x, y]
            new = section(start, p_ref[x, y], rate, number)
            new_ref[x, y] = new
            if outs is not None:
                outs[0][pl.ds((outs[1] * 16 + y) * 8, 8), :] = new
            if y < edge:
                nylo_ref[x, y] = new
            if y >= 16 - edge:
                nyhi_ref[x, y - (16 - edge)] = new

    loop(0, 3, lambda x: y_line(x, x, (nxlo_ref, x)))
    loop(29, 32, lambda x: y_line(x, x - 26, (nxhi_ref, x - (32 - edge))))
    if edge > 3:
        loop(3, edge, lambda x: y_line(x, None, (nxlo_ref, x)))
        loop(32 - edge, 29, lambda x: y_line(x, None, (nxhi_ref, x - (32 - edge))))
    loop_pairs(edge, 32 - edge, lambda x: y_line(x, None, None))


def pushes(col):
    push = (PSEUDO_STEP * col) * lax.rsqrt(col * col + 1.0)
    return push, jnp.where(col > 0, 1.0, -1.0)


def turn(src, x, ys, turned):
    for y in ys:
        col = src[x, y]
        turned[0, y] = shifted(col, -1)
        turned[1, y] = shifted(col, 1)


def sweep_line(src, dst, push, sign, x, ys, turned):
    cols = {}

    def at(y):
        if y not in cols:
            cols[y] = src[x, y]
        return cols[y]

    for y in ys:
        col, c, s = at(y), push[x, y], sign[x, y]
        here = s * col
        total = None
        for pair in ((src[x - 1, y], src[x + 1, y]), (at(y - 1), at(y + 1)), (turned[0, y], turned[1, y])):
            floor = 1e-15 if total is None else 0.0
            rise = jnp.maximum(here - jnp.minimum(s * pair[0], s * pair[1]), floor)
            total = rise * rise if total is None else total + rise * rise
        dst[x, y] = (col + c) - (c * total) * lax.rsqrt(total)


def sweep_rows(src, dst, push, sign, place, pairs, ys, even, odd):
    turn(src, place(0), ys, even)

    def two(j):
        x = place(j)
        turn(src, x + 1, ys, odd)
        sweep_line(src, dst, push, sign, x, ys, even)
        turn(src, place(jnp.minimum(j + 1, pairs - 1)), ys, even)
        sweep_line(src, dst, push, sign, x + 1, ys, odd)

    loop(0, pairs, two)


def sweep_core(adv_ref, *refs):
    levels, (push, sign, even, odd) = refs[:SWEEPS], refs[SWEEPS:]

    def prepare(x):
        for y in range(16):
            push[x, y], sign[x, y] = pushes(adv_ref[x, y])

    loop_pairs(0, 32, prepare)
    src = adv_ref
    for k in range(1, SWEEPS + 1):
        dst = levels[k - 1]
        sweep_rows(src, dst, push, sign, lambda j, k=k: k + 2 * j, 16 - k, range(k, 16 - k), even, odd)
        src = dst


def pack_corners(xhi_ref, xlo_ref, _, low_ref, high_ref):
    k = 0
    for dx in range(1, WIDE):
        for ref, x in ((xlo_ref, WIDE - dx), (xhi_ref, dx - 1)):
            for dy in range(1, WIDE - dx + 1):
                low_ref[k] = ref[pl.ds((x * 16 + dy - 1) * 8, 8), :]
                high_ref[k] = ref[pl.ds((x * 16 + 16 - dy) * 8, 8), :]
                k += 1


CORNERS = WIDE * (WIDE - 1)


def normals(last, xs, nx, ny, nz, at):
    cols = {}

    def col(y):
        if y not in cols:
            cols[y] = last[xs, y + WIDE]
        return cols[y]

    across, along, deep = {}, {}, {}
    for y in range(-1, 17):
        gx = last[xs + 1, y + WIDE] - last[xs - 1, y + WIDE]
        gy = col(y + 1) - col(y - 1)
        gz = shifted(col(y), 1) - shifted(col(y), -1)
        scale = lax.rsqrt(gx * gx + gy * gy + gz * gz + 4.0)
        across[y], along[y], deep[y] = gx * scale, gy * scale, gz * scale
    for j in range(8):
        a, b = 2 * j, 2 * j + 1
        nx[at, j] = across[a] + across[b]
        ny[at, j] = (along[b] + along[b + 1]) - (along[a - 1] + along[a])
        nz[at, j] = deep[a] + deep[b]


def gather(last, xs, nx, ny, nz, at, lump, slot, half, new, new_at):
    a, b = at, at + 1
    for j in range(8):
        deep = nz[a, j] + nz[b, j]
        total = (nx[b, j] + nx[b + 1, j]) - (nx[a - 1, j] + nx[a, j]) + (ny[a, j] + ny[b, j])
        lump[pl.ds(slot * 64 + j * 8, 8), :] = total + (shifted(deep, 1) - shifted(deep, -1))
        share = None
        for x in range(2):
            for y in range(2):
                yy = 2 * j + y
                col = last[xs + x, yy + WIDE]
                new[pl.ds(new_at + x * 128 + (yy // 8) * 64 + yy % 8, 8, stride=8), :] = col
                bend = jnp.tanh(col * (1.0 / FRONT))
                share = bend if share is None else share + bend
        lump[pl.ds(half + slot * 64 + j * 8, 8), :] = share


def restrict(lump, slots, half, send, send_at):
    k = lax.broadcasted_iota(jnp.int32, (256, 128), 0)
    n = lax.broadcasted_iota(jnp.int32, (256, 128), 1)
    table = jnp.where(lax.div(k, 2) == n, 1.0 / 16.0, 0.0)
    halves = []
    for odd_row in range(2):
        rows = []
        for kind in range(2):
            for i in slots:
                base = kind * half + i * 64 + odd_row
                rows += [lump[pl.ds(base + 2 * z, 8, stride=8), :] for z in range(4)]
        halves.append(jnp.concatenate(rows, axis=0))
    out = jnp.dot(jnp.concatenate(halves, axis=1), table, precision=HIGH, preferred_element_type=jnp.float32)
    for n, i in enumerate(slots):
        send[send_at(i), pl.ds(0, 32), :] = out[n * 32 : n * 32 + 32]
        send[send_at(i), pl.ds(32, 32), :] = out[(len(slots) + n) * 32 : (len(slots) + n) * 32 + 32] + 0.5


def sweep_sides(
    adv_ref, yhi_ref, ylo_ref, one_ref, two_ref, three_ref, four_ref,
    rims_ref, last_ref, q0, q1, push, sign, even, odd,
):
    w = WIDE
    size_y = 16 + 2 * w

    def put(x, y, col):
        q0[x, y] = col
        push[x, y], sign[x, y] = pushes(col)

    def fill(x):
        for y in range(w):
            put(x, y, ylo_ref[x, y])
            put(x, y + 16 + w, yhi_ref[x, y])
        for y in (0, 1, 2, 3, 12, 13, 14, 15):
            put(x, y + w, adv_ref[x, y])

    loop_pairs(0, 32, fill)
    src, dst = q0, q1
    for k, core_ref in enumerate((one_ref, two_ref, three_ref, four_ref), 1):
        dst = last_ref if k == SWEEPS else dst
        sides = [*range(k, k + w), *range(size_y - k - w, size_y - k)]
        sweep_rows(src, dst, push, sign, lambda j, k=k: k + 2 * j, 16 - k, sides, even, odd)
        inside = (k, k + 1, 14 - k, 15 - k) if k < SWEEPS else range(k, 16 - k)

        def take(x, core_ref=core_ref, inside=inside, dst=dst):
            for y in inside:
                dst[x, y + w] = core_ref[x, y]

        loop_pairs(k, 32 - k, take)
        if k < SWEEPS:
            for r, x in enumerate((k, k + 1, 30 - k, 31 - k)):
                for y in range(k, size_y - k):
                    inner = k + 2 <= y - w < 14 - k
                    rims_ref[k - 1, r, y] = core_ref[x, y - w] if inner else dst[x, y]
        src, dst = dst, src


def inner_outputs(last, new_ref, send_ref, nx, ny, nz, lump):
    loop_pairs(0, 22, lambda r: normals(last, r + 5, nx, ny, nz, r))

    def planes(n):
        gather(last, 2 * n + 6, nx, ny, nz, 2 * n + 1, lump, n, 640, new_ref, (2 * n + 6) * 128)

    loop_pairs(0, 10, planes)
    for x in (4, 5, 26, 27):
        for y in range(16):
            new_ref[pl.ds(x * 128 + (y // 8) * 64 + y % 8, 8, stride=8), :] = last[x, y + WIDE]
    for part in range(2):
        restrict(lump, range(5 * part, 5 * part + 5), 640, send_ref, lambda i: i)


def finish(
    adv_ref, xhi_ref, xlo_ref, yhi_ref, ylo_ref, clo_ref, chi_ref, rims_ref, rows_ref, send_mid_ref, _,
    new_ref, send_ref, q0, q1, push, sign, nx, ny, nz, lump, even, odd, ends, sems,
):
    w = WIDE
    size_y = 16 + 2 * w

    def put(x, y, col):
        q0[x, y] = col
        push[x, y], sign[x, y] = pushes(col)

    def fill_mid(r):
        x = r + jnp.where(r >= 4, 24, 0)
        at = r + w + jnp.where(r >= 4, 8, 0)
        for y in range(w):
            put(at, y, ylo_ref[x, y])
            put(at, y + 16 + w, yhi_ref[x, y])
        for y in range(16):
            put(at, y + w, adv_ref[x, y])

    def fill_side(x):
        for y in range(16):
            put(x, y + w, xlo_ref[pl.ds((x * 16 + y) * 8, 8), :])
            put(x + 16 + w, y + w, xhi_ref[pl.ds((x * 16 + y) * 8, 8), :])

    loop_pairs(0, 8, fill_mid)
    loop_pairs(0, w, fill_side)
    k = 0
    for dx in range(1, w):
        for x in (w - dx, w + 15 + dx):
            for dy in range(1, w - dx + 1):
                put(x, w - dy, clo_ref[k])
                put(x, w + 15 + dy, chi_ref[k])
                k += 1

    src, dst = q0, q1
    for k in range(1, SWEEPS + 1):

        def end_rows(j, k=k):
            return k + 2 * j + jnp.where(j >= 3, 16 - 2 * k, 0)

        sweep_rows(src, dst, push, sign, end_rows, 6, range(k, size_y - k), even, odd)
        if k < SWEEPS:
            for r, x in enumerate((k, k + 1, 14 - k, 15 - k)):
                for y in range(k, size_y - k):
                    dst[x + w, y] = rims_ref[k - 1, r, y]
        src, dst = dst, src
    last = src

    def take(r):
        x = SWEEPS + r + jnp.where(r >= 4, 16, 0)
        for y in range(SWEEPS, size_y - SWEEPS):
            last[SWEEPS + r + w, y] = rows_ref[x, y]

    loop(0, 8, take)
    loop_pairs(0, 16, lambda r: normals(last, r + w - 1 + jnp.where(r >= 8, 2, 0), nx, ny, nz, r))

    def planes(n):
        far = jnp.where(n >= 3, 1, 0)
        gather(last, 2 * n + w + 4 * far, nx, ny, nz, 2 * n + 1 + 2 * far, lump, n, 384, ends, n * 256)

    loop_pairs(0, 6, planes)
    copies = [
        pltpu.make_async_copy(ends.at[pl.ds(1024 * k, 512)], new_ref.at[pl.ds(3584 * k, 512)], sems.at[k])
        for k in range(2)
    ]
    for copy in copies:
        copy.start()
    restrict(lump, range(6), 384, send_ref, lambda i: i + (10 if i >= 3 else 0))
    send_ref[pl.ds(3, 10)] = send_mid_ref[...]
    for copy in copies:
        copy.wait()


def call(kernel, outs, *args, scratch=(), mib=48, ops=1000, name=None, anywhere=(), aliases=None):
    def spec(k):
        return pl.BlockSpec(memory_space=pl.ANY if k in anywhere else pltpu.VMEM)

    aliases = aliases or {}
    flat = outs if isinstance(outs, tuple) else (outs,)
    specs = tuple(pl.BlockSpec(memory_space=pl.ANY if k in aliases.values() else pltpu.VMEM) for k in range(len(flat)))
    return pl.pallas_call(
        kernel,
        out_shape=outs,
        in_specs=[spec(k) for k in range(len(args))],
        out_specs=specs if isinstance(outs, tuple) else specs[0],
        scratch_shapes=[pltpu.VMEM(s, jnp.float32) if isinstance(s, tuple) else s for s in scratch],
        input_output_aliases=aliases,
        compiler_params=params(mib),
        cost_estimate=cost(ops),
        name=name,
    )(*args)


def moved(values, axis, step):
    count = lax.axis_size(axis)
    return lax.ppermute(values, axis, [(i, (i + step) % count) for i in range(count)])


def star(xlo, xhi, ylo, yhi):
    return (moved(xhi, "gx", 1), moved(xlo, "gx", -1), moved(yhi, "gy", 1), moved(ylo, "gy", -1))


def per_device(level_set, flow_velocity, band_mask):
    col = (ROWS, LANES)
    block = f32(32, 16, *col)
    level_rows = level_set.reshape(32, 2, 8, 8, 128).transpose(0, 1, 3, 2, 4).reshape(4096, 128)
    flow_rows = flow_velocity.reshape(3, 16, 8, 4, 128).transpose(0, 1, 3, 2, 4).reshape(1536, 128)

    send = call(pack_velocity, f32(16, 120, 128), flow_rows, name="pack", mib=8)
    coarse = lax.all_to_all(send, "gy", split_axis=0, concat_axis=0, tiled=True)
    start, ylo, yhi = call(
        unpack_level, (block, f32(32, 3, *col), f32(32, 3, *col)), level_rows, name="unpack", mib=8
    )
    both, tips = call(
        depth_sides, (f32(2, 32, 16, *col), f32(2, 2, 16, *col)), start,
        scratch=[block.shape, block.shape, (4, 16, *col), (4, 16, *col)], name="depth", mib=14, ops=512 * 90,
    )
    coarse = coarse.reshape(1920, 128)
    xlo, xhi = call(join_x, (f32(504, 128), f32(504, 128)), start, coarse, tips, name="join", mib=4)
    halo = star(xlo, xhi, ylo, yhi)
    velocity, ends, acc = call(
        refine_and_rate, (f32(3, 32, 16, *col), f32(2, 240, 128), block), coarse, band_mask, start, both,
        scratch=[(3840, 128), (2, *col)], name="refine", mib=20, ops=512 * 110,
    )
    current = start
    for number in range(3):
        if number == 0:
            velocity, acc = call(
                refine_ends, (f32(3, 32, 16, *col), block),
                halo[0], halo[1], ends, band_mask, current, tips, velocity, acc,
                scratch=[(480, 128), (3, 2, 16, *col), (2, 16, *col), pltpu.SemaphoreType.DMA((8,))],
                name="ends", mib=8, anywhere=(6, 7), aliases={6: 0, 7: 1},
            )
        else:
            acc = call(
                inner_rate, block, current, velocity,
                scratch=[block.shape, block.shape, (4, 16, *col), (4, 16, *col)],
                name="inner", mib=12, ops=512 * 140,
            )
        edge = WIDE if number == 2 else 3
        x_edge, y_edge = f32(edge * 128, 128), f32(32, edge, *col)
        current, *edges = call(
            functools.partial(edge_rate, number, edge), (block, x_edge, x_edge, y_edge, y_edge),
            acc, start, current, velocity, *sum(turned_about(number, halo[:2], halo[2:]), ()),
            scratch=[(6, 16, *col)], name="edge", mib=12, ops=512 * 30,
        )
        halo = star(*edges)
    xlo, xhi, ylo, yhi = halo
    levels = call(
        sweep_core, (block,) * SWEEPS, current,
        scratch=[block.shape, block.shape, (2, 16, *col), (2, 16, *col)], name="core", mib=16, ops=512 * 90,
    )
    corner = f32(CORNERS, *col)
    turns = [(2, 16 + 2 * WIDE, *col)] * 2
    side = (32, 16 + 2 * WIDE, *col)
    rims, last = call(
        sweep_sides, (f32(3, 4, *side[1:]), f32(*side)), current, yhi, ylo, *levels,
        scratch=[side] * 4 + turns, name="sides", mib=24, ops=512 * 70,
    )
    corner_low, corner_high = call(
        pack_corners, (corner, corner), xhi, xlo, rims, name="corners", mib=4, anywhere=(2,)
    )
    new_rows, send_mid = call(
        inner_outputs, (f32(4096, 128), f32(10, 64, 128)), last,
        scratch=[(22, 8, *col)] * 3 + [(1280, 128)], name="outputs", mib=14, ops=512 * 40,
    )
    clo, chi = moved(corner_high, "gy", 1), moved(corner_low, "gy", -1)
    ext = (16 + 2 * WIDE, 16 + 2 * WIDE, *col)
    new_rows, packed = call(
        finish, (f32(4096, 128), f32(16, 64, 128)),
        current, xhi, xlo, yhi, ylo, clo, chi, rims, last, send_mid, new_rows,
        scratch=[ext] * 4 + [(16, 8, *col)] * 3 + [(768, 128)] + turns + [(1536, 128), pltpu.SemaphoreType.DMA((2,))],
        name="finish", mib=26, ops=512 * 250, anywhere=(10,), aliases={10: 0},
    )
    returned = lax.all_to_all(packed, "gy", split_axis=0, concat_axis=0, tiled=True).reshape(16, 2, 4, 8, 128)
    new_level = new_rows.reshape(32, 2, 8, 8, 128).transpose(0, 1, 3, 2, 4).reshape(32, 16, 1024)
    flows = [returned[:, k].transpose(0, 2, 1, 3).reshape(1, 128, 512) for k in range(2)]
    return (new_level, flows[0], flows[1])


def solution(mesh):
    placed = (P("gx", "gy", None), P(None, ("gx", "gy"), None, None), P("gx", "gy", None))
    return jax.shard_map(
        per_device,
        mesh=mesh,
        in_specs=placed,
        out_specs=(P("gx", "gy", None), P(("gx", "gy"), None, None), P(("gx", "gy"), None, None)),
        check_vma=False,
    )
```

```python
import functools

import jax
import jax.numpy as jnp
from jax import lax
from jax.experimental import pallas as pl
from jax.experimental.pallas import tpu as pltpu
from jax.sharding import PartitionSpec as P

SWEEPS = 4
TIME_STEP = 0.25
PSEUDO_STEP = 0.3
EPS = 1e-06
FRONT = 1.5
WIDE = SWEEPS + 2

ROWS, LANES = 8, 128
HIGH = lax.Precision.HIGHEST


def params(mib):
    return pltpu.CompilerParams(vmem_limit_bytes=mib * 2**20)


def f32(*shape):
    return jax.ShapeDtypeStruct(shape, jnp.float32)


def cost(vector_ops):
    return pl.CostEstimate(flops=vector_ops * 1024, bytes_accessed=2**23, transcendentals=0)


def shifted(col, step):
    lane = lax.broadcasted_iota(jnp.int32, (ROWS, LANES), 1)
    turned = pltpu.roll(col, (-step) % LANES, 1)
    if step > 0:
        return jnp.where(lane >= LANES - step, pltpu.roll(turned, ROWS - 1, 0), turned)
    return jnp.where(lane < -step, pltpu.roll(turned, 1, 0), turned)


def inverse(values):
    return pl.reciprocal(values, approx=True)


def correction(rough1, rough2, rough3, third1, third2):
    r1, r2, r3 = inverse(rough1), inverse(rough2), inverse(rough3)
    w1 = r1 * r1
    w12 = w1 + 6.0 * (r2 * r2)
    w3 = 3.0 * (r3 * r3)
    return (4.0 * w1 * third1 + (w3 - w12) * third2) * inverse(w12 + w3)


def upwind_part(speed, central, corr):
    return speed * central + jnp.abs(speed) * corr


class March:
    def __init__(self, get):
        self.get = get
        self.made = {}

    def once(self, name, j, make):
        key = (name, j)
        if key not in self.made:
            self.made[key] = make()
        return self.made[key]

    def p(self, j):
        return self.once("p", j, lambda: self.get(j))

    def d(self, j):
        return self.once("d", j, lambda: self.p(j + 1) - self.p(j))

    def curve(self, j):
        return self.once("c", j, lambda: self.d(j) - self.d(j - 1))

    def gap(self, j):
        return self.once("g", j, lambda: self.curve(j + 1) - self.curve(j))

    def third(self, j):
        return self.once("t", j, lambda: self.gap(j) - self.gap(j - 1))

    def base(self, j):
        return self.once("h", j, lambda: (4.0 / 3.0) * (self.gap(j) * self.gap(j)) + EPS)

    def cross(self, j):
        return self.once("x", j, lambda: self.curve(j) * self.curve(j + 1))

    def twice(self, j):
        return self.once("a", j, lambda: (self.curve(j) + self.curve(j)) * self.curve(j))

    def less(self, j):
        return self.once("l", j, lambda: self.base(j) - self.cross(j))

    def mid(self, j):
        return self.once("m", j, lambda: self.base(j) + self.cross(j))

    def up(self, j):
        return self.once("u", j, lambda: self.less(j) + self.twice(j + 1))

    def down(self, j):
        return self.once("v", j, lambda: self.less(j) + self.twice(j))

    def central(self, i):
        return 6.0 * (self.p(i + 1) - self.p(i - 1)) - (self.gap(i) + self.gap(i - 1))

    def part(self, i, speed):
        minus = speed < 0
        corr = correction(
            jnp.where(minus, self.up(i - 2), self.down(i + 1)),
            jnp.where(minus, self.mid(i - 1), self.mid(i)),
            jnp.where(minus, self.down(i), self.up(i - 1)),
            jnp.where(minus, self.third(i - 1), self.third(i + 1)),
            self.third(i),
        )
        return upwind_part(speed, self.central(i), corr)


def depth_rate(slope, here, turned, speed):
    m2, m1, p1, p2 = turned
    minus = speed < 0
    a = jnp.where(minus, m2, p2)
    b = jnp.where(minus, m1, p1)
    d = jnp.where(minus, p1, m1)
    g1, g2, g3 = b - a, here - b, d - here
    corr = correction(
        (4.0 / 3.0) * (g1 * g1) + EPS + b * (b + g1),
        (4.0 / 3.0) * (g2 * g2) + EPS + b * here,
        (4.0 / 3.0) * (g3 * g3) + EPS + here * (here - g3),
        g2 - g1,
        g3 - g2,
    )
    return upwind_part(speed, slope - (p1 - m1), corr)


def loop_pairs(low, high, body):
    def step(i, carry):
        body(low + 2 * i)
        body(low + 2 * i + 1)
        return carry

    lax.fori_loop(0, (high - low) // 2, step, 0)


def loop(low, high, body):
    def step(i, carry):
        body(i)
        return carry

    lax.fori_loop(low, high, step, 0)


def pack_velocity(rows_ref, out_ref):
    def to(g):
        for c in range(3):
            for r in range(10):
                block, low = (g, r - 1) if 1 <= r <= 8 else ((g + 15, 7) if r == 0 else (g + 1, 0))
                start = c * 512 + lax.rem(block, 16) * 32 + low
                out_ref[g, pl.ds((c * 10 + r) * 4, 4), :] = rows_ref[pl.ds(start, 4, stride=8), :]

    loop(0, 16, to)


def unpack_level(rows_ref, p_ref, ylo_ref, yhi_ref):
    def to(x):
        for y in range(16):
            col = rows_ref[pl.ds(x * 128 + (y // 8) * 64 + y % 8, 8, stride=8), :]
            p_ref[x, y] = col
            if y < 3:
                ylo_ref[x, y] = col
            if y >= 13:
                yhi_ref[x, y - 13] = col

    loop(0, 32, to)


def refine_table():
    k = lax.broadcasted_iota(jnp.int32, (256, 256), 0)
    n = lax.broadcasted_iota(jnp.int32, (256, 256), 1)
    beside = jnp.where(n % 2 == 0, n // 2 - 1, n // 2 + 1)
    beside = jnp.where(beside < 0, 255, jnp.where(beside > 127, 128, beside))
    return jnp.where(k == n // 2, 0.75, 0.0) + jnp.where(k == beside, 0.25, 0.0)


def refine_z(plane, table):
    count = plane.shape[0]
    row = lax.broadcasted_iota(jnp.int32, plane.shape, 0) % 4
    lane = lax.broadcasted_iota(jnp.int32, plane.shape, 1)
    after = jnp.where(row == 3, pltpu.roll(plane, 3, 0), pltpu.roll(plane, count - 1, 0))
    prior = jnp.where(row == 0, pltpu.roll(plane, count - 3, 0), pltpu.roll(plane, 1, 0))
    wide = jnp.concatenate([plane, jnp.where(lane < 64, after, prior)], axis=1)
    out = jnp.dot(wide, table, precision=HIGH, preferred_element_type=jnp.float32)
    return out[:, :128], out[:, 128:]


def band_blocks(band_ref):
    k = lax.broadcasted_iota(jnp.int32, (64, 128), 0)
    n = lax.broadcasted_iota(jnp.int32, (64, 128), 1)
    spread = jnp.where(lax.rem(k, 8) == lax.div(n, 16), -TIME_STEP / 12.0, 0.0)
    row = lax.broadcasted_iota(jnp.int32, (8, 64), 0)
    tile = lax.div(lax.broadcasted_iota(jnp.int32, (8, 64), 1), 8)
    blocks = []
    for half in range(2):
        mask = jnp.broadcast_to(band_ref[half].astype(jnp.float32), (8, 64))
        mask = jnp.where(row == tile, mask, 0.0)
        blocks.append(jnp.dot(mask, spread, precision=HIGH, preferred_element_type=jnp.float32))
    return blocks


def refine_inner(mid_ref, band_ref, v_ref, ends_ref, fine, band):
    table = refine_table()
    for half, block in enumerate(band_blocks(band_ref)):
        band[half] = block

    def along_z(k):
        left, right = refine_z(mid_ref[pl.ds(k * 480, 480), :], table)
        fine[pl.ds(k * 960, 480, stride=2), :] = left
        fine[pl.ds(k * 960 + 1, 480, stride=2), :] = right

    loop(0, 4, along_z)
    for end, plane in enumerate((0, 15)):
        ends_ref[end] = fine[pl.ds(plane * 240, 240), :]

    def along_xy(i):
        for c in range(3):
            near, far = [], []
            for r in range(10):
                at = (c * 10 + r) * 8
                near.append(fine[pl.ds(i * 240 + at, 8), :])
                far.append(fine[pl.ds(i * 240 + 240 + at, 8), :])
            for k in range(2):
                x = 2 * i + 1 + k
                line = [0.75 * a + 0.25 * b for a, b in (zip(far, near) if k else zip(near, far))]
                along_y(c, x, line, band[lax.div(x, 16)], v_ref)

    loop(0, 15, along_xy)


def along_y(c, x, line, band, v_ref):
    scaled = [band * value for value in line]
    for y in range(16):
        m = y // 2 + 1
        v_ref[c, x, y] = 0.75 * scaled[m] + 0.25 * scaled[m - 1 + 2 * (y % 2)]


def refine_ends(lo_ref, hi_ref, ends_ref, band_ref, p_ref, tips_ref, v_in, acc_in, v_out, acc_out, fine, ends, part, sems):
    table = refine_table()
    blocks = band_blocks(band_ref)
    for side, ref in enumerate((lo_ref, hi_ref)):
        left, right = refine_z(ref[pl.ds(384, 120), :], table)
        fine[pl.ds(side * 240, 120, stride=2), :] = left
        fine[pl.ds(side * 240 + 1, 120, stride=2), :] = right
    for side in range(2):
        for c in range(3):
            line = []
            for r in range(10):
                at = (c * 10 + r) * 8
                line.append(0.75 * ends_ref[side, pl.ds(at, 8), :] + 0.25 * fine[pl.ds(side * 240 + at, 8), :])
            along_y(c, side, line, blocks[side], ends)
    for side in range(2):
        x = 31 * side
        march = March(lambda y: p_ref[x, y])
        for y in range(16):
            speed = ends[2, side, y]
            total = speed * jnp.where(speed < 0, tips_ref[side, 0, y], tips_ref[side, 1, y])
            if 3 <= y < 13:
                total = total + march.part(y, ends[1, side, y])
            part[side, y] = total
    copies = []
    for side in range(2):
        copies.append((part.at[side], acc_out.at[31 * side]))
        for c in range(3):
            copies.append((ends.at[c, side], v_out.at[c, 31 * side]))
    copies = [pltpu.make_async_copy(src, dst, sems.at[k]) for k, (src, dst) in enumerate(copies)]
    for copy in copies:
        copy.start()
    for copy in copies:
        copy.wait()


def inner_rate(p_ref, v_ref, acc_ref, curve, slope, even, odd):
    def x_line(y):
        march = March(lambda x: p_ref[x, y])
        for x in range(32):
            col = march.p(x)
            before, after = shifted(col, -1), shifted(col, 1)
            curve[x, y] = (after - col) - (col - before)
            slope[x, y] = 6.0 * (after - before)
            if 3 <= x < 29:
                acc_ref[x, y] = march.part(x, v_ref[0, x, y])
            else:
                acc_ref[x, y] = jnp.zeros((ROWS, LANES), jnp.float32)

    loop(0, 16, x_line)

    def turn(x, turned):
        for y in range(16):
            col = curve[x, y]
            for k, step in enumerate((-2, -1, 1, 2)):
                turned[k, y] = shifted(col, step)

    def y_line(x, turned):
        march = March(lambda y: p_ref[x, y])
        for y in range(16):
            total = acc_ref[x, y] + depth_rate(slope[x, y], curve[x, y], [turned[k, y] for k in range(4)], v_ref[2, x, y])
            if 3 <= y < 13:
                total = total + march.part(y, v_ref[1, x, y])
            acc_ref[x, y] = total

    turn(0, even)

    def two(k):
        x = 2 * k
        turn(x + 1, odd)
        y_line(x, even)
        turn(jnp.minimum(x + 2, 31), even)
        y_line(x + 1, odd)

    loop(0, 16, two)


def depth_both(slope, here, turned):
    m2, m1, p1, p2 = turned
    gm2, gm1, g0, g1 = m1 - m2, here - m1, p1 - here, p2 - p1
    bm2, bm1, b0, b1 = [(4.0 / 3.0) * (g * g) + EPS for g in (gm2, gm1, g0, g1)]
    third = g0 - gm1
    below = correction(bm2 + m1 * (m1 + gm2), bm1 + m1 * here, b0 + here * (here - g0), gm1 - gm2, third)
    above = correction(b1 + p1 * (p1 - g1), b0 + p1 * here, bm1 + here * (here + gm1), g1 - g0, third)
    central = slope - (p1 - m1)
    return central - below, central + above


def depth_sides(p_ref, both_ref, tips_ref, curve, slope, even, odd):
    def curves(x):
        for y in range(16):
            col = p_ref[x, y]
            before, after = shifted(col, -1), shifted(col, 1)
            curve[x, y] = (after - col) - (col - before)
            slope[x, y] = 6.0 * (after - before)

    def turned_row(x, turned):
        for y in range(16):
            col = curve[x, y]
            for k, step in enumerate((-2, -1, 1, 2)):
                turned[k, y] = shifted(col, step)

    def rates(x, turned):
        for y in range(16):
            both = depth_both(slope[x, y], curve[x, y], [turned[k, y] for k in range(4)])
            both_ref[0, x, y], both_ref[1, x, y] = both

    for x in range(3):
        curves(x)
    turned_row(0, even)

    def two(k):
        x = 2 * k
        turned_row(x + 1, odd)
        rates(x, even)
        turned_row(jnp.minimum(x + 2, 31), even)
        rates(x + 1, odd)
        curves(jnp.minimum(x + 3, 31))
        curves(jnp.minimum(x + 4, 31))

    loop(0, 16, two)
    for side in range(2):
        for k in range(2):
            for y in range(16):
                tips_ref[side, k, y] = both_ref[k, 31 * side, y]


def inner_rate_first(p_ref, v_ref, both_ref, acc_ref):
    def x_line(y):
        march = March(lambda x: p_ref[x, y])
        for x in range(32):
            if 3 <= x < 29:
                acc_ref[x, y] = march.part(x, v_ref[0, x, y])
            else:
                acc_ref[x, y] = jnp.zeros((ROWS, LANES), jnp.float32)

    def y_line(x):
        march = March(lambda y: p_ref[x, y])
        for y in range(16):
            speed = v_ref[2, x, y]
            total = acc_ref[x, y] + speed * jnp.where(speed < 0, both_ref[0, x, y], both_ref[1, x, y])
            if 3 <= y < 13:
                total = total + march.part(y, v_ref[1, x, y])
            acc_ref[x, y] = total

    loop(0, 16, x_line)
    loop_pairs(1, 31, y_line)


def join_x(p_ref, coarse_ref, mark_ref, low_ref, high_ref):
    for x in range(3):
        for y in range(16):
            at = pl.ds((x * 16 + y) * 8, 8)
            low_ref[at, :] = p_ref[x, y]
            high_ref[at, :] = p_ref[29 + x, y]
    for k in range(15):
        low_ref[pl.ds(384 + 8 * k, 8), :] = coarse_ref[pl.ds(8 * k, 8), :]
        high_ref[pl.ds(384 + 8 * k, 8), :] = coarse_ref[pl.ds(1800 + 8 * k, 8), :]


def section(start, current, rate, number):
    if number == 0:
        return current + rate
    if number == 1:
        return 0.75 * start + 0.25 * (current + rate)
    return start * (1.0 / 3.0) + (2.0 / 3.0) * (current + rate)


def turned_about(number, *pairs):
    return [pair[::-1] if number % 2 else pair for pair in pairs]


def edge_rate(
    number, edge, acc_ref, start_ref, p_ref, v_ref, x1_ref, x2_ref, y1_ref, y2_ref,
    new_ref, nxlo_ref, nxhi_ref, nylo_ref, nyhi_ref, side,
):
    (xlo_ref, xhi_ref), (ylo_ref, yhi_ref) = turned_about(number, (x1_ref, x2_ref), (y1_ref, y2_ref))

    def from_rows(ref, x, y):
        return ref[pl.ds((x * 16 + y) * 8, 8), :]

    def x_line(y):
        low = March(lambda x: from_rows(xlo_ref, x + 3, y) if x < 0 else p_ref[x, y])
        high = March(lambda x: from_rows(xhi_ref, x - 32, y) if x >= 32 else p_ref[x, y])
        for k in range(3):
            side[k, y] = low.part(k, v_ref[0, k, y])
            side[k + 3, y] = high.part(29 + k, v_ref[0, 29 + k, y])

    loop_pairs(0, 16, x_line)

    def y_line(x, side_x, outs):
        low = March(lambda y: ylo_ref[x, y + 3] if y < 0 else p_ref[x, y])
        high = March(lambda y: yhi_ref[x, y - 16] if y >= 16 else p_ref[x, y])
        for y in range(16):
            rate = acc_ref[x, y]
            if side_x is not None:
                rate = rate + side[side_x, y]
            if y < 3:
                rate = rate + low.part(y, v_ref[1, x, y])
            if y >= 13:
                rate = rate + high.part(y, v_ref[1, x, y])
            start = None if number == 0 else start_ref[x, y]
            new = section(start, p_ref[x, y], rate, number)
            new_ref[x, y] = new
            if outs is not None:
                outs[0][pl.ds((outs[1] * 16 + y) * 8, 8), :] = new
            if y < edge:
                nylo_ref[x, y] = new
            if y >= 16 - edge:
                nyhi_ref[x, y - (16 - edge)] = new

    loop(0, 3, lambda x: y_line(x, x, (nxlo_ref, x)))
    loop(29, 32, lambda x: y_line(x, x - 26, (nxhi_ref, x - (32 - edge))))
    if edge > 3:
        loop(3, edge, lambda x: y_line(x, None, (nxlo_ref, x)))
        loop(32 - edge, 29, lambda x: y_line(x, None, (nxhi_ref, x - (32 - edge))))
    loop_pairs(edge, 32 - edge, lambda x: y_line(x, None, None))


def pushes(col):
    push = (PSEUDO_STEP * col) * lax.rsqrt(col * col + 1.0)
    return push, jnp.where(col > 0, 1.0, -1.0)


def turn(src, x, ys, turned):
    for y in ys:
        col = src[x, y]
        turned[0, y] = shifted(col, -1)
        turned[1, y] = shifted(col, 1)


def sweep_line(src, dst, push, sign, x, ys, turned):
    cols = {}

    def at(y):
        if y not in cols:
            cols[y] = src[x, y]
        return cols[y]

    for y in ys:
        col, c, s = at(y), push[x, y], sign[x, y]
        here = s * col
        total = None
        for pair in ((src[x - 1, y], src[x + 1, y]), (at(y - 1), at(y + 1)), (turned[0, y], turned[1, y])):
            floor = 1e-15 if total is None else 0.0
            rise = jnp.maximum(here - jnp.minimum(s * pair[0], s * pair[1]), floor)
            total = rise * rise if total is None else total + rise * rise
        dst[x, y] = (col + c) - (c * total) * lax.rsqrt(total)


def sweep_rows(src, dst, push, sign, place, pairs, ys, even, odd):
    turn(src, place(0), ys, even)

    def two(j):
        x = place(j)
        turn(src, x + 1, ys, odd)
        sweep_line(src, dst, push, sign, x, ys, even)
        turn(src, place(jnp.minimum(j + 1, pairs - 1)), ys, even)
        sweep_line(src, dst, push, sign, x + 1, ys, odd)

    loop(0, pairs, two)


def sweep_core(adv_ref, *refs):
    levels, (push, sign, even, odd) = refs[:SWEEPS], refs[SWEEPS:]

    def prepare(x):
        for y in range(16):
            push[x, y], sign[x, y] = pushes(adv_ref[x, y])

    loop_pairs(0, 32, prepare)
    src = adv_ref
    for k in range(1, SWEEPS + 1):
        dst = levels[k - 1]
        sweep_rows(src, dst, push, sign, lambda j, k=k: k + 2 * j, 16 - k, range(k, 16 - k), even, odd)
        src = dst


def pack_corners(xhi_ref, xlo_ref, _, low_ref, high_ref):
    k = 0
    for dx in range(1, WIDE):
        for ref, x in ((xlo_ref, WIDE - dx), (xhi_ref, dx - 1)):
            for dy in range(1, WIDE - dx + 1):
                low_ref[k] = ref[pl.ds((x * 16 + dy - 1) * 8, 8), :]
                high_ref[k] = ref[pl.ds((x * 16 + 16 - dy) * 8, 8), :]
                k += 1


CORNERS = WIDE * (WIDE - 1)


def normals(last, xs, nx, ny, nz, at):
    cols = {}

    def col(y):
        if y not in cols:
            cols[y] = last[xs, y + WIDE]
        return cols[y]

    across, along, deep = {}, {}, {}
    for y in range(-1, 17):
        gx = last[xs + 1, y + WIDE] - last[xs - 1, y + WIDE]
        gy = col(y + 1) - col(y - 1)
        gz = shifted(col(y), 1) - shifted(col(y), -1)
        scale = lax.rsqrt(gx * gx + gy * gy + gz * gz + 4.0)
        across[y], along[y], deep[y] = gx * scale, gy * scale, gz * scale
    for j in range(8):
        a, b = 2 * j, 2 * j + 1
        nx[at, j] = across[a] + across[b]
        ny[at, j] = (along[b] + along[b + 1]) - (along[a - 1] + along[a])
        nz[at, j] = deep[a] + deep[b]


def gather(last, xs, nx, ny, nz, at, lump, slot, half, new, new_at):
    a, b = at, at + 1
    for j in range(8):
        deep = nz[a, j] + nz[b, j]
        total = (nx[b, j] + nx[b + 1, j]) - (nx[a - 1, j] + nx[a, j]) + (ny[a, j] + ny[b, j])
        lump[pl.ds(slot * 64 + j * 8, 8), :] = total + (shifted(deep, 1) - shifted(deep, -1))
        share = None
        for x in range(2):
            for y in range(2):
                yy = 2 * j + y
                col = last[xs + x, yy + WIDE]
                new[pl.ds(new_at + x * 128 + (yy // 8) * 64 + yy % 8, 8, stride=8), :] = col
                bend = jnp.tanh(col * (1.0 / FRONT))
                share = bend if share is None else share + bend
        lump[pl.ds(half + slot * 64 + j * 8, 8), :] = share


def restrict(lump, slots, half, send, send_at):
    k = lax.broadcasted_iota(jnp.int32, (256, 128), 0)
    n = lax.broadcasted_iota(jnp.int32, (256, 128), 1)
    table = jnp.where(lax.div(k, 2) == n, 1.0 / 16.0, 0.0)
    halves = []
    for odd_row in range(2):
        rows = []
        for kind in range(2):
            for i in slots:
                base = kind * half + i * 64 + odd_row
                rows += [lump[pl.ds(base + 2 * z, 8, stride=8), :] for z in range(4)]
        halves.append(jnp.concatenate(rows, axis=0))
    out = jnp.dot(jnp.concatenate(halves, axis=1), table, precision=HIGH, preferred_element_type=jnp.float32)
    for n, i in enumerate(slots):
        send[send_at(i), pl.ds(0, 32), :] = out[n * 32 : n * 32 + 32]
        send[send_at(i), pl.ds(32, 32), :] = out[(len(slots) + n) * 32 : (len(slots) + n) * 32 + 32] + 0.5


def sweep_sides(
    adv_ref, yhi_ref, ylo_ref, one_ref, two_ref, three_ref, four_ref,
    rims_ref, last_ref, q0, q1, push, sign, even, odd,
):
    w = WIDE
    size_y = 16 + 2 * w

    def put(x, y, col):
        q0[x, y] = col
        push[x, y], sign[x, y] = pushes(col)

    def fill(x):
        for y in range(w):
            put(x, y, ylo_ref[x, y])
            put(x, y + 16 + w, yhi_ref[x, y])
        for y in (0, 1, 2, 3, 12, 13, 14, 15):
            put(x, y + w, adv_ref[x, y])

    loop_pairs(0, 32, fill)
    src, dst = q0, q1
    for k, core_ref in enumerate((one_ref, two_ref, three_ref, four_ref), 1):
        dst = last_ref if k == SWEEPS else dst
        sides = [*range(k, k + w), *range(size_y - k - w, size_y - k)]
        sweep_rows(src, dst, push, sign, lambda j, k=k: k + 2 * j, 16 - k, sides, even, odd)
        inside = (k, k + 1, 14 - k, 15 - k) if k < SWEEPS else range(k, 16 - k)

        def take(x, core_ref=core_ref, inside=inside, dst=dst):
            for y in inside:
                dst[x, y + w] = core_ref[x, y]

        loop_pairs(k, 32 - k, take)
        if k < SWEEPS:
            for r, x in enumerate((k, k + 1, 30 - k, 31 - k)):
                for y in range(k, size_y - k):
                    inner = k + 2 <= y - w < 14 - k
                    rims_ref[k - 1, r, y] = core_ref[x, y - w] if inner else dst[x, y]
        src, dst = dst, src


def inner_outputs(last, new_ref, send_ref, nx, ny, nz, lump):
    loop_pairs(0, 22, lambda r: normals(last, r + 5, nx, ny, nz, r))

    def planes(n):
        gather(last, 2 * n + 6, nx, ny, nz, 2 * n + 1, lump, n, 640, new_ref, (2 * n + 6) * 128)

    loop_pairs(0, 10, planes)
    for x in (4, 5, 26, 27):
        for y in range(16):
            new_ref[pl.ds(x * 128 + (y // 8) * 64 + y % 8, 8, stride=8), :] = last[x, y + WIDE]
    for part in range(2):
        restrict(lump, range(5 * part, 5 * part + 5), 640, send_ref, lambda i: i)


def finish(
    adv_ref, xhi_ref, xlo_ref, yhi_ref, ylo_ref, clo_ref, chi_ref, rims_ref, rows_ref, send_mid_ref, _,
    new_ref, send_ref, q0, q1, push, sign, nx, ny, nz, lump, even, odd, ends, sems,
):
    w = WIDE
    size_y = 16 + 2 * w

    def put(x, y, col):
        q0[x, y] = col
        push[x, y], sign[x, y] = pushes(col)

    def fill_mid(r):
        x = r + jnp.where(r >= 4, 24, 0)
        at = r + w + jnp.where(r >= 4, 8, 0)
        for y in range(w):
            put(at, y, ylo_ref[x, y])
            put(at, y + 16 + w, yhi_ref[x, y])
        for y in range(16):
            put(at, y + w, adv_ref[x, y])

    def fill_side(x):
        for y in range(16):
            put(x, y + w, xlo_ref[pl.ds((x * 16 + y) * 8, 8), :])
            put(x + 16 + w, y + w, xhi_ref[pl.ds((x * 16 + y) * 8, 8), :])

    loop_pairs(0, 8, fill_mid)
    loop_pairs(0, w, fill_side)
    k = 0
    for dx in range(1, w):
        for x in (w - dx, w + 15 + dx):
            for dy in range(1, w - dx + 1):
                put(x, w - dy, clo_ref[k])
                put(x, w + 15 + dy, chi_ref[k])
                k += 1

    src, dst = q0, q1
    for k in range(1, SWEEPS + 1):

        def end_rows(j, k=k):
            return k + 2 * j + jnp.where(j >= 3, 16 - 2 * k, 0)

        sweep_rows(src, dst, push, sign, end_rows, 6, range(k, size_y - k), even, odd)
        if k < SWEEPS:
            for r, x in enumerate((k, k + 1, 14 - k, 15 - k)):
                for y in range(k, size_y - k):
                    dst[x + w, y] = rims_ref[k - 1, r, y]
        src, dst = dst, src
    last = src

    def take(r):
        x = SWEEPS + r + jnp.where(r >= 4, 16, 0)
        for y in range(SWEEPS, size_y - SWEEPS):
            last[SWEEPS + r + w, y] = rows_ref[x, y]

    loop(0, 8, take)
    loop_pairs(0, 16, lambda r: normals(last, r + w - 1 + jnp.where(r >= 8, 2, 0), nx, ny, nz, r))

    def planes(n):
        far = jnp.where(n >= 3, 1, 0)
        gather(last, 2 * n + w + 4 * far, nx, ny, nz, 2 * n + 1 + 2 * far, lump, n, 384, ends, n * 256)

    loop_pairs(0, 6, planes)
    copies = [
        pltpu.make_async_copy(ends.at[pl.ds(1024 * k, 512)], new_ref.at[pl.ds(3584 * k, 512)], sems.at[k])
        for k in range(2)
    ]
    for copy in copies:
        copy.start()
    restrict(lump, range(6), 384, send_ref, lambda i: i + (10 if i >= 3 else 0))
    send_ref[pl.ds(3, 10)] = send_mid_ref[...]
    for copy in copies:
        copy.wait()


def call(kernel, outs, *args, scratch=(), mib=48, ops=1000, name=None, anywhere=(), aliases=None):
    def spec(k):
        return pl.BlockSpec(memory_space=pl.ANY if k in anywhere else pltpu.VMEM)

    aliases = aliases or {}
    flat = outs if isinstance(outs, tuple) else (outs,)
    specs = tuple(pl.BlockSpec(memory_space=pl.ANY if k in aliases.values() else pltpu.VMEM) for k in range(len(flat)))
    return pl.pallas_call(
        kernel,
        out_shape=outs,
        in_specs=[spec(k) for k in range(len(args))],
        out_specs=specs if isinstance(outs, tuple) else specs[0],
        scratch_shapes=[pltpu.VMEM(s, jnp.float32) if isinstance(s, tuple) else s for s in scratch],
        input_output_aliases=aliases,
        compiler_params=params(mib),
        cost_estimate=cost(ops),
        name=name,
    )(*args)


def moved(values, axis, step):
    count = lax.axis_size(axis)
    return lax.ppermute(values, axis, [(i, (i + step) % count) for i in range(count)])


def star(xlo, xhi, ylo, yhi):
    return (moved(xhi, "gx", 1), moved(xlo, "gx", -1), moved(yhi, "gy", 1), moved(ylo, "gy", -1))


def per_device(level_set, flow_velocity, band_mask):
    col = (ROWS, LANES)
    block = f32(32, 16, *col)
    level_rows = level_set.reshape(32, 2, 8, 8, 128).transpose(0, 1, 3, 2, 4).reshape(4096, 128)
    flow_rows = flow_velocity.reshape(3, 16, 8, 4, 128).transpose(0, 1, 3, 2, 4).reshape(1536, 128)

    send = call(pack_velocity, f32(16, 120, 128), flow_rows, name="pack", mib=8)
    coarse = lax.all_to_all(send, "gy", split_axis=0, concat_axis=0, tiled=True)
    start, ylo, yhi = call(
        unpack_level, (block, f32(32, 3, *col), f32(32, 3, *col)), level_rows, name="unpack", mib=8
    )
    both, tips = call(
        depth_sides, (f32(2, 32, 16, *col), f32(2, 2, 16, *col)), start,
        scratch=[block.shape, block.shape, (4, 16, *col), (4, 16, *col)], name="depth", mib=14, ops=512 * 90,
    )
    coarse = coarse.reshape(1920, 128)
    xlo, xhi = call(join_x, (f32(504, 128), f32(504, 128)), start, coarse, tips, name="join", mib=4)
    halo = star(xlo, xhi, ylo, yhi)
    velocity, ends = call(
        refine_inner, (f32(3, 32, 16, *col), f32(2, 240, 128)), coarse, band_mask,
        scratch=[(3840, 128), (2, *col)], name="refine", mib=20, ops=512 * 20,
    )
    acc = call(inner_rate_first, block, start, velocity, both, name="first", mib=12, ops=512 * 90)
    current = start
    for number in range(3):
        if number == 0:
            velocity, acc = call(
                refine_ends, (f32(3, 32, 16, *col), block),
                halo[0], halo[1], ends, band_mask, current, tips, velocity, acc,
                scratch=[(480, 128), (3, 2, 16, *col), (2, 16, *col), pltpu.SemaphoreType.DMA((8,))],
                name="ends", mib=8, anywhere=(6, 7), aliases={6: 0, 7: 1},
            )
        else:
            acc = call(
                inner_rate, block, current, velocity,
                scratch=[block.shape, block.shape, (4, 16, *col), (4, 16, *col)],
                name="inner", mib=12, ops=512 * 140,
            )
        edge = WIDE if number == 2 else 3
        x_edge, y_edge = f32(edge * 128, 128), f32(32, edge, *col)
        current, *edges = call(
            functools.partial(edge_rate, number, edge), (block, x_edge, x_edge, y_edge, y_edge),
            acc, start, current, velocity, *sum(turned_about(number, halo[:2], halo[2:]), ()),
            scratch=[(6, 16, *col)], name="edge", mib=12, ops=512 * 30,
        )
        halo = star(*edges)
    xlo, xhi, ylo, yhi = halo
    levels = call(
        sweep_core, (block,) * SWEEPS, current,
        scratch=[block.shape, block.shape, (2, 16, *col), (2, 16, *col)], name="core", mib=16, ops=512 * 90,
    )
    corner = f32(CORNERS, *col)
    turns = [(2, 16 + 2 * WIDE, *col)] * 2
    side = (32, 16 + 2 * WIDE, *col)
    rims, last = call(
        sweep_sides, (f32(3, 4, *side[1:]), f32(*side)), current, yhi, ylo, *levels,
        scratch=[side] * 4 + turns, name="sides", mib=24, ops=512 * 70,
    )
    corner_low, corner_high = call(
        pack_corners, (corner, corner), xhi, xlo, rims, name="corners", mib=4, anywhere=(2,)
    )
    new_rows, send_mid = call(
        inner_outputs, (f32(4096, 128), f32(10, 64, 128)), last,
        scratch=[(22, 8, *col)] * 3 + [(1280, 128)], name="outputs", mib=14, ops=512 * 40,
    )
    clo, chi = moved(corner_high, "gy", 1), moved(corner_low, "gy", -1)
    ext = (16 + 2 * WIDE, 16 + 2 * WIDE, *col)
    new_rows, packed = call(
        finish, (f32(4096, 128), f32(16, 64, 128)),
        current, xhi, xlo, yhi, ylo, clo, chi, rims, last, send_mid, new_rows,
        scratch=[ext] * 4 + [(16, 8, *col)] * 3 + [(768, 128)] + turns + [(1536, 128), pltpu.SemaphoreType.DMA((2,))],
        name="finish", mib=26, ops=512 * 250, anywhere=(10,), aliases={10: 0},
    )
    returned = lax.all_to_all(packed, "gy", split_axis=0, concat_axis=0, tiled=True).reshape(16, 2, 4, 8, 128)
    new_level = new_rows.reshape(32, 2, 8, 8, 128).transpose(0, 1, 3, 2, 4).reshape(32, 16, 1024)
    flows = [returned[:, k].transpose(0, 2, 1, 3).reshape(1, 128, 512) for k in range(2)]
    return (new_level, flows[0], flows[1])


def solution(mesh):
    placed = (P("gx", "gy", None), P(None, ("gx", "gy"), None, None), P("gx", "gy", None))
    return jax.shard_map(
        per_device,
        mesh=mesh,
        in_specs=placed,
        out_specs=(P("gx", "gy", None), P(("gx", "gy"), None, None), P(("gx", "gy"), None, None)),
        check_vma=False,
    )
```

```python
import functools

import jax
import jax.numpy as jnp
from jax import lax
from jax.experimental import pallas as pl
from jax.experimental.pallas import tpu as pltpu
from jax.sharding import PartitionSpec as P

SWEEPS = 4
TIME_STEP = 0.25
PSEUDO_STEP = 0.3
EPS = 1e-06
FRONT = 1.5
WIDE = SWEEPS + 2

ROWS, LANES = 8, 128
HIGH = lax.Precision.HIGHEST


def params(mib):
    return pltpu.CompilerParams(vmem_limit_bytes=mib * 2**20)


def f32(*shape):
    return jax.ShapeDtypeStruct(shape, jnp.float32)


def cost(vector_ops):
    return pl.CostEstimate(flops=vector_ops * 1024, bytes_accessed=2**23, transcendentals=0)


def shifted(col, step):
    lane = lax.broadcasted_iota(jnp.int32, (ROWS, LANES), 1)
    turned = pltpu.roll(col, (-step) % LANES, 1)
    if step > 0:
        return jnp.where(lane >= LANES - step, pltpu.roll(turned, ROWS - 1, 0), turned)
    return jnp.where(lane < -step, pltpu.roll(turned, 1, 0), turned)


def inverse(values):
    return pl.reciprocal(values, approx=True)


def correction(rough1, rough2, rough3, third1, third2):
    r1, r2, r3 = inverse(rough1), inverse(rough2), inverse(rough3)
    w1 = r1 * r1
    w12 = w1 + 6.0 * (r2 * r2)
    w3 = 3.0 * (r3 * r3)
    return (4.0 * w1 * third1 + (w3 - w12) * third2) * inverse(w12 + w3)


def upwind_part(speed, central, corr):
    return speed * central + jnp.abs(speed) * corr


class March:
    def __init__(self, get):
        self.get = get
        self.made = {}

    def once(self, name, j, make):
        key = (name, j)
        if key not in self.made:
            self.made[key] = make()
        return self.made[key]

    def p(self, j):
        return self.once("p", j, lambda: self.get(j))

    def d(self, j):
        return self.once("d", j, lambda: self.p(j + 1) - self.p(j))

    def curve(self, j):
        return self.once("c", j, lambda: self.d(j) - self.d(j - 1))

    def gap(self, j):
        return self.once("g", j, lambda: self.curve(j + 1) - self.curve(j))

    def third(self, j):
        return self.once("t", j, lambda: self.gap(j) - self.gap(j - 1))

    def base(self, j):
        return self.once("h", j, lambda: (4.0 / 3.0) * (self.gap(j) * self.gap(j)) + EPS)

    def cross(self, j):
        return self.once("x", j, lambda: self.curve(j) * self.curve(j + 1))

    def twice(self, j):
        return self.once("a", j, lambda: (self.curve(j) + self.curve(j)) * self.curve(j))

    def less(self, j):
        return self.once("l", j, lambda: self.base(j) - self.cross(j))

    def mid(self, j):
        return self.once("m", j, lambda: self.base(j) + self.cross(j))

    def up(self, j):
        return self.once("u", j, lambda: self.less(j) + self.twice(j + 1))

    def down(self, j):
        return self.once("v", j, lambda: self.less(j) + self.twice(j))

    def central(self, i):
        return 6.0 * (self.p(i + 1) - self.p(i - 1)) - (self.gap(i) + self.gap(i - 1))

    def part(self, i, speed):
        minus = speed < 0
        corr = correction(
            jnp.where(minus, self.up(i - 2), self.down(i + 1)),
            jnp.where(minus, self.mid(i - 1), self.mid(i)),
            jnp.where(minus, self.down(i), self.up(i - 1)),
            jnp.where(minus, self.third(i - 1), self.third(i + 1)),
            self.third(i),
        )
        return upwind_part(speed, self.central(i), corr)


def depth_rate(slope, here, turned, speed):
    m2, m1, p1, p2 = turned
    minus = speed < 0
    a = jnp.where(minus, m2, p2)
    b = jnp.where(minus, m1, p1)
    d = jnp.where(minus, p1, m1)
    g1, g2, g3 = b - a, here - b, d - here
    corr = correction(
        (4.0 / 3.0) * (g1 * g1) + EPS + b * (b + g1),
        (4.0 / 3.0) * (g2 * g2) + EPS + b * here,
        (4.0 / 3.0) * (g3 * g3) + EPS + here * (here - g3),
        g2 - g1,
        g3 - g2,
    )
    return upwind_part(speed, slope - (p1 - m1), corr)


def loop_pairs(low, high, body):
    def step(i, carry):
        body(low + 2 * i)
        body(low + 2 * i + 1)
        return carry

    lax.fori_loop(0, (high - low) // 2, step, 0)


def loop(low, high, body):
    def step(i, carry):
        body(i)
        return carry

    lax.fori_loop(low, high, step, 0)


def pack_velocity(rows_ref, out_ref):
    def to(g):
        for c in range(3):
            for r in range(10):
                block, low = (g, r - 1) if 1 <= r <= 8 else ((g + 15, 7) if r == 0 else (g + 1, 0))
                start = c * 512 + lax.rem(block, 16) * 32 + low
                out_ref[g, pl.ds((c * 10 + r) * 4, 4), :] = rows_ref[pl.ds(start, 4, stride=8), :]

    loop_pairs(0, 16, to)


def unpack_level(rows_ref, p_ref, ylo_ref, yhi_ref):
    def to(x):
        for y in range(16):
            col = rows_ref[pl.ds(x * 128 + (y // 8) * 64 + y % 8, 8, stride=8), :]
            p_ref[x, y] = col
            if y < 3:
                ylo_ref[x, y] = col
            if y >= 13:
                yhi_ref[x, y - 13] = col

    loop_pairs(0, 32, to)


def refine_table():
    k = lax.broadcasted_iota(jnp.int32, (256, 256), 0)
    n = lax.broadcasted_iota(jnp.int32, (256, 256), 1)
    beside = jnp.where(n % 2 == 0, n // 2 - 1, n // 2 + 1)
    beside = jnp.where(beside < 0, 255, jnp.where(beside > 127, 128, beside))
    return jnp.where(k == n // 2, 0.75, 0.0) + jnp.where(k == beside, 0.25, 0.0)


def refine_z(plane, table):
    count = plane.shape[0]
    row = lax.broadcasted_iota(jnp.int32, plane.shape, 0) % 4
    lane = lax.broadcasted_iota(jnp.int32, plane.shape, 1)
    after = jnp.where(row == 3, pltpu.roll(plane, 3, 0), pltpu.roll(plane, count - 1, 0))
    prior = jnp.where(row == 0, pltpu.roll(plane, count - 3, 0), pltpu.roll(plane, 1, 0))
    wide = jnp.concatenate([plane, jnp.where(lane < 64, after, prior)], axis=1)
    out = jnp.dot(wide, table, precision=HIGH, preferred_element_type=jnp.float32)
    return out[:, :128], out[:, 128:]


def band_blocks(band_ref):
    k = lax.broadcasted_iota(jnp.int32, (64, 128), 0)
    n = lax.broadcasted_iota(jnp.int32, (64, 128), 1)
    spread = jnp.where(lax.rem(k, 8) == lax.div(n, 16), -TIME_STEP / 12.0, 0.0)
    row = lax.broadcasted_iota(jnp.int32, (8, 64), 0)
    tile = lax.div(lax.broadcasted_iota(jnp.int32, (8, 64), 1), 8)
    blocks = []
    for half in range(2):
        mask = jnp.broadcast_to(band_ref[half].astype(jnp.float32), (8, 64))
        mask = jnp.where(row == tile, mask, 0.0)
        blocks.append(jnp.dot(mask, spread, precision=HIGH, preferred_element_type=jnp.float32))
    return blocks


def refine_inner(mid_ref, band_ref, v_ref, ends_ref, fine, band):
    table = refine_table()
    for half, block in enumerate(band_blocks(band_ref)):
        band[half] = block

    def along_z(k):
        left, right = refine_z(mid_ref[pl.ds(k * 480, 480), :], table)
        fine[pl.ds(k * 960, 480, stride=2), :] = left
        fine[pl.ds(k * 960 + 1, 480, stride=2), :] = right

    loop(0, 4, along_z)
    for end, plane in enumerate((0, 15)):
        ends_ref[end] = fine[pl.ds(plane * 240, 240), :]

    def along_xy(i):
        for c in range(3):
            near, far = [], []
            for r in range(10):
                at = (c * 10 + r) * 8
                near.append(fine[pl.ds(i * 240 + at, 8), :])
                far.append(fine[pl.ds(i * 240 + 240 + at, 8), :])
            for k in range(2):
                x = 2 * i + 1 + k
                line = [0.75 * a + 0.25 * b for a, b in (zip(far, near) if k else zip(near, far))]
                along_y(c, x, line, band[lax.div(x, 16)], v_ref)

    loop(0, 15, along_xy)


def along_y(c, x, line, band, v_ref):
    scaled = [band * value for value in line]
    for y in range(16):
        m = y // 2 + 1
        v_ref[c, x, y] = 0.75 * scaled[m] + 0.25 * scaled[m - 1 + 2 * (y % 2)]


def refine_ends(lo_ref, hi_ref, ends_ref, band_ref, p_ref, tips_ref, v_in, acc_in, v_out, acc_out, fine, ends, part, sems):
    table = refine_table()
    blocks = band_blocks(band_ref)
    for side, ref in enumerate((lo_ref, hi_ref)):
        left, right = refine_z(ref[pl.ds(384, 120), :], table)
        fine[pl.ds(side * 240, 120, stride=2), :] = left
        fine[pl.ds(side * 240 + 1, 120, stride=2), :] = right
    for side in range(2):
        for c in range(3):
            line = []
            for r in range(10):
                at = (c * 10 + r) * 8
                line.append(0.75 * ends_ref[side, pl.ds(at, 8), :] + 0.25 * fine[pl.ds(side * 240 + at, 8), :])
            along_y(c, side, line, blocks[side], ends)
    for side in range(2):
        x = 31 * side
        march = March(lambda y: p_ref[x, y])
        for y in range(16):
            speed = ends[2, side, y]
            total = speed * jnp.where(speed < 0, tips_ref[side, 0, y], tips_ref[side, 1, y])
            if 3 <= y < 13:
                total = total + march.part(y, ends[1, side, y])
            part[side, y] = total
    copies = []
    for side in range(2):
        copies.append((part.at[side], acc_out.at[31 * side]))
        for c in range(3):
            copies.append((ends.at[c, side], v_out.at[c, 31 * side]))
    copies = [pltpu.make_async_copy(src, dst, sems.at[k]) for k, (src, dst) in enumerate(copies)]
    for copy in copies:
        copy.start()
    for copy in copies:
        copy.wait()


def inner_rate(p_ref, v_ref, acc_ref, curve, slope, even, odd):
    def x_line(y):
        march = March(lambda x: p_ref[x, y])
        for x in range(32):
            col = march.p(x)
            before, after = shifted(col, -1), shifted(col, 1)
            curve[x, y] = (after - col) - (col - before)
            slope[x, y] = 6.0 * (after - before)
            if 3 <= x < 29:
                acc_ref[x, y] = march.part(x, v_ref[0, x, y])
            else:
                acc_ref[x, y] = jnp.zeros((ROWS, LANES), jnp.float32)

    loop(0, 16, x_line)

    def turn(x, turned):
        for y in range(16):
            col = curve[x, y]
            for k, step in enumerate((-2, -1, 1, 2)):
                turned[k, y] = shifted(col, step)

    def y_line(x, turned):
        march = March(lambda y: p_ref[x, y])
        for y in range(16):
            total = acc_ref[x, y] + depth_rate(slope[x, y], curve[x, y], [turned[k, y] for k in range(4)], v_ref[2, x, y])
            if 3 <= y < 13:
                total = total + march.part(y, v_ref[1, x, y])
            acc_ref[x, y] = total

    turn(0, even)

    def two(k):
        x = 2 * k
        turn(x + 1, odd)
        y_line(x, even)
        turn(jnp.minimum(x + 2, 31), even)
        y_line(x + 1, odd)

    loop(0, 16, two)


def depth_both(slope, here, turned):
    m2, m1, p1, p2 = turned
    gm2, gm1, g0, g1 = m1 - m2, here - m1, p1 - here, p2 - p1
    bm2, bm1, b0, b1 = [(4.0 / 3.0) * (g * g) + EPS for g in (gm2, gm1, g0, g1)]
    third = g0 - gm1
    below = correction(bm2 + m1 * (m1 + gm2), bm1 + m1 * here, b0 + here * (here - g0), gm1 - gm2, third)
    above = correction(b1 + p1 * (p1 - g1), b0 + p1 * here, bm1 + here * (here + gm1), g1 - g0, third)
    central = slope - (p1 - m1)
    return central - below, central + above


def depth_sides(p_ref, both_ref, tips_ref, curve, slope, even, odd):
    def curves(x):
        for y in range(16):
            col = p_ref[x, y]
            before, after = shifted(col, -1), shifted(col, 1)
            curve[x, y] = (after - col) - (col - before)
            slope[x, y] = 6.0 * (after - before)

    def turned_row(x, turned):
        for y in range(16):
            col = curve[x, y]
            for k, step in enumerate((-2, -1, 1, 2)):
                turned[k, y] = shifted(col, step)

    def rates(x, turned):
        for y in range(16):
            both = depth_both(slope[x, y], curve[x, y], [turned[k, y] for k in range(4)])
            both_ref[0, x, y], both_ref[1, x, y] = both

    for x in range(3):
        curves(x)
    turned_row(0, even)

    def two(k):
        x = 2 * k
        turned_row(x + 1, odd)
        rates(x, even)
        turned_row(jnp.minimum(x + 2, 31), even)
        rates(x + 1, odd)
        curves(jnp.minimum(x + 3, 31))
        curves(jnp.minimum(x + 4, 31))

    loop(0, 16, two)
    for side in range(2):
        for k in range(2):
            for y in range(16):
                tips_ref[side, k, y] = both_ref[k, 31 * side, y]


def inner_rate_first(p_ref, v_ref, both_ref, acc_ref):
    def x_line(y):
        march = March(lambda x: p_ref[x, y])
        for x in range(32):
            if 3 <= x < 29:
                acc_ref[x, y] = march.part(x, v_ref[0, x, y])
            else:
                acc_ref[x, y] = jnp.zeros((ROWS, LANES), jnp.float32)

    def y_line(x):
        march = March(lambda y: p_ref[x, y])
        for y in range(16):
            speed = v_ref[2, x, y]
            total = acc_ref[x, y] + speed * jnp.where(speed < 0, both_ref[0, x, y], both_ref[1, x, y])
            if 3 <= y < 13:
                total = total + march.part(y, v_ref[1, x, y])
            acc_ref[x, y] = total

    loop_pairs(0, 16, x_line)
    loop_pairs(1, 31, y_line)


def join_x(p_ref, coarse_ref, mark_ref, low_ref, high_ref):
    for x in range(3):
        for y in range(16):
            at = pl.ds((x * 16 + y) * 8, 8)
            low_ref[at, :] = p_ref[x, y]
            high_ref[at, :] = p_ref[29 + x, y]
    for k in range(15):
        low_ref[pl.ds(384 + 8 * k, 8), :] = coarse_ref[pl.ds(8 * k, 8), :]
        high_ref[pl.ds(384 + 8 * k, 8), :] = coarse_ref[pl.ds(1800 + 8 * k, 8), :]


def section(start, current, rate, number):
    if number == 0:
        return current + rate
    if number == 1:
        return 0.75 * start + 0.25 * (current + rate)
    return start * (1.0 / 3.0) + (2.0 / 3.0) * (current + rate)


def turned_about(number, *pairs):
    return [pair[::-1] if number % 2 else pair for pair in pairs]


def edge_rate(
    number, edge, acc_ref, start_ref, p_ref, v_ref, x1_ref, x2_ref, y1_ref, y2_ref,
    new_ref, nxlo_ref, nxhi_ref, nylo_ref, nyhi_ref, side,
):
    (xlo_ref, xhi_ref), (ylo_ref, yhi_ref) = turned_about(number, (x1_ref, x2_ref), (y1_ref, y2_ref))

    def from_rows(ref, x, y):
        return ref[pl.ds((x * 16 + y) * 8, 8), :]

    def x_line(y):
        low = March(lambda x: from_rows(xlo_ref, x + 3, y) if x < 0 else p_ref[x, y])
        high = March(lambda x: from_rows(xhi_ref, x - 32, y) if x >= 32 else p_ref[x, y])
        for k in range(3):
            side[k, y] = low.part(k, v_ref[0, k, y])
            side[k + 3, y] = high.part(29 + k, v_ref[0, 29 + k, y])

    loop_pairs(0, 16, x_line)

    def y_line(x, side_x, outs):
        low = March(lambda y: ylo_ref[x, y + 3] if y < 0 else p_ref[x, y])
        high = March(lambda y: yhi_ref[x, y - 16] if y >= 16 else p_ref[x, y])
        for y in range(16):
            rate = acc_ref[x, y]
            if side_x is not None:
                rate = rate + side[side_x, y]
            if y < 3:
                rate = rate + low.part(y, v_ref[1, x, y])
            if y >= 13:
                rate = rate + high.part(y, v_ref[1, x, y])
            start = None if number == 0 else start_ref[x, y]
            new = section(start, p_ref[x, y], rate, number)
            new_ref[x, y] = new
            if outs is not None:
                outs[0][pl.ds((outs[1] * 16 + y) * 8, 8), :] = new
            if y < edge:
                nylo_ref[x, y] = new
            if y >= 16 - edge:
                nyhi_ref[x, y - (16 - edge)] = new

    loop(0, 3, lambda x: y_line(x, x, (nxlo_ref, x)))
    loop(29, 32, lambda x: y_line(x, x - 26, (nxhi_ref, x - (32 - edge))))
    if edge > 3:
        loop(3, edge, lambda x: y_line(x, None, (nxlo_ref, x)))
        loop(32 - edge, 29, lambda x: y_line(x, None, (nxhi_ref, x - (32 - edge))))
    loop_pairs(edge, 32 - edge, lambda x: y_line(x, None, None))


def pushes(col):
    push = (PSEUDO_STEP * col) * lax.rsqrt(col * col + 1.0)
    return push, jnp.where(col > 0, 1.0, -1.0)


def turn(src, x, ys, turned):
    for y in ys:
        col = src[x, y]
        turned[0, y] = shifted(col, -1)
        turned[1, y] = shifted(col, 1)


def sweep_line(src, dst, push, sign, x, ys, turned):
    cols = {}

    def at(y):
        if y not in cols:
            cols[y] = src[x, y]
        return cols[y]

    for y in ys:
        col, c, s = at(y), push[x, y], sign[x, y]
        here = s * col
        total = None
        for pair in ((src[x - 1, y], src[x + 1, y]), (at(y - 1), at(y + 1)), (turned[0, y], turned[1, y])):
            floor = 1e-15 if total is None else 0.0
            rise = jnp.maximum(here - jnp.minimum(s * pair[0], s * pair[1]), floor)
            total = rise * rise if total is None else total + rise * rise
        dst[x, y] = (col + c) - (c * total) * lax.rsqrt(total)


def sweep_rows(src, dst, push, sign, place, pairs, ys, even, odd):
    turn(src, place(0), ys, even)

    def two(j):
        x = place(j)
        turn(src, x + 1, ys, odd)
        sweep_line(src, dst, push, sign, x, ys, even)
        turn(src, place(jnp.minimum(j + 1, pairs - 1)), ys, even)
        sweep_line(src, dst, push, sign, x + 1, ys, odd)

    loop(0, pairs, two)


def sweep_core(adv_ref, *refs):
    levels, (push, sign, even, odd) = refs[:SWEEPS], refs[SWEEPS:]

    def prepare(x):
        for y in range(16):
            push[x, y], sign[x, y] = pushes(adv_ref[x, y])

    loop_pairs(0, 32, prepare)
    src = adv_ref
    for k in range(1, SWEEPS + 1):
        dst = levels[k - 1]
        sweep_rows(src, dst, push, sign, lambda j, k=k: k + 2 * j, 16 - k, range(k, 16 - k), even, odd)
        src = dst


def pack_corners(xhi_ref, xlo_ref, _, low_ref, high_ref):
    k = 0
    for dx in range(1, WIDE):
        for ref, x in ((xlo_ref, WIDE - dx), (xhi_ref, dx - 1)):
            for dy in range(1, WIDE - dx + 1):
                low_ref[k] = ref[pl.ds((x * 16 + dy - 1) * 8, 8), :]
                high_ref[k] = ref[pl.ds((x * 16 + 16 - dy) * 8, 8), :]
                k += 1


CORNERS = WIDE * (WIDE - 1)


def normals(last, xs, nx, ny, nz, at):
    cols = {}

    def col(y):
        if y not in cols:
            cols[y] = last[xs, y + WIDE]
        return cols[y]

    across, along, deep = {}, {}, {}
    for y in range(-1, 17):
        gx = last[xs + 1, y + WIDE] - last[xs - 1, y + WIDE]
        gy = col(y + 1) - col(y - 1)
        gz = shifted(col(y), 1) - shifted(col(y), -1)
        scale = lax.rsqrt(gx * gx + gy * gy + gz * gz + 4.0)
        across[y], along[y], deep[y] = gx * scale, gy * scale, gz * scale
    for j in range(8):
        a, b = 2 * j, 2 * j + 1
        nx[at, j] = across[a] + across[b]
        ny[at, j] = (along[b] + along[b + 1]) - (along[a - 1] + along[a])
        nz[at, j] = deep[a] + deep[b]


def gather(last, xs, nx, ny, nz, at, lump, slot, half, new, new_at):
    a, b = at, at + 1
    for j in range(8):
        deep = nz[a, j] + nz[b, j]
        total = (nx[b, j] + nx[b + 1, j]) - (nx[a - 1, j] + nx[a, j]) + (ny[a, j] + ny[b, j])
        lump[pl.ds(slot * 64 + j * 8, 8), :] = total + (shifted(deep, 1) - shifted(deep, -1))
        share = None
        for x in range(2):
            for y in range(2):
                yy = 2 * j + y
                col = last[xs + x, yy + WIDE]
                new[pl.ds(new_at + x * 128 + (yy // 8) * 64 + yy % 8, 8, stride=8), :] = col
                bend = jnp.tanh(col * (1.0 / FRONT))
                share = bend if share is None else share + bend
        lump[pl.ds(half + slot * 64 + j * 8, 8), :] = share


def restrict(lump, slots, half, send, send_at):
    k = lax.broadcasted_iota(jnp.int32, (256, 128), 0)
    n = lax.broadcasted_iota(jnp.int32, (256, 128), 1)
    table = jnp.where(lax.div(k, 2) == n, 1.0 / 16.0, 0.0)
    halves = []
    for odd_row in range(2):
        rows = []
        for kind in range(2):
            for i in slots:
                base = kind * half + i * 64 + odd_row
                rows += [lump[pl.ds(base + 2 * z, 8, stride=8), :] for z in range(4)]
        halves.append(jnp.concatenate(rows, axis=0))
    out = jnp.dot(jnp.concatenate(halves, axis=1), table, precision=HIGH, preferred_element_type=jnp.float32)
    for n, i in enumerate(slots):
        send[send_at(i), pl.ds(0, 32), :] = out[n * 32 : n * 32 + 32]
        send[send_at(i), pl.ds(32, 32), :] = out[(len(slots) + n) * 32 : (len(slots) + n) * 32 + 32] + 0.5


def sweep_sides(
    adv_ref, yhi_ref, ylo_ref, one_ref, two_ref, three_ref, four_ref,
    rims_ref, last_ref, q0, q1, push, sign, even, odd,
):
    w = WIDE
    size_y = 16 + 2 * w

    def put(x, y, col):
        q0[x, y] = col
        push[x, y], sign[x, y] = pushes(col)

    def fill(x):
        for y in range(w):
            put(x, y, ylo_ref[x, y])
            put(x, y + 16 + w, yhi_ref[x, y])
        for y in (0, 1, 2, 3, 12, 13, 14, 15):
            put(x, y + w, adv_ref[x, y])

    loop_pairs(0, 32, fill)
    src, dst = q0, q1
    for k, core_ref in enumerate((one_ref, two_ref, three_ref, four_ref), 1):
        dst = last_ref if k == SWEEPS else dst
        sides = [*range(k, k + w), *range(size_y - k - w, size_y - k)]
        sweep_rows(src, dst, push, sign, lambda j, k=k: k + 2 * j, 16 - k, sides, even, odd)
        inside = (k, k + 1, 14 - k, 15 - k) if k < SWEEPS else range(k, 16 - k)

        def take(x, core_ref=core_ref, inside=inside, dst=dst):
            for y in inside:
                dst[x, y + w] = core_ref[x, y]

        loop_pairs(k, 32 - k, take)
        if k < SWEEPS:
            for r, x in enumerate((k, k + 1, 30 - k, 31 - k)):
                for y in range(k, size_y - k):
                    inner = k + 2 <= y - w < 14 - k
                    rims_ref[k - 1, r, y] = core_ref[x, y - w] if inner else dst[x, y]
        src, dst = dst, src


def inner_outputs(last, new_ref, send_ref, nx, ny, nz, lump):
    loop_pairs(0, 22, lambda r: normals(last, r + 5, nx, ny, nz, r))

    def planes(n):
        gather(last, 2 * n + 6, nx, ny, nz, 2 * n + 1, lump, n, 640, new_ref, (2 * n + 6) * 128)

    loop_pairs(0, 10, planes)
    for x in (4, 5, 26, 27):
        for y in range(16):
            new_ref[pl.ds(x * 128 + (y // 8) * 64 + y % 8, 8, stride=8), :] = last[x, y + WIDE]
    for part in range(2):
        restrict(lump, range(5 * part, 5 * part + 5), 640, send_ref, lambda i: i)


def finish(
    adv_ref, xhi_ref, xlo_ref, yhi_ref, ylo_ref, clo_ref, chi_ref, rims_ref, rows_ref, send_mid_ref, _,
    new_ref, send_ref, q0, q1, push, sign, nx, ny, nz, lump, even, odd, ends, sems,
):
    w = WIDE
    size_y = 16 + 2 * w

    def put(x, y, col):
        q0[x, y] = col
        push[x, y], sign[x, y] = pushes(col)

    def fill_mid(r):
        x = r + jnp.where(r >= 4, 24, 0)
        at = r + w + jnp.where(r >= 4, 8, 0)
        for y in range(w):
            put(at, y, ylo_ref[x, y])
            put(at, y + 16 + w, yhi_ref[x, y])
        for y in range(16):
            put(at, y + w, adv_ref[x, y])

    def fill_side(x):
        for y in range(16):
            put(x, y + w, xlo_ref[pl.ds((x * 16 + y) * 8, 8), :])
            put(x + 16 + w, y + w, xhi_ref[pl.ds((x * 16 + y) * 8, 8), :])

    loop_pairs(0, 8, fill_mid)
    loop_pairs(0, w, fill_side)
    k = 0
    for dx in range(1, w):
        for x in (w - dx, w + 15 + dx):
            for dy in range(1, w - dx + 1):
                put(x, w - dy, clo_ref[k])
                put(x, w + 15 + dy, chi_ref[k])
                k += 1

    src, dst = q0, q1
    for k in range(1, SWEEPS + 1):

        def end_rows(j, k=k):
            return k + 2 * j + jnp.where(j >= 3, 16 - 2 * k, 0)

        sweep_rows(src, dst, push, sign, end_rows, 6, range(k, size_y - k), even, odd)
        if k < SWEEPS:
            for r, x in enumerate((k, k + 1, 14 - k, 15 - k)):
                for y in range(k, size_y - k):
                    dst[x + w, y] = rims_ref[k - 1, r, y]
        src, dst = dst, src
    last = src

    def take(r):
        x = SWEEPS + r + jnp.where(r >= 4, 16, 0)
        for y in range(SWEEPS, size_y - SWEEPS):
            last[SWEEPS + r + w, y] = rows_ref[x, y]

    loop(0, 8, take)
    loop_pairs(0, 16, lambda r: normals(last, r + w - 1 + jnp.where(r >= 8, 2, 0), nx, ny, nz, r))

    def planes(n):
        far = jnp.where(n >= 3, 1, 0)
        gather(last, 2 * n + w + 4 * far, nx, ny, nz, 2 * n + 1 + 2 * far, lump, n, 384, ends, n * 256)

    loop_pairs(0, 6, planes)
    copies = [
        pltpu.make_async_copy(ends.at[pl.ds(1024 * k, 512)], new_ref.at[pl.ds(3584 * k, 512)], sems.at[k])
        for k in range(2)
    ]
    for copy in copies:
        copy.start()
    restrict(lump, range(6), 384, send_ref, lambda i: i + (10 if i >= 3 else 0))
    send_ref[pl.ds(3, 10)] = send_mid_ref[...]
    for copy in copies:
        copy.wait()


def call(kernel, outs, *args, scratch=(), mib=48, ops=1000, name=None, anywhere=(), aliases=None):
    def spec(k):
        return pl.BlockSpec(memory_space=pl.ANY if k in anywhere else pltpu.VMEM)

    aliases = aliases or {}
    flat = outs if isinstance(outs, tuple) else (outs,)
    specs = tuple(pl.BlockSpec(memory_space=pl.ANY if k in aliases.values() else pltpu.VMEM) for k in range(len(flat)))
    return pl.pallas_call(
        kernel,
        out_shape=outs,
        in_specs=[spec(k) for k in range(len(args))],
        out_specs=specs if isinstance(outs, tuple) else specs[0],
        scratch_shapes=[pltpu.VMEM(s, jnp.float32) if isinstance(s, tuple) else s for s in scratch],
        input_output_aliases=aliases,
        compiler_params=params(mib),
        cost_estimate=cost(ops),
        name=name,
    )(*args)


def moved(values, axis, step):
    count = lax.axis_size(axis)
    return lax.ppermute(values, axis, [(i, (i + step) % count) for i in range(count)])


def star(xlo, xhi, ylo, yhi):
    return (moved(xhi, "gx", 1), moved(xlo, "gx", -1), moved(yhi, "gy", 1), moved(ylo, "gy", -1))


def per_device(level_set, flow_velocity, band_mask):
    col = (ROWS, LANES)
    block = f32(32, 16, *col)
    level_rows = level_set.reshape(32, 2, 8, 8, 128).transpose(0, 1, 3, 2, 4).reshape(4096, 128)
    flow_rows = flow_velocity.reshape(3, 16, 8, 4, 128).transpose(0, 1, 3, 2, 4).reshape(1536, 128)

    send = call(pack_velocity, f32(16, 120, 128), flow_rows, name="pack", mib=8)
    coarse = lax.all_to_all(send, "gy", split_axis=0, concat_axis=0, tiled=True)
    start, ylo, yhi = call(
        unpack_level, (block, f32(32, 3, *col), f32(32, 3, *col)), level_rows, name="unpack", mib=8
    )
    both, tips = call(
        depth_sides, (f32(2, 32, 16, *col), f32(2, 2, 16, *col)), start,
        scratch=[block.shape, block.shape, (4, 16, *col), (4, 16, *col)], name="depth", mib=14, ops=512 * 90,
    )
    coarse = coarse.reshape(1920, 128)
    xlo, xhi = call(join_x, (f32(504, 128), f32(504, 128)), start, coarse, tips, name="join", mib=4)
    halo = star(xlo, xhi, ylo, yhi)
    velocity, ends = call(
        refine_inner, (f32(3, 32, 16, *col), f32(2, 240, 128)), coarse, band_mask,
        scratch=[(3840, 128), (2, *col)], name="refine", mib=20, ops=512 * 20,
    )
    acc = call(inner_rate_first, block, start, velocity, both, name="first", mib=12, ops=512 * 90)
    current = start
    for number in range(3):
        if number == 0:
            velocity, acc = call(
                refine_ends, (f32(3, 32, 16, *col), block),
                halo[0], halo[1], ends, band_mask, current, tips, velocity, acc,
                scratch=[(480, 128), (3, 2, 16, *col), (2, 16, *col), pltpu.SemaphoreType.DMA((8,))],
                name="ends", mib=8, anywhere=(6, 7), aliases={6: 0, 7: 1},
            )
        else:
            acc = call(
                inner_rate, block, current, velocity,
                scratch=[block.shape, block.shape, (4, 16, *col), (4, 16, *col)],
                name="inner", mib=12, ops=512 * 140,
            )
        edge = WIDE if number == 2 else 3
        x_edge, y_edge = f32(edge * 128, 128), f32(32, edge, *col)
        current, *edges = call(
            functools.partial(edge_rate, number, edge), (block, x_edge, x_edge, y_edge, y_edge),
            acc, start, current, velocity, *sum(turned_about(number, halo[:2], halo[2:]), ()),
            scratch=[(6, 16, *col)], name="edge", mib=12, ops=512 * 30,
        )
        halo = star(*edges)
    xlo, xhi, ylo, yhi = halo
    levels = call(
        sweep_core, (block,) * SWEEPS, current,
        scratch=[block.shape, block.shape, (2, 16, *col), (2, 16, *col)], name="core", mib=16, ops=512 * 90,
    )
    corner = f32(CORNERS, *col)
    turns = [(2, 16 + 2 * WIDE, *col)] * 2
    side = (32, 16 + 2 * WIDE, *col)
    rims, last = call(
        sweep_sides, (f32(3, 4, *side[1:]), f32(*side)), current, yhi, ylo, *levels,
        scratch=[side] * 4 + turns, name="sides", mib=24, ops=512 * 70,
    )
    corner_low, corner_high = call(
        pack_corners, (corner, corner), xhi, xlo, rims, name="corners", mib=4, anywhere=(2,)
    )
    new_rows, send_mid = call(
        inner_outputs, (f32(4096, 128), f32(10, 64, 128)), last,
        scratch=[(22, 8, *col)] * 3 + [(1280, 128)], name="outputs", mib=14, ops=512 * 40,
    )
    clo, chi = moved(corner_high, "gy", 1), moved(corner_low, "gy", -1)
    ext = (16 + 2 * WIDE, 16 + 2 * WIDE, *col)
    new_rows, packed = call(
        finish, (f32(4096, 128), f32(16, 64, 128)),
        current, xhi, xlo, yhi, ylo, clo, chi, rims, last, send_mid, new_rows,
        scratch=[ext] * 4 + [(16, 8, *col)] * 3 + [(768, 128)] + turns + [(1536, 128), pltpu.SemaphoreType.DMA((2,))],
        name="finish", mib=26, ops=512 * 250, anywhere=(10,), aliases={10: 0},
    )
    returned = lax.all_to_all(packed, "gy", split_axis=0, concat_axis=0, tiled=True).reshape(16, 2, 4, 8, 128)
    new_level = new_rows.reshape(32, 2, 8, 8, 128).transpose(0, 1, 3, 2, 4).reshape(32, 16, 1024)
    flows = [returned[:, k].transpose(0, 2, 1, 3).reshape(1, 128, 512) for k in range(2)]
    return (new_level, flows[0], flows[1])


def solution(mesh):
    placed = (P("gx", "gy", None), P(None, ("gx", "gy"), None, None), P("gx", "gy", None))
    return jax.shard_map(
        per_device,
        mesh=mesh,
        in_specs=placed,
        out_specs=(P("gx", "gy", None), P(("gx", "gy"), None, None), P(("gx", "gy"), None, None)),
        check_vma=False,
    )
```
